512 devices in a mesh: gx: 16 (over y, z_lo), gy: 4 (over z_hi), gz: 8 (over x, core).
Axes of the slice: x: 4, y: 8, z: 8 (z_hi: 4, z_lo: 2; z = z_hi * 2 + z_lo), core: 2. Of those that a mesh axis runs over, the one named last changes fastest.
Arguments:
- stiffness: float32 [128, 384, 512], P('gz', 'gx', 'gy'), may hold values from 0.03 to 0.1
- older_wave: float32 [128, 384, 512], P('gz', 'gx', 'gy'), may hold values from -4 to 4
- wave_now: float32 [128, 384, 512], P('gz', 'gx', 'gy'), may hold values from -5.2 to 5.2
- forward_wave: bfloat16 [4, 128, 384, 512], P(None, 'gz', 'gx', 'gy'), may hold values from -6 to 6
- residuals: float32 [4, 65536], P(None, ('gx', 'gy', 'gz')), may hold values from -6 to 6
- owners: int32 [65536, 1], P(('gx', 'gy', 'gz')), may hold values from 0 to 63; in each aligned block of 128 rows (0 to 127, 128 to 255, ...) at most 8 rows name the same one
- receivers: int32 [65536], P(('gx', 'gy', 'gz')), may hold values from 0 to 3071
- source_cell: int32 [1], replicated, may hold values from 0 to 196607
Outputs:
- image: float32 [128, 384, 512], P('gz', 'gx', 'gy')
- last_older: float32 [128, 384, 512], P('gz', 'gx', 'gy')
- last_wave: float32 [128, 384, 512], P('gz', 'gx', 'gy')
The draws below stay inside these ranges and needn't reach their ends.
Inputs may be any that keep to these rules, and one draw needn't show every extreme that they name: `owners`: in the rows of one device (aligned blocks of 128 rows) no owner is named more than 8 times, a bound that some block reaches.
All inputs are finite; a program needn't handle non-finite values.
Results may differ from the reference program's by a relative error of at most 0.0003.
Values sent between devices are 32-bit elements; how exact they have to be, the bound alone decides.
No kernel may reach another device: no remote copies, remote signals or barrier semaphores. Data moves between devices by JAX's collectives and lax.ppermute only.
A program may use at most 64 MiB of HBM per device.

```python
import math
import jax
import jax.numpy as jnp
import numpy as np

CX = 24
CY = 128
STEPS = 4
TR_DEV = 128
GY_TILES = 4
OWNERS = 64
CAP = 8
NX = 384
NY = 512
NZ = 128
TRACES = 65536


def wave_pair(key):
    common_key = jax.random.fold_in(key, 17)
    change_key = jax.random.fold_in(key, 29)
    extent = (NZ, NX, NY)
    common = jnp.clip(jax.random.normal(common_key, extent, jnp.float32), -4.0, 4.0)
    change = 0.3 * jnp.clip(jax.random.normal(change_key, extent, jnp.float32), -4.0, 4.0)
    return (common, common + change)


def draw_older_wave(key, part):
    return wave_pair(key)[0]


def draw_wave_now(key, part):
    return wave_pair(key)[1]


def plant(values, stream_key, low, largest):
    place = [jax.random.randint(jax.random.fold_in(stream_key, axis), (), 0, length) for axis, length in enumerate(values.shape)]
    main_axis = values.shape.index(max(values.shape))
    beside = place[:main_axis] + [(place[main_axis] + 1) % values.shape[main_axis]] + place[main_axis + 1:]
    return values.at[tuple(place)].set(low).at[tuple(beside)].set(largest)


def level_of(stream_key, shape, split, low, largest):
    def one(position, parts):
        draws = jax.random.uniform(jax.random.fold_in(jax.random.fold_in(stream_key, 6), position), (parts,), jnp.float32, low / len(split), largest / len(split))
        return jnp.repeat(jnp.exp(draws), shape[position] // parts).reshape((-1,) + (1,) * (len(shape) - position - 1))

    gain = one(*split[0])
    for cut in split[1:]:
        gain = gain * one(*cut)
    return gain


def deal_out(stream_key, own, number, rows, amount, top, reach, slope):
    sequence = jax.random.permutation(stream_key, amount)
    crowded, ordinary = portions_of(amount, rows * top, reach, slope, True), portions_of(amount, rows * top, reach, slope, False)
    places = jnp.arange(amount)

    def named(sizes, offset_by):
        used = int((sizes > 0).sum())
        fixed = max(1, used // 4)
        shifted = fixed + (places - fixed + offset_by * (used - fixed)) % max(1, amount - fixed)
        return jnp.zeros((amount,), jnp.int32).at[sequence[jnp.where(places < fixed, places, shifted)]].set(jnp.asarray(sizes, jnp.int32))

    sizes = jnp.where(number % 4 == 0, named(crowded, number // 4), named(ordinary, number - number // 4 - 1))
    mixed = jax.random.permutation(jax.random.fold_in(own, 3), amount)
    source_of, taker = mixed[0:amount // 2 * 2:2], mixed[1:amount // 2 * 2:2]
    slack = jnp.minimum(sizes[source_of] - 1, reach - sizes[taker]) // 2
    slack = jnp.where((source_of == sequence[0]) | (taker == sequence[0]) | (sizes[taker] == 0), 0, jnp.maximum(slack, 0))
    shifted = jax.random.randint(jax.random.fold_in(own, 4), (amount // 2,), 0, 1 << 20) % (slack + 1)
    sizes = sizes.at[source_of].add(-shifted).at[taker].add(shifted)
    labels = jnp.searchsorted(jnp.cumsum(sizes), jnp.arange(rows * top), side="right").astype(jnp.int32)
    table = labels.reshape(top, rows).T
    table = table[jax.random.permutation(jax.random.fold_in(own, 1), rows)]
    offset_by = jax.random.randint(jax.random.fold_in(own, 2), (rows, 1), 0, top)
    return jnp.take_along_axis(table, (jnp.arange(top)[None, :] + offset_by) % top, axis=1)


def portions_of(amount, total, reach, skew, full):
    weights = [(1 << 20) // math.isqrt(grade ** skew) + 1 for grade in range(1, amount + 1)]
    largest = reach if full else min(reach, max(-(-total // amount), total * weights[0] // sum(weights)))
    least = 1 if total - largest >= amount - 1 else 0
    given, surplus = [largest] + [least] * (amount - 1), total - largest - least * (amount - 1)
    while surplus > 0:
        movable = [i for i in range(1, amount) if given[i] < largest] or [i for i in range(1, amount) if given[i] < reach]
        mass, remaining = sum([weights[i] for i in movable]), surplus
        for i in movable:
            extra = min(reach - given[i], max(1, remaining * weights[i] // mass), surplus)
            given[i] = given[i] + extra
            surplus = surplus - extra
    return np.array(given)


def centred(own_key, shape, deviation, bound, split=(), held_as=jnp.bfloat16):
    array = deviation * jax.random.normal(own_key, shape, jnp.float32)
    if split:
        array = array * level_of(own_key, shape, split, -0.22, 0.18)
    return jnp.clip(array, -bound, bound).astype(held_as)


def setup_inputs(seed: int = 0) -> dict:
    splits = jax.random.split(jax.random.key(seed), 9)
    stiffness = jnp.clip(jnp.exp(math.log(0.1) - 1.2039728 * jax.random.uniform(splits[0], (NZ, NX, NY), jnp.float32) ** level_of(splits[0], (NZ, NX, NY), ((0, 8), (1, 16), (2, 4)), -0.2, 0.2)), 0.03, 0.1)
    older_wave = draw_older_wave(jax.random.fold_in(splits[8], 71), 0)
    wave_now = draw_wave_now(jax.random.fold_in(splits[8], 71), 0)
    forward_wave = centred(splits[3], (STEPS, NZ, NX, NY), 1.0, 6.0, ((1, 8), (2, 16), (3, 4)))
    residuals = centred(splits[4], (STEPS, TRACES), 1.0, 6.0, ((1, 512),), jnp.float32)
    owners_keys = jax.random.split(jax.random.fold_in(splits[5], 1), TRACES // TR_DEV)
    owners_turns = jax.random.permutation(jax.random.fold_in(splits[5], 3), TRACES // TR_DEV)
    owners = jax.vmap(lambda own, number: deal_out(jax.random.fold_in(splits[5], 2), own, number, TR_DEV, OWNERS, 1, CAP, 2))(owners_keys, owners_turns).reshape((TRACES, 1))
    receivers = plant(jax.random.randint(splits[6], (TRACES,), 0, CX * CY), jax.random.fold_in(splits[6], 1), 0, (CX * CY) - 1).astype(jnp.int32)
    source_cell = jax.random.randint(splits[7], (1,), 0, NX * NY).astype(jnp.int32)
    return {"stiffness": stiffness, "older_wave": older_wave, "wave_now": wave_now, "forward_wave": forward_wave, "residuals": residuals, "owners": owners, "receivers": receivers, "source_cell": source_cell}


def stencil_weights():
    radius = 8
    window = [math.cos(math.pi * offset / 20.0) for offset in range(1, radius + 1)]
    alternating = sum((-1.0) ** (offset + 1) * window[offset - 1] for offset in range(1, radius + 1))
    factor = 1.0 / (2.0 * alternating)
    weights = []
    for offset in range(1, radius + 1):
        weights.append(factor * 2.0 * (-1.0) ** (offset + 1) * window[offset - 1] / (offset * offset))
    return weights, -2.0 * sum(weights)


def laplace(field):
    weights, center = stencil_weights()
    depth, rows, cols = field.shape
    total = (3.0 * center) * field[8:depth - 8, 8:rows - 8, 8:cols - 8]
    for offset in range(1, 9):
        near = field[8 + offset:depth - 8 + offset, 8:rows - 8, 8:cols - 8] + field[8 - offset:depth - 8 - offset, 8:rows - 8, 8:cols - 8]
        near = near + field[8:depth - 8, 8 + offset:rows - 8 + offset, 8:cols - 8] + field[8:depth - 8, 8 - offset:rows - 8 - offset, 8:cols - 8]
        near = near + field[8:depth - 8, 8:rows - 8, 8 + offset:cols - 8 + offset] + field[8:depth - 8, 8:rows - 8, 8 - offset:cols - 8 - offset]
        total = total + weights[offset - 1] * near
    return total


def reference(stiffness, older_wave, wave_now, forward_wave, residuals, owners, receivers, source_cell):
    owner = owners[:, 0]
    column_x = (owner // GY_TILES) * CX + receivers // CY
    column_y = (owner % GY_TILES) * CY + receivers % CY
    flat = (column_x * NY + column_y).astype(jnp.int32)
    plane = jnp.zeros((STEPS, NX * NY), jnp.float32).at[:, flat].add(residuals.astype(jnp.float32))
    plane = plane.reshape(STEPS, NX, NY)
    image_sum = jnp.zeros((NZ, NX, NY), jnp.float32)
    for moment in range(STEPS):
        laplacian = laplace(jnp.pad(wave_now, 8)).at[0].add(plane[moment])
        fresh = 2.0 * wave_now - older_wave + stiffness * laplacian
        image_sum = image_sum + forward_wave[moment].astype(jnp.float32) * fresh
        older_wave, wave_now = wave_now, fresh
    shot_x = source_cell[0] // NY
    shot_y = source_cell[0] % NY
    depth_gap = jnp.arange(NZ, dtype=jnp.int32).astype(jnp.float32)
    gap_x = (jnp.arange(NX, dtype=jnp.int32) - shot_x).astype(jnp.float32)
    gap_y = (jnp.arange(NY, dtype=jnp.int32) - shot_y).astype(jnp.float32)
    distance = (depth_gap * depth_gap)[:, None, None] + (gap_x * gap_x)[None, :, None] + (gap_y * gap_y)[None, None, :]
    weight = jnp.minimum(1.0, distance / 576.0)
    return weight * image_sum, older_wave, wave_now
```

```python
import functools
import math

import jax
import jax.numpy as jnp
import numpy as np
from jax import lax
from jax.experimental import pallas as pl
from jax.experimental.pallas import tpu as pltpu
from jax.sharding import PartitionSpec as P

STEPS = 4
RADIUS = 8
LANES = 128
STRIP = 32
CAP = 8
SLOTS = 3 * CAP
F32 = jnp.float32
BF16 = jnp.bfloat16


def stencil_weights():
    window = [math.cos(math.pi * offset / 20.0) for offset in range(1, RADIUS + 1)]
    alternating = sum(
        ((-1.0) ** (offset + 1) * window[offset - 1] for offset in range(1, RADIUS + 1))
    )
    factor = 1.0 / (2.0 * alternating)
    weights = []
    for offset in range(1, RADIUS + 1):
        weights.append(
            factor * 2.0 * (-1.0) ** (offset + 1) * window[offset - 1] / (offset * offset)
        )
    return (weights, -2.0 * sum(weights))


WEIGHTS, CENTER = stencil_weights()


def band():
    size = 2 * LANES
    matrix = np.zeros((size, size), np.float64)
    for column in range(size):
        matrix[column, column] = 3.0 * CENTER
        for offset in range(1, RADIUS + 1):
            matrix[(column + offset) % size, column] = WEIGHTS[offset - 1]
            matrix[(column - offset) % size, column] = WEIGHTS[offset - 1]
    matrix = matrix.astype(np.float32)
    high = matrix.astype(jnp.bfloat16)
    low = (matrix - high.astype(np.float32)).astype(jnp.bfloat16)
    return high, low


def lane_of(shape):
    return lax.broadcasted_iota(jnp.int32, shape, len(shape) - 1)


def vmem():
    return pl.BlockSpec(memory_space=pltpu.VMEM)


def smem():
    return pl.BlockSpec(memory_space=pltpu.SMEM)


def call(body, outs, ins, scratch=(), flops=1_000_000, in_specs=None):
    return pl.pallas_call(
        body,
        out_shape=outs,
        in_specs=in_specs or [smem()] + [vmem()] * (len(ins) - 1),
        out_specs=jax.tree.map(lambda _: vmem(), outs),
        scratch_shapes=list(scratch),
        compiler_params=pltpu.CompilerParams(vmem_limit_bytes=32 * 1024 * 1024),
        cost_estimate=pl.CostEstimate(flops=flops, bytes_accessed=2_000_000, transcendentals=0),
    )(*ins)


def shaped(*shape):
    return jax.ShapeDtypeStruct(shape, F32)


def split3(value):
    high = value.astype(BF16)
    rest = value - high.astype(F32)
    middle = rest.astype(BF16)
    return high, middle, (rest - middle.astype(F32)).astype(BF16)


def dot_nt(left, right):
    return lax.dot_general(left, right, (((1,), (1,)), ((), ())), preferred_element_type=F32)


def slot_kernel(span_y, tiles, ids, residuals, owner_column, owner_row, cell_row, out):
    rows = residuals.shape[1]
    owner = owner_row[...]
    earlier = (owner_column[...] == owner) & (
        lax.broadcasted_iota(jnp.int32, (rows, rows), 0)
        < lax.broadcasted_iota(jnp.int32, (rows, rows), 1)
    )
    rank = jnp.sum(earlier.astype(jnp.int32), axis=0, keepdims=True)
    cell = cell_row[...]
    along = cell & (LANES - 1)
    fields = [residuals[pl.ds(field, 1), :] for field in range(STEPS)] + [cell.astype(F32)]
    stacked = jnp.concatenate(
        [jnp.broadcast_to(field, (SLOTS, rows)) for field in fields]
        + [jnp.zeros((LANES - SLOTS * len(fields), rows), F32)],
        axis=0,
    )
    line = lax.broadcasted_iota(jnp.int32, (LANES, rows), 0)
    slot = line - SLOTS * (line // SLOTS)
    tile = lax.broadcasted_iota(jnp.int32, (tiles, rows), 0)
    place = tile & (span_y - 1)
    total = jnp.zeros((tiles, LANES), F32)
    for group in range(3):
        named = owner == tile + (group - 1)
        wanted = slot == rank + CAP * group
        if group == 0:
            named = named & (place != 0)
            wanted = wanted & (along >= LANES - STRIP)
        if group == 2:
            named = named & (place != span_y - 1)
            wanted = wanted & (along < STRIP)
        chosen = named.astype(F32).astype(BF16)
        for part in split3(jnp.where(wanted, stacked, 0.0)):
            total = total + dot_nt(chosen, part)
    out[...] = total


def plane_kernel(rows, ids, packets, main, side, turned):
    main[...] = jnp.zeros(main.shape, F32)
    side[...] = jnp.zeros(side.shape, F32)

    @pl.when(ids[0] == 0)
    def _():
        turned[...] = jnp.transpose(packets[...])
        count = packets.shape[0]
        line = lax.broadcasted_iota(jnp.int32, (rows, count), 0)
        spot = lax.broadcasted_iota(jnp.int32, (LANES, count), 0)

        def product(slot):
            cell = turned[pl.ds(SLOTS * STEPS + slot, 1), :].astype(jnp.int32)
            hit = (cell >> 7) == line
            highs, lows = [], []
            for step in range(STEPS):
                value = turned[pl.ds(SLOTS * step + slot, 1), :]
                high = value.astype(BF16).astype(F32)
                highs.append(jnp.where(hit, high, 0.0))
                lows.append(jnp.where(hit, value - high, 0.0))
            left = jnp.concatenate(highs + lows, axis=0).astype(BF16)
            right = jnp.where((cell & (LANES - 1)) == spot, 1.0, 0.0).astype(BF16)
            both = dot_nt(left, right)
            return both[: STEPS * rows] + both[STEPS * rows :]

        for slot in range(SLOTS):
            target = main if slot // CAP == 1 else side
            target[...] += product(slot).reshape(target.shape)


def strip_pack_kernel(ids, wave, older, stiff, even, odd):
    parity = ids[2] & 1
    quarter = lane_of(wave.shape[1:]) // STRIP
    low, high = quarter == 0, quarter == 3
    quarters = LANES // STRIP
    for number, field in enumerate((wave, older, stiff)):
        for chunk in range(field.shape[0] // quarters):
            lows = highs = None
            for turn in range(quarters):
                value = field[quarters * chunk + turn]
                one = jnp.where(low, value, 0.0)
                two = jnp.where(high, value, 0.0)
                if turn:
                    one = pltpu.roll(one, STRIP * turn, 1)
                    two = pltpu.roll(two, STRIP * turn, 1)
                lows = one if lows is None else lows + one
                highs = two if highs is None else highs + two
            place = number * (field.shape[0] // quarters) + chunk
            even[place] = jnp.where(parity == 0, highs, lows)
            odd[place] = jnp.where(parity == 0, lows, highs)


def fold(first, second):
    return first + pltpu.roll(second, LANES // 2, 1)


def write_faces(ids, main, side, z_even, z_odd, x_even, x_odd):
    z_parity, x_parity = ids[0] & 1, ids[1] & 1
    depth, rows, _ = main.shape
    half = RADIUS // 2
    for face, start in (
        (z_even, (depth - RADIUS) * (1 - z_parity)),
        (z_odd, (depth - RADIUS) * z_parity),
    ):
        face[pl.ds(0, RADIUS)] = main[pl.ds(start, RADIUS)]
        for plane in range(half):
            face[RADIUS + plane] = fold(side[start + plane], side[start + half + plane])
    for face, start in (
        (x_even, (rows - RADIUS) * (1 - x_parity)),
        (x_odd, (rows - RADIUS) * x_parity),
    ):
        start = pl.multiple_of(start, RADIUS)
        face[pl.ds(0, depth)] = main[:, pl.ds(start, RADIUS), :]
        for plane in range(depth // 2):
            face[depth + plane] = fold(
                side[plane, pl.ds(start, RADIUS), :],
                side[plane + depth // 2, pl.ds(start, RADIUS), :],
            )


def strip_unpack_kernel(
    ids, even, odd, wave, wave_side, older_side, stiff_side, z_even, z_odd, x_even, x_odd
):
    parity = ids[2] & 1
    quarters = LANES // STRIP
    quarter = lane_of(wave.shape[1:]) // STRIP
    from_even = quarter == 3 * parity
    from_odd = quarter == 3 * (1 - parity)
    chunks = wave.shape[0] // quarters
    for number, side in enumerate((wave_side, older_side, stiff_side)):
        for chunk in range(chunks):
            one, two = even[number * chunks + chunk], odd[number * chunks + chunk]
            for turn in range(quarters):
                back = (LANES - STRIP * turn) % LANES
                first = pltpu.roll(one, back, 1) if back else one
                second = pltpu.roll(two, back, 1) if back else two
                side[quarters * chunk + turn] = jnp.where(
                    from_even, first, jnp.where(from_odd, second, 0.0)
                )
    write_faces(ids, wave, wave_side, z_even, z_odd, x_even, x_odd)


def fill(ids, wave, side, z_even, z_odd, x_even, x_odd, z_ext, x_ext):
    z_parity, x_parity = ids[0] & 1, ids[1] & 1
    depth, rows, _ = wave.shape
    half = RADIUS // 2
    outer = lane_of((RADIUS, LANES))
    kept = (outer < STRIP) | (outer >= LANES - STRIP)
    kept_plane = lane_of((rows, LANES))
    kept_plane = (kept_plane < STRIP) | (kept_plane >= LANES - STRIP)
    for part, field in enumerate((wave, side)):
        z_ext[part, pl.ds(RADIUS, depth)] = field[...]
        x_ext[part, :, pl.ds(RADIUS, rows), :] = field[...]
    pair = z_even.at[1 - z_parity]
    for face, start in (
        (pair, (depth + RADIUS) * (1 - z_parity)),
        (z_odd, (depth + RADIUS) * z_parity),
    ):
        z_ext[0, pl.ds(start, RADIUS)] = face[pl.ds(0, RADIUS)]
        for plane in range(half):
            both = face[RADIUS + plane]
            z_ext[1, start + plane] = jnp.where(kept_plane, both, 0.0)
            z_ext[1, start + half + plane] = jnp.where(
                kept_plane, pltpu.roll(both, LANES // 2, 1), 0.0
            )
    for face, start in (
        (x_even, (rows + RADIUS) * (1 - x_parity)),
        (x_odd, (rows + RADIUS) * x_parity),
    ):
        start = pl.multiple_of(start, RADIUS)
        x_ext[0, :, pl.ds(start, RADIUS), :] = face[pl.ds(0, depth)]
        for plane in range(depth // 2):
            both = face[depth + plane]
            x_ext[1, plane, pl.ds(start, RADIUS), :] = jnp.where(kept, both, 0.0)
            x_ext[1, plane + depth // 2, pl.ds(start, RADIUS), :] = jnp.where(
                kept, pltpu.roll(both, LANES // 2, 1), 0.0
            )


def advance(step, ids, refs, wave, side, older, older_side, stiff, stiff_side, forward, image_in,
            plane, plane_side, band_high, band_low, fresh, fresh_side, image, z_ext, x_ext, y_terms):
    depth, rows, _ = wave.shape
    last = step == STEPS - 1
    width = LANES if last else 2 * LANES
    both = jnp.concatenate(
        [wave[...].reshape(depth * rows, LANES), side[...].reshape(depth * rows, LANES)], axis=1
    )
    high = both.astype(BF16)
    low = (both - high.astype(F32)).astype(BF16)
    matrix, rest = band_high[:, :width], band_low[:, :width]
    y_terms[:, :width] = (
        jnp.dot(high, matrix, preferred_element_type=F32)
        + jnp.dot(low, matrix, preferred_element_type=F32)
        + jnp.dot(high, rest, preferred_element_type=F32)
    )

    def one(z, part, field, before, speed, source, target):
        column = x_ext[part, z]
        turned = [None] + [
            pltpu.roll(column, rows + 2 * RADIUS - offset, 0) for offset in range(1, RADIUS)
        ]
        total = y_terms[z * rows : (z + 1) * rows, part * LANES : (part + 1) * LANES]
        for offset in range(1, RADIUS + 1):
            near = z_ext[part, RADIUS + z + offset] + z_ext[part, RADIUS + z - offset]
            if offset < RADIUS:
                near = near + turned[offset][RADIUS : RADIUS + rows]
                near = near + turned[RADIUS - offset][:rows]
            else:
                near = near + column[2 * RADIUS :] + column[:rows]
            total = total + WEIGHTS[offset - 1] * near
        if z == 0:
            total = total + source[step]
        value = 2.0 * field[z] - before[z] + speed[z] * total
        target[z] = value
        return value

    for z in range(depth):
        value = one(z, 0, wave, older, stiff, plane, fresh)
        product = forward[step, z].astype(F32) * value
        if step:
            product = product + image_in[z]
        if last:
            product = product * muting(ids, z, depth, rows)
        image[z] = product
        if not last:
            one(z, 1, side, older_side, stiff_side, plane_side, fresh_side)


def muting(ids, z, depth, rows):
    gap_z = (ids[0] * depth + z).astype(F32)
    gap_x = (
        ids[1] * rows + lax.broadcasted_iota(jnp.int32, (rows, LANES), 0) - ids[3]
    ).astype(F32)
    gap_y = (ids[2] * LANES + lane_of((rows, LANES)) - ids[4]).astype(F32)
    distance = gap_z * gap_z + gap_x * gap_x + gap_y * gap_y
    return jnp.minimum(1.0, distance / 576.0)


def step_kernel(step, ids, z_even_in, z_odd_in, x_even_in, x_odd_in, wave, side, older,
                older_side, stiff, stiff_side, forward, plane, plane_side, band_high, band_low,
                *rest):
    image_in = None
    if step:
        image_in, *rest = rest
    last = step == STEPS - 1
    if last:
        image, fresh, z_ext, x_ext, y_terms = rest
        fresh_side = None
    else:
        (image, fresh, fresh_side, z_even, z_odd, x_even, x_odd, z_ext, x_ext, y_terms) = rest
    fill(ids, wave, side, z_even_in, z_odd_in, x_even_in, x_odd_in, z_ext, x_ext)
    advance(step, ids, None, wave, side, older, older_side, stiff, stiff_side, forward, image_in,
            plane, plane_side, band_high, band_low, fresh, fresh_side, image, z_ext, x_ext,
            y_terms)
    if not last:
        write_faces(ids, fresh, fresh_side, z_even, z_odd, x_even, x_odd)


def swap(block, axis, parity):
    count = lax.axis_size(axis)
    pairs = []
    for left in range(parity, count - 1, 2):
        pairs += [(left, left + 1), (left + 1, left)]
    return lax.ppermute(block, axis, pairs)


def exchange(faces):
    z_even, z_odd, x_even, x_odd = faces
    count = lax.axis_size("gz")
    groups = [[2 * chip, 2 * chip + 1] for chip in range(count // 2)]
    x_odd = swap(x_odd, "gx", 1)
    x_even = swap(x_even, "gx", 0)
    z_odd = swap(z_odd, "gz", 1)
    z_even = lax.all_gather(z_even, "gz", axis=0, tiled=False, axis_index_groups=groups)
    return z_even, z_odd, x_even, x_odd


def on_device(
    stiffness, older_wave, wave_now, forward_wave, residuals, owners, receivers, source_cell
):
    depth, rows, cols = wave_now.shape
    span_x, span_y, span_z = (lax.axis_size(axis) for axis in ("gx", "gy", "gz"))
    tiles = span_x * span_y
    total_y = cols * span_y
    ids = jnp.stack(
        [
            lax.axis_index("gz"),
            lax.axis_index("gx"),
            lax.axis_index("gy"),
            source_cell[0] // total_y,
            source_cell[0] % total_y,
        ]
    ).astype(jnp.int32)
    band_high, band_low = (jnp.asarray(part) for part in band())
    block = shaped(depth, rows, LANES)
    z_face = shaped(RADIUS + RADIUS // 2, rows, LANES)
    x_face = shaped(depth + depth // 2, RADIUS, LANES)
    faces_out = [z_face, z_face, x_face, x_face]

    packets = call(
        functools.partial(slot_kernel, span_y, tiles),
        shaped(tiles, LANES),
        [ids, residuals, owners, owners.reshape(1, -1), receivers.reshape(1, -1)],
    )
    strips = shaped(3 * depth * STRIP // LANES, rows, LANES)
    even, odd = call(strip_pack_kernel, [strips, strips], [ids, wave_now, older_wave, stiffness])

    packets = lax.all_to_all(packets, ("gx", "gy"), 0, 0, tiled=True)
    odd = swap(odd, "gy", 1)
    even = swap(even, "gy", 0)
    side, older_side, stiff_side, *faces = call(
        strip_unpack_kernel, [block] * 3 + faces_out, [ids, even, odd, wave_now]
    )
    packets = jnp.broadcast_to(packets[None], (span_z, tiles, LANES))
    packets = lax.all_to_all(packets, "gz", 0, 0, tiled=True).reshape(span_z * tiles, LANES)
    plane_out = shaped(STEPS, rows, LANES)
    plane, plane_side = call(
        functools.partial(plane_kernel, rows),
        [plane_out, plane_out],
        [ids, packets],
        scratch=[pltpu.VMEM((LANES, span_z * tiles), F32)],
    )

    scratch = [
        pltpu.VMEM((2, depth + 2 * RADIUS, rows, LANES), F32),
        pltpu.VMEM((2, depth, rows + 2 * RADIUS, LANES), F32),
        pltpu.VMEM((depth * rows, 2 * LANES), F32),
    ]
    wave, older = wave_now, older_wave
    image = None
    for step in range(STEPS):
        faces = exchange(faces)
        ins = [ids, *faces, wave, side, older, older_side, stiffness, stiff_side, forward_wave,
               plane, plane_side, band_high, band_low]
        if step:
            ins.append(image)
        outs = [block, block]
        if step < STEPS - 1:
            outs += [block] + faces_out
        image, fresh, *rest = call(functools.partial(step_kernel, step), outs, ins, scratch)
        older, wave = wave, fresh
        if step < STEPS - 1:
            older_side, side = side, rest[0]
            faces = rest[1:]
    return image, older, wave


def solution(mesh):
    in_specs = (
        P("gz", "gx", "gy"),
        P("gz", "gx", "gy"),
        P("gz", "gx", "gy"),
        P(None, "gz", "gx", "gy"),
        P(None, ("gx", "gy", "gz")),
        P(("gx", "gy", "gz"), None),
        P(("gx", "gy", "gz")),
        P(),
    )
    out_specs = (P("gz", "gx", "gy"), P("gz", "gx", "gy"), P("gz", "gx", "gy"))
    return jax.shard_map(
        on_device, mesh=mesh, in_specs=in_specs, out_specs=out_specs, check_vma=False
    )
```

```python
import functools
import math

import jax
import jax.numpy as jnp
import numpy as np
from jax import lax
from jax.experimental import pallas as pl
from jax.experimental.pallas import tpu as pltpu
from jax.sharding import PartitionSpec as P

STEPS = 4
RADIUS = 8
LANES = 128
STRIP = 32
CAP = 8
SLOTS = 3 * CAP
F32 = jnp.float32
BF16 = jnp.bfloat16


def stencil_weights():
    window = [math.cos(math.pi * offset / 20.0) for offset in range(1, RADIUS + 1)]
    alternating = sum(
        ((-1.0) ** (offset + 1) * window[offset - 1] for offset in range(1, RADIUS + 1))
    )
    factor = 1.0 / (2.0 * alternating)
    weights = []
    for offset in range(1, RADIUS + 1):
        weights.append(
            factor * 2.0 * (-1.0) ** (offset + 1) * window[offset - 1] / (offset * offset)
        )
    return (weights, -2.0 * sum(weights))


WEIGHTS, CENTER = stencil_weights()


def band():
    size = 2 * LANES
    matrix = np.zeros((size, size), np.float64)
    for column in range(size):
        matrix[column, column] = 3.0 * CENTER
        for offset in range(1, RADIUS + 1):
            matrix[(column + offset) % size, column] = WEIGHTS[offset - 1]
            matrix[(column - offset) % size, column] = WEIGHTS[offset - 1]
    matrix = matrix.astype(np.float32)
    high = matrix.astype(jnp.bfloat16)
    low = (matrix - high.astype(np.float32)).astype(jnp.bfloat16)
    return high, low


def lane_of(shape):
    return lax.broadcasted_iota(jnp.int32, shape, len(shape) - 1)


def vmem():
    return pl.BlockSpec(memory_space=pltpu.VMEM)


def smem():
    return pl.BlockSpec(memory_space=pltpu.SMEM)


def call(body, outs, ins, scratch=(), flops=1_000_000, in_specs=None):
    return pl.pallas_call(
        body,
        out_shape=outs,
        in_specs=in_specs or [smem()] + [vmem()] * (len(ins) - 1),
        out_specs=jax.tree.map(lambda _: vmem(), outs),
        scratch_shapes=list(scratch),
        compiler_params=pltpu.CompilerParams(vmem_limit_bytes=32 * 1024 * 1024),
        cost_estimate=pl.CostEstimate(flops=flops, bytes_accessed=2_000_000, transcendentals=0),
    )(*ins)


def shaped(*shape):
    return jax.ShapeDtypeStruct(shape, F32)


def split3(value):
    high = value.astype(BF16)
    rest = value - high.astype(F32)
    middle = rest.astype(BF16)
    return high, middle, (rest - middle.astype(F32)).astype(BF16)


def dot_nt(left, right):
    return lax.dot_general(left, right, (((1,), (1,)), ((), ())), preferred_element_type=F32)


def slot_kernel(span_y, tiles, ids, residuals, owner_column, owner_row, cell_row, out):
    rows = residuals.shape[1]
    owner = owner_row[...]
    earlier = (owner_column[...] == owner) & (
        lax.broadcasted_iota(jnp.int32, (rows, rows), 0)
        < lax.broadcasted_iota(jnp.int32, (rows, rows), 1)
    )
    rank = jnp.sum(earlier.astype(jnp.int32), axis=0, keepdims=True)
    cell = cell_row[...]
    along = cell & (LANES - 1)
    fields = [residuals[pl.ds(field, 1), :] for field in range(STEPS)] + [cell.astype(F32)]
    stacked = jnp.concatenate(
        [jnp.broadcast_to(field, (SLOTS, rows)) for field in fields]
        + [jnp.zeros((LANES - SLOTS * len(fields), rows), F32)],
        axis=0,
    )
    line = lax.broadcasted_iota(jnp.int32, (LANES, rows), 0)
    slot = line - SLOTS * (line // SLOTS)
    tile = lax.broadcasted_iota(jnp.int32, (tiles, rows), 0)
    place = tile & (span_y - 1)
    total = jnp.zeros((tiles, LANES), F32)
    for group in range(3):
        named = owner == tile + (group - 1)
        wanted = slot == rank + CAP * group
        if group == 0:
            named = named & (place != 0)
            wanted = wanted & (along >= LANES - STRIP)
        if group == 2:
            named = named & (place != span_y - 1)
            wanted = wanted & (along < STRIP)
        chosen = named.astype(F32).astype(BF16)
        for part in split3(jnp.where(wanted, stacked, 0.0)):
            total = total + dot_nt(chosen, part)
    out[...] = total


def plane_kernel(rows, ids, *refs):
    *packets, main, side, turned = refs
    main[...] = jnp.zeros(main.shape, F32)
    side[...] = jnp.zeros(side.shape, F32)

    @pl.when(ids[0] == 0)
    def _():
        count = turned.shape[1]
        share = count // len(packets)
        for number, packet in enumerate(packets):
            turned[:, share * number : share * (number + 1)] = jnp.transpose(packet[...])
        line = lax.broadcasted_iota(jnp.int32, (rows, count), 0)
        spot = lax.broadcasted_iota(jnp.int32, (LANES, count), 0)

        def product(slot):
            cell = turned[pl.ds(SLOTS * STEPS + slot, 1), :].astype(jnp.int32)
            hit = (cell >> 7) == line
            highs, lows = [], []
            for step in range(STEPS):
                value = turned[pl.ds(SLOTS * step + slot, 1), :]
                high = value.astype(BF16).astype(F32)
                highs.append(jnp.where(hit, high, 0.0))
                lows.append(jnp.where(hit, value - high, 0.0))
            left = jnp.concatenate(highs + lows, axis=0).astype(BF16)
            right = jnp.where((cell & (LANES - 1)) == spot, 1.0, 0.0).astype(BF16)
            both = dot_nt(left, right)
            return both[: STEPS * rows] + both[STEPS * rows :]

        for slot in range(SLOTS):
            target = main if slot // CAP == 1 else side
            target[...] += product(slot).reshape(target.shape)


def strip_pack_kernel(ids, wave, older, stiff, even, odd):
    parity = ids[2] & 1
    quarter = lane_of(wave.shape[1:]) // STRIP
    low, high = quarter == 0, quarter == 3
    quarters = LANES // STRIP
    for number, field in enumerate((wave, older, stiff)):
        for chunk in range(field.shape[0] // quarters):
            lows = highs = None
            for turn in range(quarters):
                value = field[quarters * chunk + turn]
                one = jnp.where(low, value, 0.0)
                two = jnp.where(high, value, 0.0)
                if turn:
                    one = pltpu.roll(one, STRIP * turn, 1)
                    two = pltpu.roll(two, STRIP * turn, 1)
                lows = one if lows is None else lows + one
                highs = two if highs is None else highs + two
            place = number * (field.shape[0] // quarters) + chunk
            even[place] = jnp.where(parity == 0, highs, lows)
            odd[place] = jnp.where(parity == 0, lows, highs)


def strip_width(step):
    return {0: STRIP, 1: STRIP // 2, 2: STRIP // 4}.get(step, 0)


def folds(width):
    return LANES // (2 * width) if width else 0


def folded(length, width):
    return length // folds(width) if width else 0


def kept_lanes(shape, width):
    lane = lane_of(shape)
    return (lane < width) | (lane >= LANES - width)


def fold(pieces, width):
    total = None
    for turn, piece in enumerate(pieces):
        piece = jnp.where(kept_lanes(piece.shape, width), piece, 0.0)
        if turn:
            piece = pltpu.roll(piece, 2 * width * turn, 1)
        total = piece if total is None else total + piece
    return total


def unfold(both, turn, width):
    if turn:
        both = pltpu.roll(both, LANES - 2 * width * turn, 1)
    return jnp.where(kept_lanes(both.shape, width), both, 0.0)


def write_faces(width, ids, main, side, z_even, z_odd, x_even, x_odd):
    z_parity, x_parity = ids[0] & 1, ids[1] & 1
    depth, rows, _ = main.shape
    count = folds(width)
    for face, start in (
        (z_even, (depth - RADIUS) * (1 - z_parity)),
        (z_odd, (depth - RADIUS) * z_parity),
    ):
        face[pl.ds(0, RADIUS)] = main[pl.ds(start, RADIUS)]
        span = folded(RADIUS, width)
        for plane in range(span):
            face[RADIUS + plane] = fold(
                [side[start + plane + span * turn] for turn in range(count)], width
            )
    for face, start in (
        (x_even, (rows - RADIUS) * (1 - x_parity)),
        (x_odd, (rows - RADIUS) * x_parity),
    ):
        start = pl.multiple_of(start, RADIUS)
        face[pl.ds(0, depth)] = main[:, pl.ds(start, RADIUS), :]
        span = folded(depth, width)
        for plane in range(span):
            face[depth + plane] = fold(
                [side[plane + span * turn, pl.ds(start, RADIUS), :] for turn in range(count)],
                width,
            )


def strip_unpack_kernel(
    ids, even, odd, wave, wave_side, older_side, stiff_side, z_even, z_odd, x_even, x_odd
):
    parity = ids[2] & 1
    quarters = LANES // STRIP
    quarter = lane_of(wave.shape[1:]) // STRIP
    from_even = quarter == 3 * parity
    from_odd = quarter == 3 * (1 - parity)
    chunks = wave.shape[0] // quarters
    for number, side in enumerate((wave_side, older_side, stiff_side)):
        for chunk in range(chunks):
            one, two = even[number * chunks + chunk], odd[number * chunks + chunk]
            for turn in range(quarters):
                back = (LANES - STRIP * turn) % LANES
                first = pltpu.roll(one, back, 1) if back else one
                second = pltpu.roll(two, back, 1) if back else two
                side[quarters * chunk + turn] = jnp.where(
                    from_even, first, jnp.where(from_odd, second, 0.0)
                )
    write_faces(STRIP, ids, wave, wave_side, z_even, z_odd, x_even, x_odd)


def fill(width, ids, wave, side, z_even, z_odd, x_even, x_odd, z_ext, x_ext):
    z_parity, x_parity = ids[0] & 1, ids[1] & 1
    depth, rows, _ = wave.shape
    count = folds(width)
    for part, field in enumerate((wave, side) if width else (wave,)):
        z_ext[part, pl.ds(RADIUS, depth)] = field[...]
        x_ext[part, :, pl.ds(RADIUS, rows), :] = field[...]
    pair = z_even.at[1 - z_parity]
    for face, start in (
        (pair, (depth + RADIUS) * (1 - z_parity)),
        (z_odd, (depth + RADIUS) * z_parity),
    ):
        z_ext[0, pl.ds(start, RADIUS)] = face[pl.ds(0, RADIUS)]
        span = folded(RADIUS, width)
        for plane in range(span):
            both = face[RADIUS + plane]
            for turn in range(count):
                z_ext[1, start + plane + span * turn] = unfold(both, turn, width)
    for face, start in (
        (x_even, (rows + RADIUS) * (1 - x_parity)),
        (x_odd, (rows + RADIUS) * x_parity),
    ):
        start = pl.multiple_of(start, RADIUS)
        x_ext[0, :, pl.ds(start, RADIUS), :] = face[pl.ds(0, depth)]
        span = folded(depth, width)
        for plane in range(span):
            both = face[depth + plane]
            for turn in range(count):
                x_ext[1, plane + span * turn, pl.ds(start, RADIUS), :] = unfold(both, turn, width)


def advance(step, ids, refs, wave, side, older, older_side, stiff, stiff_side, forward, image_in,
            plane, plane_side, band_high, band_low, fresh, fresh_side, image, z_ext, x_ext, y_terms):
    depth, rows, _ = wave.shape
    last = step == STEPS - 1
    width = LANES if last else 2 * LANES
    both = jnp.concatenate(
        [wave[...].reshape(depth * rows, LANES), side[...].reshape(depth * rows, LANES)], axis=1
    )
    high = both.astype(BF16)
    low = (both - high.astype(F32)).astype(BF16)
    matrix, rest = band_high[:, :width], band_low[:, :width]
    y_terms[:, :width] = (
        jnp.dot(high, matrix, preferred_element_type=F32)
        + jnp.dot(low, matrix, preferred_element_type=F32)
        + jnp.dot(high, rest, preferred_element_type=F32)
    )

    def one(z, part, field, before, speed, source, target):
        column = x_ext[part, z]
        turned = [None] + [
            pltpu.roll(column, rows + 2 * RADIUS - offset, 0) for offset in range(1, RADIUS)
        ]
        total = y_terms[z * rows : (z + 1) * rows, part * LANES : (part + 1) * LANES]
        for offset in range(1, RADIUS + 1):
            near = z_ext[part, RADIUS + z + offset] + z_ext[part, RADIUS + z - offset]
            if offset < RADIUS:
                near = near + turned[offset][RADIUS : RADIUS + rows]
                near = near + turned[RADIUS - offset][:rows]
            else:
                near = near + column[2 * RADIUS :] + column[:rows]
            total = total + WEIGHTS[offset - 1] * near
        if z == 0:
            total = total + source[step]
        value = 2.0 * field[z] - before[z] + speed[z] * total
        target[z] = value
        return value

    for z in range(depth):
        value = one(z, 0, wave, older, stiff, plane, fresh)
        product = forward[step, z].astype(F32) * value
        if step:
            product = product + image_in[z]
        if last:
            product = product * muting(ids, z, depth, rows)
        image[z] = product
        if not last:
            one(z, 1, side, older_side, stiff_side, plane_side, fresh_side)


def muting(ids, z, depth, rows):
    gap_z = (ids[0] * depth + z).astype(F32)
    gap_x = (
        ids[1] * rows + lax.broadcasted_iota(jnp.int32, (rows, LANES), 0) - ids[3]
    ).astype(F32)
    gap_y = (ids[2] * LANES + lane_of((rows, LANES)) - ids[4]).astype(F32)
    distance = gap_z * gap_z + gap_x * gap_x + gap_y * gap_y
    return jnp.minimum(1.0, distance / 576.0)


def step_kernel(step, ids, x_odd_in, x_even_in, z_odd_in, z_even_in, wave, side, older,
                older_side, stiff, stiff_side, forward, plane, plane_side, band_high, band_low,
                *rest):
    image_in = None
    if step:
        image_in, *rest = rest
    last = step == STEPS - 1
    if last:
        image, fresh, z_ext, x_ext, y_terms = rest
        fresh_side = None
    else:
        (image, fresh, fresh_side, z_even, z_odd, x_even, x_odd, z_ext, x_ext, y_terms) = rest
    fill(strip_width(step), ids, wave, side, z_even_in, z_odd_in, x_even_in, x_odd_in, z_ext, x_ext)
    advance(step, ids, None, wave, side, older, older_side, stiff, stiff_side, forward, image_in,
            plane, plane_side, band_high, band_low, fresh, fresh_side, image, z_ext, x_ext,
            y_terms)
    if not last:
        write_faces(strip_width(step + 1), ids, fresh, fresh_side, z_even, z_odd, x_even, x_odd)


def swap(block, axis, parity):
    count = lax.axis_size(axis)
    pairs = []
    for left in range(parity, count - 1, 2):
        pairs += [(left, left + 1), (left + 1, left)]
    return lax.ppermute(block, axis, pairs)


def core_pairs(count):
    return [[2 * chip, 2 * chip + 1] for chip in range(count // 2)]


def exchange(faces):
    z_even, z_odd, x_even, x_odd = faces
    count = lax.axis_size("gz")
    groups = core_pairs(count)
    z_odd = swap(z_odd, "gz", 1)
    x_even = swap(x_even, "gx", 0)
    x_odd = swap(x_odd, "gx", 1)
    z_even = lax.all_gather(z_even, "gz", axis=0, tiled=False, axis_index_groups=groups)
    return z_even, z_odd, x_even, x_odd


def on_device(
    stiffness, older_wave, wave_now, forward_wave, residuals, owners, receivers, source_cell
):
    depth, rows, cols = wave_now.shape
    span_x, span_y, span_z = (lax.axis_size(axis) for axis in ("gx", "gy", "gz"))
    tiles = span_x * span_y
    total_y = cols * span_y
    ids = jnp.stack(
        [
            lax.axis_index("gz"),
            lax.axis_index("gx"),
            lax.axis_index("gy"),
            source_cell[0] // total_y,
            source_cell[0] % total_y,
        ]
    ).astype(jnp.int32)
    band_high, band_low = (jnp.asarray(part) for part in band())
    block = shaped(depth, rows, LANES)

    def faces_out(step):
        width = strip_width(step)
        z_face = shaped(RADIUS + folded(RADIUS, width), rows, LANES)
        x_face = shaped(depth + folded(depth, width), RADIUS, LANES)
        return [z_face, z_face, x_face, x_face]

    packets = call(
        functools.partial(slot_kernel, span_y, tiles),
        shaped(tiles, LANES),
        [ids, residuals, owners, owners.reshape(1, -1), receivers.reshape(1, -1)],
    )
    packets = lax.all_to_all(packets, ("gx", "gy"), 0, 0, tiled=True)
    ids, packets = lax.optimization_barrier((ids, packets))
    strips = shaped(3 * depth * STRIP // LANES, rows, LANES)
    even, odd = call(strip_pack_kernel, [strips, strips], [ids, wave_now, older_wave, stiffness])

    odd = swap(odd, "gy", 1)
    even = swap(even, "gy", 0)
    side, older_side, stiff_side, *faces = call(
        strip_unpack_kernel, [block] * 3 + faces_out(0), [ids, even, odd, wave_now]
    )
    packets = lax.all_gather(
        packets, "gz", axis=0, tiled=True, axis_index_groups=core_pairs(span_z)
    )
    packets = [packets] + [
        lax.ppermute(packets, "gz", [(layer, 0)]) for layer in range(2, span_z, 2)
    ]
    plane_out = shaped(STEPS, rows, LANES)
    plane, plane_side = call(
        functools.partial(plane_kernel, rows),
        [plane_out, plane_out],
        [ids, *packets],
        scratch=[pltpu.VMEM((LANES, span_z * tiles), F32)],
    )

    scratch = [
        pltpu.VMEM((2, depth + 2 * RADIUS, rows, LANES), F32),
        pltpu.VMEM((2, depth, rows + 2 * RADIUS, LANES), F32),
        pltpu.VMEM((depth * rows, 2 * LANES), F32),
    ]
    wave, older = wave_now, older_wave
    image = None
    for step in range(STEPS):
        faces = exchange(faces)
        ins = [ids, *faces[::-1], wave, side, older, older_side, stiffness, stiff_side, forward_wave,
               plane, plane_side, band_high, band_low]
        if step:
            ins.append(image)
        outs = [block, block]
        if step < STEPS - 1:
            outs += [block] + faces_out(step + 1)
        image, fresh, *rest = call(functools.partial(step_kernel, step), outs, ins, scratch)
        older, wave = wave, fresh
        if step < STEPS - 1:
            older_side, side = side, rest[0]
            faces = rest[1:]
    return image, older, wave


def solution(mesh):
    in_specs = (
        P("gz", "gx", "gy"),
        P("gz", "gx", "gy"),
        P("gz", "gx", "gy"),
        P(None, "gz", "gx", "gy"),
        P(None, ("gx", "gy", "gz")),
        P(("gx", "gy", "gz"), None),
        P(("gx", "gy", "gz")),
        P(),
    )
    out_specs = (P("gz", "gx", "gy"), P("gz", "gx", "gy"), P("gz", "gx", "gy"))
    return jax.shard_map(
        on_device, mesh=mesh, in_specs=in_specs, out_specs=out_specs, check_vma=False
    )
```

```python
import functools
import math

import jax
import jax.numpy as jnp
import numpy as np
from jax import lax
from jax.experimental import pallas as pl
from jax.experimental.pallas import tpu as pltpu
from jax.sharding import PartitionSpec as P

STEPS = 4
RADIUS = 8
LANES = 128
STRIP = 32
CAP = 8
SLOTS = 3 * CAP
F32 = jnp.float32
BF16 = jnp.bfloat16


def stencil_weights():
    window = [math.cos(math.pi * offset / 20.0) for offset in range(1, RADIUS + 1)]
    alternating = sum(
        ((-1.0) ** (offset + 1) * window[offset - 1] for offset in range(1, RADIUS + 1))
    )
    factor = 1.0 / (2.0 * alternating)
    weights = []
    for offset in range(1, RADIUS + 1):
        weights.append(
            factor * 2.0 * (-1.0) ** (offset + 1) * window[offset - 1] / (offset * offset)
        )
    return (weights, -2.0 * sum(weights))


WEIGHTS, CENTER = stencil_weights()


def band():
    size = 2 * LANES
    matrix = np.zeros((size, size), np.float64)
    for column in range(size):
        matrix[column, column] = 3.0 * CENTER
        for offset in range(1, RADIUS + 1):
            matrix[(column + offset) % size, column] = WEIGHTS[offset - 1]
            matrix[(column - offset) % size, column] = WEIGHTS[offset - 1]
    matrix = matrix.astype(np.float32)
    high = matrix.astype(jnp.bfloat16)
    low = (matrix - high.astype(np.float32)).astype(jnp.bfloat16)
    return high, low


def lane_of(shape):
    return lax.broadcasted_iota(jnp.int32, shape, len(shape) - 1)


def vmem():
    return pl.BlockSpec(memory_space=pltpu.VMEM)


def smem():
    return pl.BlockSpec(memory_space=pltpu.SMEM)


def call(body, outs, ins, scratch=(), flops=1_000_000, in_specs=None):
    return pl.pallas_call(
        body,
        out_shape=outs,
        in_specs=in_specs or [smem()] + [vmem()] * (len(ins) - 1),
        out_specs=jax.tree.map(lambda _: vmem(), outs),
        scratch_shapes=list(scratch),
        compiler_params=pltpu.CompilerParams(vmem_limit_bytes=32 * 1024 * 1024),
        cost_estimate=pl.CostEstimate(flops=flops, bytes_accessed=2_000_000, transcendentals=0),
    )(*ins)


def shaped(*shape):
    return jax.ShapeDtypeStruct(shape, F32)


def split3(value):
    high = value.astype(BF16)
    rest = value - high.astype(F32)
    middle = rest.astype(BF16)
    return high, middle, (rest - middle.astype(F32)).astype(BF16)


def dot_nt(left, right):
    return lax.dot_general(left, right, (((1,), (1,)), ((), ())), preferred_element_type=F32)


def prepare_kernel(span_y, tiles, ids, residuals, owners, cells, wave, older, stiff, packets,
                   even, odd):
    pack_slots(span_y, tiles, residuals, owners, cells, packets)
    pack_strips(ids, wave, older, stiff, even, odd)


def pack_slots(span_y, tiles, residuals, owner_row, cell_row, out):
    rows = residuals.shape[1]
    owner = owner_row[...]
    owner_column = jnp.transpose(jnp.broadcast_to(owner.astype(F32), (rows, rows)))
    earlier = (owner_column.astype(jnp.int32) == owner) & (
        lax.broadcasted_iota(jnp.int32, (rows, rows), 0)
        < lax.broadcasted_iota(jnp.int32, (rows, rows), 1)
    )
    rank = jnp.sum(earlier.astype(jnp.int32), axis=0, keepdims=True)
    cell = cell_row[...]
    along = cell & (LANES - 1)
    fields = [residuals[pl.ds(field, 1), :] for field in range(STEPS)] + [cell.astype(F32)]
    stacked = jnp.concatenate(
        [jnp.broadcast_to(field, (SLOTS, rows)) for field in fields]
        + [jnp.zeros((LANES - SLOTS * len(fields), rows), F32)],
        axis=0,
    )
    line = lax.broadcasted_iota(jnp.int32, (LANES, rows), 0)
    slot = line - SLOTS * (line // SLOTS)
    tile = lax.broadcasted_iota(jnp.int32, (tiles, rows), 0)
    place = tile & (span_y - 1)
    total = jnp.zeros((tiles, LANES), F32)
    for group in range(3):
        named = owner == tile + (group - 1)
        wanted = slot == rank + CAP * group
        if group == 0:
            named = named & (place != 0)
            wanted = wanted & (along >= LANES - STRIP)
        if group == 2:
            named = named & (place != span_y - 1)
            wanted = wanted & (along < STRIP)
        chosen = named.astype(F32).astype(BF16)
        for part in split3(jnp.where(wanted, stacked, 0.0)):
            total = total + dot_nt(chosen, part)
    out[...] = total


def plane_kernel(rows, ids, *refs):
    *packets, main, side, turned = refs
    main[...] = jnp.zeros(main.shape, F32)
    side[...] = jnp.zeros(side.shape, F32)

    @pl.when(ids[0] == 0)
    def _():
        count = turned.shape[1]
        share = count // len(packets)
        for number, packet in enumerate(packets):
            turned[:, share * number : share * (number + 1)] = jnp.transpose(packet[...])
        line = lax.broadcasted_iota(jnp.int32, (rows, count), 0)
        spot = lax.broadcasted_iota(jnp.int32, (LANES, count), 0)

        def product(slot):
            cell = turned[pl.ds(SLOTS * STEPS + slot, 1), :].astype(jnp.int32)
            hit = (cell >> 7) == line
            highs, lows = [], []
            for step in range(STEPS):
                value = turned[pl.ds(SLOTS * step + slot, 1), :]
                high = value.astype(BF16).astype(F32)
                highs.append(jnp.where(hit, high, 0.0))
                lows.append(jnp.where(hit, value - high, 0.0))
            left = jnp.concatenate(highs + lows, axis=0).astype(BF16)
            right = jnp.where((cell & (LANES - 1)) == spot, 1.0, 0.0).astype(BF16)
            both = dot_nt(left, right)
            return both[: STEPS * rows] + both[STEPS * rows :]

        for slot in range(SLOTS):
            target = main if slot // CAP == 1 else side
            target[...] += product(slot).reshape(target.shape)


def pack_strips(ids, wave, older, stiff, even, odd):
    parity = ids[2] & 1
    quarter = lane_of(wave.shape[1:]) // STRIP
    low, high = quarter == 0, quarter == 3
    quarters = LANES // STRIP
    for number, field in enumerate((wave, older, stiff)):
        for chunk in range(field.shape[0] // quarters):
            lows = highs = None
            for turn in range(quarters):
                value = field[quarters * chunk + turn]
                one = jnp.where(low, value, 0.0)
                two = jnp.where(high, value, 0.0)
                if turn:
                    one = pltpu.roll(one, STRIP * turn, 1)
                    two = pltpu.roll(two, STRIP * turn, 1)
                lows = one if lows is None else lows + one
                highs = two if highs is None else highs + two
            place = number * (field.shape[0] // quarters) + chunk
            even[place] = jnp.where(parity == 0, highs, lows)
            odd[place] = jnp.where(parity == 0, lows, highs)


def strip_width(step):
    return {0: STRIP, 1: STRIP // 2, 2: STRIP // 4}.get(step, 0)


def folds(width):
    return LANES // (2 * width) if width else 0


def folded(length, width):
    return length // folds(width) if width else 0


def kept_lanes(shape, width):
    lane = lane_of(shape)
    return (lane < width) | (lane >= LANES - width)


def fold(pieces, width):
    total = None
    for turn, piece in enumerate(pieces):
        piece = jnp.where(kept_lanes(piece.shape, width), piece, 0.0)
        if turn:
            piece = pltpu.roll(piece, 2 * width * turn, 1)
        total = piece if total is None else total + piece
    return total


def unfold(both, turn, width):
    if turn:
        both = pltpu.roll(both, LANES - 2 * width * turn, 1)
    return jnp.where(kept_lanes(both.shape, width), both, 0.0)


def write_faces(width, ids, main, side, z_even, z_odd, x_even, x_odd):
    z_parity, x_parity = ids[0] & 1, ids[1] & 1
    depth, rows, _ = main.shape
    count = folds(width)
    for face, start in (
        (z_even, (depth - RADIUS) * (1 - z_parity)),
        (z_odd, (depth - RADIUS) * z_parity),
    ):
        face[pl.ds(0, RADIUS)] = main[pl.ds(start, RADIUS)]
        span = folded(RADIUS, width)
        for plane in range(span):
            face[RADIUS + plane] = fold(
                [side[start + plane + span * turn] for turn in range(count)], width
            )
    for face, start in (
        (x_even, (rows - RADIUS) * (1 - x_parity)),
        (x_odd, (rows - RADIUS) * x_parity),
    ):
        start = pl.multiple_of(start, RADIUS)
        face[pl.ds(0, depth)] = main[:, pl.ds(start, RADIUS), :]
        span = folded(depth, width)
        for plane in range(span):
            face[depth + plane] = fold(
                [side[plane + span * turn, pl.ds(start, RADIUS), :] for turn in range(count)],
                width,
            )


def strip_unpack_kernel(
    span_y, ids, even, odd, wave, wave_side, older_side, stiff_side, z_even, z_odd, x_even, x_odd
):
    parity = ids[2] & 1
    quarters = LANES // STRIP
    quarter = lane_of(wave.shape[1:]) // STRIP
    from_even = quarter == 3 * parity
    edge = jnp.where(parity == 0, ids[2] == 0, ids[2] == span_y - 1)
    from_odd = quarter == jnp.where(edge, -1, 3 * (1 - parity))
    chunks = wave.shape[0] // quarters
    for number, side in enumerate((wave_side, older_side, stiff_side)):
        for chunk in range(chunks):
            one = even[1 - parity, number * chunks + chunk]
            two = odd[parity, number * chunks + chunk]
            for turn in range(quarters):
                back = (LANES - STRIP * turn) % LANES
                first = pltpu.roll(one, back, 1) if back else one
                second = pltpu.roll(two, back, 1) if back else two
                side[quarters * chunk + turn] = jnp.where(
                    from_even, first, jnp.where(from_odd, second, 0.0)
                )
    write_faces(STRIP, ids, wave, wave_side, z_even, z_odd, x_even, x_odd)


def fill(width, ids, wave, side, z_even, z_odd, x_even, x_odd, z_ext, x_ext):
    z_parity, x_parity = ids[0] & 1, ids[1] & 1
    depth, rows, _ = wave.shape
    count = folds(width)
    for part, field in enumerate((wave, side) if width else (wave,)):
        z_ext[part, pl.ds(RADIUS, depth)] = field[...]
        x_ext[part, :, pl.ds(RADIUS, rows), :] = field[...]
    pair = z_even.at[1 - z_parity]
    for face, start in (
        (pair, (depth + RADIUS) * (1 - z_parity)),
        (z_odd, (depth + RADIUS) * z_parity),
    ):
        z_ext[0, pl.ds(start, RADIUS)] = face[pl.ds(0, RADIUS)]
        span = folded(RADIUS, width)
        for plane in range(span):
            both = face[RADIUS + plane]
            for turn in range(count):
                z_ext[1, start + plane + span * turn] = unfold(both, turn, width)
    for face, start in (
        (x_even, (rows + RADIUS) * (1 - x_parity)),
        (x_odd, (rows + RADIUS) * x_parity),
    ):
        start = pl.multiple_of(start, RADIUS)
        x_ext[0, :, pl.ds(start, RADIUS), :] = face[pl.ds(0, depth)]
        span = folded(depth, width)
        for plane in range(span):
            both = face[depth + plane]
            for turn in range(count):
                x_ext[1, plane + span * turn, pl.ds(start, RADIUS), :] = unfold(both, turn, width)


def advance(step, ids, refs, wave, side, older, older_side, stiff, stiff_side, forward, image_in,
            plane, plane_side, band_high, band_low, fresh, fresh_side, image, z_ext, x_ext, y_terms):
    depth, rows, _ = wave.shape
    last = step == STEPS - 1
    width = LANES if last else 2 * LANES
    both = jnp.concatenate(
        [wave[...].reshape(depth * rows, LANES), side[...].reshape(depth * rows, LANES)], axis=1
    )
    high = both.astype(BF16)
    low = (both - high.astype(F32)).astype(BF16)
    matrix, rest = band_high[:, :width], band_low[:, :width]
    y_terms[:, :width] = (
        jnp.dot(high, matrix, preferred_element_type=F32)
        + jnp.dot(low, matrix, preferred_element_type=F32)
        + jnp.dot(high, rest, preferred_element_type=F32)
    )

    def one(z, part, field, before, speed, source, target):
        column = x_ext[part, z]
        turned = [None] + [
            pltpu.roll(column, rows + 2 * RADIUS - offset, 0) for offset in range(1, RADIUS)
        ]
        total = y_terms[z * rows : (z + 1) * rows, part * LANES : (part + 1) * LANES]
        for offset in range(1, RADIUS + 1):
            near = z_ext[part, RADIUS + z + offset] + z_ext[part, RADIUS + z - offset]
            if offset < RADIUS:
                near = near + turned[offset][RADIUS : RADIUS + rows]
                near = near + turned[RADIUS - offset][:rows]
            else:
                near = near + column[2 * RADIUS :] + column[:rows]
            total = total + WEIGHTS[offset - 1] * near
        if z == 0:
            total = total + source[step]
        value = 2.0 * field[z] - before[z] + speed[z] * total
        target[z] = value
        return value

    for z in range(depth):
        value = one(z, 0, wave, older, stiff, plane, fresh)
        product = forward[step, z].astype(F32) * value
        if step:
            product = product + image_in[z]
        if last:
            product = product * muting(ids, z, depth, rows)
        image[z] = product
        if not last:
            one(z, 1, side, older_side, stiff_side, plane_side, fresh_side)


def muting(ids, z, depth, rows):
    gap_z = (ids[0] * depth + z).astype(F32)
    gap_x = (
        ids[1] * rows + lax.broadcasted_iota(jnp.int32, (rows, LANES), 0) - ids[3]
    ).astype(F32)
    gap_y = (ids[2] * LANES + lane_of((rows, LANES)) - ids[4]).astype(F32)
    distance = gap_z * gap_z + gap_x * gap_x + gap_y * gap_y
    return jnp.minimum(1.0, distance / 576.0)


def step_kernel(step, ids, x_odd_in, x_even_in, z_odd_in, z_even_in, wave, side, older,
                older_side, stiff, stiff_side, forward, plane, plane_side, band_high, band_low,
                *rest):
    image_in = None
    if step:
        image_in, *rest = rest
    last = step == STEPS - 1
    if last:
        image, fresh, z_ext, x_ext, y_terms = rest
        fresh_side = None
    else:
        (image, fresh, fresh_side, z_even, z_odd, x_even, x_odd, z_ext, x_ext, y_terms) = rest
    fill(strip_width(step), ids, wave, side, z_even_in, z_odd_in, x_even_in, x_odd_in, z_ext, x_ext)
    advance(step, ids, None, wave, side, older, older_side, stiff, stiff_side, forward, image_in,
            plane, plane_side, band_high, band_low, fresh, fresh_side, image, z_ext, x_ext,
            y_terms)
    if not last:
        write_faces(strip_width(step + 1), ids, fresh, fresh_side, z_even, z_odd, x_even, x_odd)


def swap(block, axis, parity):
    count = lax.axis_size(axis)
    pairs = []
    for left in range(parity, count - 1, 2):
        pairs += [(left, left + 1), (left + 1, left)]
    return lax.ppermute(block, axis, pairs)


def pair_gather(block, axis, parity):
    count = lax.axis_size(axis)
    groups = [
        [(2 * pair + parity) % count, (2 * pair + parity + 1) % count]
        for pair in range(count // 2)
    ]
    return lax.all_gather(block, axis, axis=0, tiled=False, axis_index_groups=groups)


def exchange(faces):
    z_even, z_odd, x_even, x_odd = faces
    z_odd = swap(z_odd, "gz", 1)
    x_even = swap(x_even, "gx", 0)
    x_odd = swap(x_odd, "gx", 1)
    z_even = pair_gather(z_even, "gz", 0)
    return z_even, z_odd, x_even, x_odd


def on_device(
    stiffness, older_wave, wave_now, forward_wave, residuals, owners, receivers, source_cell
):
    depth, rows, cols = wave_now.shape
    span_x, span_y, span_z = (lax.axis_size(axis) for axis in ("gx", "gy", "gz"))
    tiles = span_x * span_y
    total_y = cols * span_y
    ids = jnp.stack(
        [
            lax.axis_index("gz"),
            lax.axis_index("gx"),
            lax.axis_index("gy"),
            source_cell[0] // total_y,
            source_cell[0] % total_y,
        ]
    ).astype(jnp.int32)
    band_high, band_low = (jnp.asarray(part) for part in band())
    block = shaped(depth, rows, LANES)

    def faces_out(step):
        width = strip_width(step)
        z_face = shaped(RADIUS + folded(RADIUS, width), rows, LANES)
        x_face = shaped(depth + folded(depth, width), RADIUS, LANES)
        return [z_face, z_face, x_face, x_face]

    strips = shaped(3 * depth * STRIP // LANES, rows, LANES)
    packets, even, odd = call(
        functools.partial(prepare_kernel, span_y, tiles),
        [shaped(tiles, LANES), strips, strips],
        [ids, residuals, owners.reshape(1, -1), receivers.reshape(1, -1), wave_now, older_wave,
         stiffness],
        in_specs=[smem()] + [pl.BlockSpec()] * 6,
    )
    packets = lax.all_to_all(packets, ("gx", "gy"), 0, 0, tiled=True)
    even, odd = (pair_gather(strip, "gy", parity) for parity, strip in enumerate((even, odd)))
    side, older_side, stiff_side, *faces = call(
        functools.partial(strip_unpack_kernel, span_y),
        [block] * 3 + faces_out(0),
        [ids, even, odd, wave_now],
    )
    packets, faces = lax.optimization_barrier((packets, faces))
    packets = pair_gather(packets, "gz", 0).reshape(2 * tiles, LANES)
    packets = [packets] + [
        lax.ppermute(packets, "gz", [(layer, 0)]) for layer in range(2, span_z, 2)
    ]
    plane_out = shaped(STEPS, rows, LANES)
    plane, plane_side = call(
        functools.partial(plane_kernel, rows),
        [plane_out, plane_out],
        [ids, *packets],
        scratch=[pltpu.VMEM((LANES, span_z * tiles), F32)],
    )

    scratch = [
        pltpu.VMEM((2, depth + 2 * RADIUS, rows, LANES), F32),
        pltpu.VMEM((2, depth, rows + 2 * RADIUS, LANES), F32),
        pltpu.VMEM((depth * rows, 2 * LANES), F32),
    ]
    wave, older = wave_now, older_wave
    image = None
    for step in range(STEPS):
        faces = exchange(faces)
        ins = [ids, *faces[::-1], wave, side, older, older_side, stiffness, stiff_side, forward_wave,
               plane, plane_side, band_high, band_low]
        if step:
            ins.append(image)
        outs = [block, block]
        if step < STEPS - 1:
            outs += [block] + faces_out(step + 1)
        image, fresh, *rest = call(functools.partial(step_kernel, step), outs, ins, scratch)
        older, wave = wave, fresh
        if step < STEPS - 1:
            older_side, side = side, rest[0]
            faces = rest[1:]
    return image, older, wave


def solution(mesh):
    in_specs = (
        P("gz", "gx", "gy"),
        P("gz", "gx", "gy"),
        P("gz", "gx", "gy"),
        P(None, "gz", "gx", "gy"),
        P(None, ("gx", "gy", "gz")),
        P(("gx", "gy", "gz"), None),
        P(("gx", "gy", "gz")),
        P(),
    )
    out_specs = (P("gz", "gx", "gy"), P("gz", "gx", "gy"), P("gz", "gx", "gy"))
    return jax.shard_map(
        on_device, mesh=mesh, in_specs=in_specs, out_specs=out_specs, check_vma=False
    )
```

```python
import functools
import math

import jax
import jax.numpy as jnp
import numpy as np
from jax import lax
from jax.experimental import pallas as pl
from jax.experimental.pallas import tpu as pltpu
from jax.sharding import PartitionSpec as P

STEPS = 4
RADIUS = 8
LANES = 128
STRIP = 32
CAP = 8
SLOTS = 3 * CAP
F32 = jnp.float32
BF16 = jnp.bfloat16


def stencil_weights():
    window = [math.cos(math.pi * offset / 20.0) for offset in range(1, RADIUS + 1)]
    alternating = sum(
        ((-1.0) ** (offset + 1) * window[offset - 1] for offset in range(1, RADIUS + 1))
    )
    factor = 1.0 / (2.0 * alternating)
    weights = []
    for offset in range(1, RADIUS + 1):
        weights.append(
            factor * 2.0 * (-1.0) ** (offset + 1) * window[offset - 1] / (offset * offset)
        )
    return (weights, -2.0 * sum(weights))


WEIGHTS, CENTER = stencil_weights()


def band():
    size = 2 * LANES
    matrix = np.zeros((size, size), np.float64)
    for column in range(size):
        matrix[column, column] = 3.0 * CENTER
        for offset in range(1, RADIUS + 1):
            matrix[(column + offset) % size, column] = WEIGHTS[offset - 1]
            matrix[(column - offset) % size, column] = WEIGHTS[offset - 1]
    matrix = matrix.astype(np.float32)
    high = matrix.astype(jnp.bfloat16)
    low = (matrix - high.astype(np.float32)).astype(jnp.bfloat16)
    return high, low


def lane_of(shape):
    return lax.broadcasted_iota(jnp.int32, shape, len(shape) - 1)


def vmem():
    return pl.BlockSpec(memory_space=pltpu.VMEM)


def smem():
    return pl.BlockSpec(memory_space=pltpu.SMEM)


def call(body, outs, ins, scratch=(), in_specs=None, grant=32):
    return pl.pallas_call(
        body,
        out_shape=outs,
        in_specs=in_specs or [smem()] + [vmem()] * (len(ins) - 1),
        out_specs=jax.tree.map(lambda _: vmem(), outs),
        scratch_shapes=list(scratch),
        compiler_params=pltpu.CompilerParams(vmem_limit_bytes=grant * 1024 * 1024),
        cost_estimate=pl.CostEstimate(flops=1_000_000, bytes_accessed=2_000_000, transcendentals=0),
    )(*ins)


def shaped(*shape):
    return jax.ShapeDtypeStruct(shape, F32)


def split3(value):
    high = value.astype(BF16)
    rest = value - high.astype(F32)
    middle = rest.astype(BF16)
    return high, middle, (rest - middle.astype(F32)).astype(BF16)


def dot_nt(left, right):
    return lax.dot_general(left, right, (((1,), (1,)), ((), ())), preferred_element_type=F32)


def prepare_kernel(span_y, tiles, ids, residuals, owners, cells, wave, older, stiff, packets,
                   even, odd):
    pack_slots(span_y, tiles, residuals, owners, cells, packets)
    pack_strips(ids, wave, older, stiff, even, odd)


def pack_slots(span_y, tiles, residuals, owner_row, cell_row, out):
    rows = residuals.shape[1]
    owner = owner_row[...]
    owner_column = jnp.transpose(jnp.broadcast_to(owner.astype(F32), (rows, rows)))
    earlier = (owner_column.astype(jnp.int32) == owner) & (
        lax.broadcasted_iota(jnp.int32, (rows, rows), 0)
        < lax.broadcasted_iota(jnp.int32, (rows, rows), 1)
    )
    rank = jnp.sum(earlier.astype(jnp.int32), axis=0, keepdims=True)
    cell = cell_row[...]
    along = cell & (LANES - 1)
    fields = [residuals[pl.ds(field, 1), :] for field in range(STEPS)] + [cell.astype(F32)]
    stacked = jnp.concatenate(
        [jnp.broadcast_to(field, (SLOTS, rows)) for field in fields]
        + [jnp.zeros((LANES - SLOTS * len(fields), rows), F32)],
        axis=0,
    )
    line = lax.broadcasted_iota(jnp.int32, (LANES, rows), 0)
    slot = line - SLOTS * (line // SLOTS)
    tile = lax.broadcasted_iota(jnp.int32, (tiles, rows), 0)
    place = tile & (span_y - 1)
    total = jnp.zeros((tiles, LANES), F32)
    for group in range(3):
        named = owner == tile + (group - 1)
        wanted = slot == rank + CAP * group
        if group == 0:
            named = named & (place != 0)
            wanted = wanted & (along >= LANES - STRIP)
        if group == 2:
            named = named & (place != span_y - 1)
            wanted = wanted & (along < STRIP)
        chosen = named.astype(F32).astype(BF16)
        for part in split3(jnp.where(wanted, stacked, 0.0)):
            total = total + dot_nt(chosen, part)
    out[...] = total


def plane_kernel(face, rows, ids, z_even, *refs):
    *packets, out, turned = refs
    out[pl.ds(0, face)] = z_even[...]
    out[pl.ds(face, 2 * STEPS)] = jnp.zeros((2 * STEPS, rows, LANES), F32)

    @pl.when(ids[0] < 2)
    def _():
        count = turned.shape[1]
        share = count // len(packets)
        for number, packet in enumerate(packets):
            turned[:, share * number : share * (number + 1)] = jnp.transpose(packet[...])
        line = lax.broadcasted_iota(jnp.int32, (rows, count), 0)
        spot = lax.broadcasted_iota(jnp.int32, (LANES, count), 0)

        def product(slot):
            cell = turned[pl.ds(SLOTS * STEPS + slot, 1), :].astype(jnp.int32)
            hit = (cell >> 7) == line
            highs, lows = [], []
            for step in range(STEPS):
                value = turned[pl.ds(SLOTS * step + slot, 1), :]
                high = value.astype(BF16).astype(F32)
                highs.append(jnp.where(hit, high, 0.0))
                lows.append(jnp.where(hit, value - high, 0.0))
            left = jnp.concatenate(highs + lows, axis=0).astype(BF16)
            right = jnp.where((cell & (LANES - 1)) == spot, 1.0, 0.0).astype(BF16)
            both = dot_nt(left, right)
            return both[: STEPS * rows] + both[STEPS * rows :]

        for part, groups in enumerate(((1,), (0, 2))):
            total = None
            for slot in [CAP * group + rank for group in groups for rank in range(CAP)]:
                total = product(slot) if total is None else total + product(slot)
            out[pl.ds(face + STEPS * part, STEPS)] = total.reshape(STEPS, rows, LANES)


def pack_strips(ids, wave, older, stiff, even, odd):
    parity = ids[2] & 1
    quarter = lane_of(wave.shape[1:]) // STRIP
    low, high = quarter == 0, quarter == 3
    quarters = LANES // STRIP
    for number, field in enumerate((wave, older, stiff)):
        for chunk in range(field.shape[0] // quarters):
            lows = highs = None
            for turn in range(quarters):
                value = field[quarters * chunk + turn]
                one = jnp.where(low, value, 0.0)
                two = jnp.where(high, value, 0.0)
                if turn:
                    one = pltpu.roll(one, STRIP * turn, 1)
                    two = pltpu.roll(two, STRIP * turn, 1)
                lows = one if lows is None else lows + one
                highs = two if highs is None else highs + two
            place = number * (field.shape[0] // quarters) + chunk
            even[place] = jnp.where(parity == 0, highs, lows)
            odd[place] = jnp.where(parity == 0, lows, highs)


def strip_width(step):
    return {0: STRIP, 1: STRIP // 2, 2: STRIP // 4}.get(step, 0)


def folds(width):
    return LANES // (2 * width) if width else 0


def folded(length, width):
    return length // folds(width) if width else 0


def kept_lanes(shape, width):
    lane = lane_of(shape)
    return (lane < width) | (lane >= LANES - width)


def fold(pieces, width):
    total = None
    for turn, piece in enumerate(pieces):
        piece = jnp.where(kept_lanes(piece.shape, width), piece, 0.0)
        if turn:
            piece = pltpu.roll(piece, 2 * width * turn, 1)
        total = piece if total is None else total + piece
    return total


def unfold(both, turn, width):
    if turn:
        both = pltpu.roll(both, LANES - 2 * width * turn, 1)
    return jnp.where(kept_lanes(both.shape, width), both, 0.0)


def write_faces(width, ids, main, side, z_even, z_odd, x_even, x_odd):
    z_parity, x_parity = ids[0] & 1, ids[1] & 1
    depth, rows, _ = main.shape
    count = folds(width)
    for face, start in (
        (z_even, (depth - RADIUS) * (1 - z_parity)),
        (z_odd, (depth - RADIUS) * z_parity),
    ):
        face[pl.ds(0, RADIUS)] = main[pl.ds(start, RADIUS)]
        span = folded(RADIUS, width)
        for plane in range(span):
            face[RADIUS + plane] = fold(
                [side[start + plane + span * turn] for turn in range(count)], width
            )
    for face, start in (
        (x_even, (rows - RADIUS) * (1 - x_parity)),
        (x_odd, (rows - RADIUS) * x_parity),
    ):
        start = pl.multiple_of(start, RADIUS)
        face[pl.ds(0, depth)] = main[:, pl.ds(start, RADIUS), :]
        span = folded(depth, width)
        for plane in range(span):
            face[depth + plane] = fold(
                [side[plane + span * turn, pl.ds(start, RADIUS), :] for turn in range(count)],
                width,
            )


def strip_unpack_kernel(
    ids, even, odd, wave, wave_side, older_side, stiff_side, z_even, z_odd, x_even, x_odd
):
    parity = ids[2] & 1
    quarters = LANES // STRIP
    quarter = lane_of(wave.shape[1:]) // STRIP
    from_even = quarter == 3 * parity
    from_odd = quarter == 3 * (1 - parity)
    chunks = wave.shape[0] // quarters
    for number, side in enumerate((wave_side, older_side, stiff_side)):
        for chunk in range(chunks):
            one, two = even[number * chunks + chunk], odd[number * chunks + chunk]
            for turn in range(quarters):
                back = (LANES - STRIP * turn) % LANES
                first = pltpu.roll(one, back, 1) if back else one
                second = pltpu.roll(two, back, 1) if back else two
                side[quarters * chunk + turn] = jnp.where(
                    from_even, first, jnp.where(from_odd, second, 0.0)
                )
    write_faces(STRIP, ids, wave, wave_side, z_even, z_odd, x_even, x_odd)


def fill(width, ids, wave, side, z_even, z_odd, x_even, x_odd, z_ext, x_ext):
    z_parity, x_parity = ids[0] & 1, ids[1] & 1
    depth, rows, _ = wave.shape
    count = folds(width)
    for part, field in enumerate((wave, side) if width else (wave,)):
        z_ext[part, pl.ds(RADIUS, depth)] = field[...]
        x_ext[part, :, pl.ds(RADIUS, rows), :] = field[...]
    pair = z_even.at[1 - z_parity]
    for face, start in (
        (pair, (depth + RADIUS) * (1 - z_parity)),
        (z_odd, (depth + RADIUS) * z_parity),
    ):
        z_ext[0, pl.ds(start, RADIUS)] = face[pl.ds(0, RADIUS)]
        span = folded(RADIUS, width)
        for plane in range(span):
            both = face[RADIUS + plane]
            for turn in range(count):
                z_ext[1, start + plane + span * turn] = unfold(both, turn, width)
    for face, start in (
        (x_even, (rows + RADIUS) * (1 - x_parity)),
        (x_odd, (rows + RADIUS) * x_parity),
    ):
        start = pl.multiple_of(start, RADIUS)
        x_ext[0, :, pl.ds(start, RADIUS), :] = face[pl.ds(0, depth)]
        span = folded(depth, width)
        for plane in range(span):
            both = face[depth + plane]
            for turn in range(count):
                x_ext[1, plane + span * turn, pl.ds(start, RADIUS), :] = unfold(both, turn, width)


def advance(step, ids, wave, side, older, older_side, stiff, stiff_side, forward, image_in,
            planes, band_high, band_low, fresh, fresh_side, image, z_ext, x_ext, y_terms):
    depth, rows, _ = wave.shape
    last = step == STEPS - 1
    width = LANES if last else 2 * LANES
    both = jnp.concatenate(
        [wave[...].reshape(depth * rows, LANES), side[...].reshape(depth * rows, LANES)], axis=1
    )
    high = both.astype(BF16)
    low = (both - high.astype(F32)).astype(BF16)
    matrix, rest = band_high[:, :width], band_low[:, :width]
    y_terms[:, :width] = (
        jnp.dot(high, matrix, preferred_element_type=F32)
        + jnp.dot(low, matrix, preferred_element_type=F32)
        + jnp.dot(high, rest, preferred_element_type=F32)
    )

    def one(z, part, field, before, speed, target):
        column = x_ext[part, z]
        turned = [None] + [
            pltpu.roll(column, rows + 2 * RADIUS - offset, 0) for offset in range(1, RADIUS)
        ]
        total = y_terms[z * rows : (z + 1) * rows, part * LANES : (part + 1) * LANES]
        for offset in range(1, RADIUS + 1):
            near = z_ext[part, RADIUS + z + offset] + z_ext[part, RADIUS + z - offset]
            if offset < RADIUS:
                near = near + turned[offset][RADIUS : RADIUS + rows]
                near = near + turned[RADIUS - offset][:rows]
            else:
                near = near + column[2 * RADIUS :] + column[:rows]
            total = total + WEIGHTS[offset - 1] * near
        if z == 0:
            total = total + planes[STEPS * part + step]
        value = 2.0 * field[z] - before[z] + speed[z] * total
        target[z] = value
        return value

    for z in range(depth):
        value = one(z, 0, wave, older, stiff, fresh)
        product = forward[step, z].astype(F32) * value
        if step:
            product = product + image_in[z]
        if last:
            product = product * muting(ids, z, depth, rows)
        image[z] = product
        if not last:
            one(z, 1, side, older_side, stiff_side, fresh_side)


def muting(ids, z, depth, rows):
    gap_z = (ids[0] * depth + z).astype(F32)
    gap_x = (
        ids[1] * rows + lax.broadcasted_iota(jnp.int32, (rows, LANES), 0) - ids[3]
    ).astype(F32)
    gap_y = (ids[2] * LANES + lane_of((rows, LANES)) - ids[4]).astype(F32)
    distance = gap_z * gap_z + gap_x * gap_x + gap_y * gap_y
    return jnp.minimum(1.0, distance / 576.0)


def step_kernel(step, ids, x_odd_in, x_even_in, z_odd_in, z_even_in, wave, side, older,
                older_side, stiff, stiff_side, forward, band_high, band_low, *rest):
    image_in = None
    if step:
        planes, image_in, *rest = rest
    else:
        planes, *rest = rest
        face = z_even_in.shape[1] - 2 * STEPS
        both = z_even_in[0, pl.ds(face, 2 * STEPS)] + z_even_in[1, pl.ds(face, 2 * STEPS)]
        planes[...] = jnp.where(ids[0] == 0, both, 0.0)
    last = step == STEPS - 1
    if last:
        image, fresh, z_ext, x_ext, y_terms = rest
        fresh_side = None
    else:
        (image, fresh, fresh_side, z_even, z_odd, x_even, x_odd, z_ext, x_ext, y_terms) = rest
    fill(strip_width(step), ids, wave, side, z_even_in, z_odd_in, x_even_in, x_odd_in, z_ext, x_ext)
    advance(step, ids, wave, side, older, older_side, stiff, stiff_side, forward, image_in,
            planes, band_high, band_low, fresh, fresh_side, image, z_ext, x_ext, y_terms)
    if not last:
        write_faces(strip_width(step + 1), ids, fresh, fresh_side, z_even, z_odd, x_even, x_odd)


def swap(block, axis, parity):
    count = lax.axis_size(axis)
    pairs = []
    for left in range(parity, count - 1, 2):
        pairs += [(left, left + 1), (left + 1, left)]
    return lax.ppermute(block, axis, pairs)


def pair_gather(block, axis, parity):
    count = lax.axis_size(axis)
    groups = [
        [(2 * pair + parity) % count, (2 * pair + parity + 1) % count]
        for pair in range(count // 2)
    ]
    return lax.all_gather(block, axis, axis=0, tiled=False, axis_index_groups=groups)


def exchange(faces):
    z_even, z_odd, x_even, x_odd = faces
    z_odd = swap(z_odd, "gz", 1)
    x_even = swap(x_even, "gx", 0)
    x_odd = swap(x_odd, "gx", 1)
    z_even = pair_gather(z_even, "gz", 0)
    return z_even, z_odd, x_even, x_odd


def on_device(
    stiffness, older_wave, wave_now, forward_wave, residuals, owners, receivers, source_cell
):
    depth, rows, cols = wave_now.shape
    span_x, span_y, span_z = (lax.axis_size(axis) for axis in ("gx", "gy", "gz"))
    tiles = span_x * span_y
    total_y = cols * span_y
    ids = jnp.stack(
        [
            lax.axis_index("gz"),
            lax.axis_index("gx"),
            lax.axis_index("gy"),
            source_cell[0] // total_y,
            source_cell[0] % total_y,
        ]
    ).astype(jnp.int32)
    band_high, band_low = (jnp.asarray(part) for part in band())
    block = shaped(depth, rows, LANES)

    def faces_out(step):
        width = strip_width(step)
        z_face = shaped(RADIUS + folded(RADIUS, width), rows, LANES)
        x_face = shaped(depth + folded(depth, width), RADIUS, LANES)
        return [z_face, z_face, x_face, x_face]

    strips = shaped(3 * depth * STRIP // LANES, rows, LANES)
    packets, even, odd = call(
        functools.partial(prepare_kernel, span_y, tiles),
        [shaped(tiles, LANES), strips, strips],
        [ids, residuals, owners.reshape(1, -1), receivers.reshape(1, -1), wave_now, older_wave,
         stiffness],
        in_specs=[smem()] + [pl.BlockSpec()] * 6,
        grant=60,
    )
    packets = lax.all_to_all(packets, ("gx", "gy"), 0, 0, tiled=True)
    even, odd = (swap(strip, "gy", parity) for parity, strip in enumerate((even, odd)))
    side, older_side, stiff_side, *faces = call(
        strip_unpack_kernel,
        [block] * 3 + faces_out(0),
        [ids, even, odd, wave_now],
    )
    cores = 2
    packets = [packets] + [
        lax.ppermute(packets, "gz", [(chip + core, core) for core in range(cores)])
        for chip in range(cores, span_z, cores)
    ]
    face = faces[0].shape[0]
    faces[0] = call(
        functools.partial(plane_kernel, face, rows),
        shaped(face + 2 * STEPS, rows, LANES),
        [ids, faces[0], *packets],
        scratch=[pltpu.VMEM((LANES, span_z // cores * tiles), F32)],
    )

    scratch = [
        pltpu.VMEM((2, depth + 2 * RADIUS, rows, LANES), F32),
        pltpu.VMEM((2, depth, rows + 2 * RADIUS, LANES), F32),
        pltpu.VMEM((depth * rows, 2 * LANES), F32),
    ]
    wave, older = wave_now, older_wave
    image = None
    for step in range(STEPS):
        faces = exchange(faces)
        ins = [ids, *faces[::-1], wave, side, older, older_side, stiffness, stiff_side, forward_wave,
               band_high, band_low]
        outs = [block, block]
        if step:
            ins += [planes, image]
        else:
            outs = [shaped(2 * STEPS, rows, LANES)] + outs
        if step < STEPS - 1:
            outs += [block] + faces_out(step + 1)
        rest = call(functools.partial(step_kernel, step), outs, ins, scratch)
        if not step:
            planes, *rest = rest
        image, fresh, *rest = rest
        older, wave = wave, fresh
        if step < STEPS - 1:
            older_side, side = side, rest[0]
            faces = rest[1:]
    return image, older, wave


def solution(mesh):
    in_specs = (
        P("gz", "gx", "gy"),
        P("gz", "gx", "gy"),
        P("gz", "gx", "gy"),
        P(None, "gz", "gx", "gy"),
        P(None, ("gx", "gy", "gz")),
        P(("gx", "gy", "gz"), None),
        P(("gx", "gy", "gz")),
        P(),
    )
    out_specs = (P("gz", "gx", "gy"), P("gz", "gx", "gy"), P("gz", "gx", "gy"))
    return jax.shard_map(
        on_device, mesh=mesh, in_specs=in_specs, out_specs=out_specs, check_vma=False
    )
```

```python
import functools
import math

import jax
import jax.numpy as jnp
import numpy as np
from jax import lax
from jax.experimental import pallas as pl
from jax.experimental.pallas import tpu as pltpu
from jax.sharding import PartitionSpec as P

STEPS = 4
RADIUS = 8
LANES = 128
STRIP = 32
CAP = 8
SLOTS = 3 * CAP
F32 = jnp.float32
BF16 = jnp.bfloat16


def stencil_weights():
    window = [math.cos(math.pi * offset / 20.0) for offset in range(1, RADIUS + 1)]
    alternating = sum(
        ((-1.0) ** (offset + 1) * window[offset - 1] for offset in range(1, RADIUS + 1))
    )
    factor = 1.0 / (2.0 * alternating)
    weights = []
    for offset in range(1, RADIUS + 1):
        weights.append(
            factor * 2.0 * (-1.0) ** (offset + 1) * window[offset - 1] / (offset * offset)
        )
    return (weights, -2.0 * sum(weights))


WEIGHTS, CENTER = stencil_weights()


def band():
    size = 2 * LANES
    matrix = np.zeros((size, size), np.float64)
    for column in range(size):
        matrix[column, column] = 3.0 * CENTER
        for offset in range(1, RADIUS + 1):
            matrix[(column + offset) % size, column] = WEIGHTS[offset - 1]
            matrix[(column - offset) % size, column] = WEIGHTS[offset - 1]
    matrix = matrix.astype(np.float32)
    high = matrix.astype(jnp.bfloat16)
    low = (matrix - high.astype(np.float32)).astype(jnp.bfloat16)
    return high, low


def lane_of(shape):
    return lax.broadcasted_iota(jnp.int32, shape, len(shape) - 1)


def vmem():
    return pl.BlockSpec(memory_space=pltpu.VMEM)


def smem():
    return pl.BlockSpec(memory_space=pltpu.SMEM)


def call(body, outs, ins, scratch=(), in_specs=None, grant=32):
    return pl.pallas_call(
        body,
        out_shape=outs,
        in_specs=in_specs or [smem()] + [vmem()] * (len(ins) - 1),
        out_specs=jax.tree.map(lambda _: vmem(), outs),
        scratch_shapes=list(scratch),
        compiler_params=pltpu.CompilerParams(vmem_limit_bytes=grant * 1024 * 1024),
        cost_estimate=pl.CostEstimate(flops=1_000_000, bytes_accessed=2_000_000, transcendentals=0),
    )(*ins)


def shaped(*shape):
    return jax.ShapeDtypeStruct(shape, F32)


def split3(value):
    high = value.astype(BF16)
    rest = value - high.astype(F32)
    middle = rest.astype(BF16)
    return high, middle, (rest - middle.astype(F32)).astype(BF16)


def dot_nt(left, right):
    return lax.dot_general(left, right, (((1,), (1,)), ((), ())), preferred_element_type=F32)


def prepare_kernel(span_y, tiles, ids, residuals, owners, cells, wave, older, stiff, packets,
                   even, odd):
    pack_slots(span_y, tiles, residuals, owners, cells, packets)
    pack_strips(ids, wave, older, stiff, even, odd)


def pack_slots(span_y, tiles, residuals, owner_row, cell_row, out):
    rows = residuals.shape[1]
    owner = owner_row[...]
    owner_column = jnp.transpose(jnp.broadcast_to(owner.astype(F32), (rows, rows)))
    earlier = (owner_column.astype(jnp.int32) == owner) & (
        lax.broadcasted_iota(jnp.int32, (rows, rows), 0)
        < lax.broadcasted_iota(jnp.int32, (rows, rows), 1)
    )
    rank = jnp.sum(earlier.astype(jnp.int32), axis=0, keepdims=True)
    cell = cell_row[...]
    along = cell & (LANES - 1)
    fields = [residuals[pl.ds(field, 1), :] for field in range(STEPS)] + [cell.astype(F32)]
    stacked = jnp.concatenate(
        [jnp.broadcast_to(field, (SLOTS, rows)) for field in fields]
        + [jnp.zeros((LANES - SLOTS * len(fields), rows), F32)],
        axis=0,
    )
    line = lax.broadcasted_iota(jnp.int32, (LANES, rows), 0)
    slot = line - SLOTS * (line // SLOTS)
    tile = lax.broadcasted_iota(jnp.int32, (tiles, rows), 0)
    place = tile & (span_y - 1)
    total = jnp.zeros((tiles, LANES), F32)
    for group in range(3):
        named = owner == tile + (group - 1)
        wanted = slot == rank + CAP * group
        if group == 0:
            named = named & (place != 0)
            wanted = wanted & (along >= LANES - STRIP)
        if group == 2:
            named = named & (place != span_y - 1)
            wanted = wanted & (along < STRIP)
        chosen = named.astype(F32).astype(BF16)
        for part in split3(jnp.where(wanted, stacked, 0.0)):
            total = total + dot_nt(chosen, part)
    out[...] = total


def plane_kernel(face, rows, ids, z_even, *refs):
    *packets, out, turned = refs
    out[pl.ds(0, face)] = z_even[...]
    out[pl.ds(face, 2 * STEPS)] = jnp.zeros((2 * STEPS, rows, LANES), F32)

    @pl.when(ids[0] < 2)
    def _():
        count = turned.shape[1]
        share = count // len(packets)
        for number, packet in enumerate(packets):
            turned[:, share * number : share * (number + 1)] = jnp.transpose(packet[...])
        line = lax.broadcasted_iota(jnp.int32, (rows, count), 0)
        spot = lax.broadcasted_iota(jnp.int32, (LANES, count), 0)

        def product(slot):
            cell = turned[pl.ds(SLOTS * STEPS + slot, 1), :].astype(jnp.int32)
            hit = (cell >> 7) == line
            highs, lows = [], []
            for step in range(STEPS):
                value = turned[pl.ds(SLOTS * step + slot, 1), :]
                high = value.astype(BF16).astype(F32)
                highs.append(jnp.where(hit, high, 0.0))
                lows.append(jnp.where(hit, value - high, 0.0))
            left = jnp.concatenate(highs + lows, axis=0).astype(BF16)
            right = jnp.where((cell & (LANES - 1)) == spot, 1.0, 0.0).astype(BF16)
            both = dot_nt(left, right)
            return both[: STEPS * rows] + both[STEPS * rows :]

        for part, groups in enumerate(((1,), (0, 2))):
            total = None
            for slot in [CAP * group + rank for group in groups for rank in range(CAP)]:
                total = product(slot) if total is None else total + product(slot)
            out[pl.ds(face + STEPS * part, STEPS)] = total.reshape(STEPS, rows, LANES)


def pack_strips(ids, wave, older, stiff, even, odd):
    parity = ids[2] & 1
    quarter = lane_of(wave.shape[1:]) // STRIP
    low, high = quarter == 0, quarter == 3
    quarters = LANES // STRIP
    for number, field in enumerate((wave, older, stiff)):
        for chunk in range(field.shape[0] // quarters):
            lows = highs = None
            for turn in range(quarters):
                value = field[quarters * chunk + turn]
                one = jnp.where(low, value, 0.0)
                two = jnp.where(high, value, 0.0)
                if turn:
                    one = pltpu.roll(one, STRIP * turn, 1)
                    two = pltpu.roll(two, STRIP * turn, 1)
                lows = one if lows is None else lows + one
                highs = two if highs is None else highs + two
            place = number * (field.shape[0] // quarters) + chunk
            even[place] = jnp.where(parity == 0, highs, lows)
            odd[place] = jnp.where(parity == 0, lows, highs)


def strip_width(step):
    return {0: STRIP, 1: STRIP // 2, 2: STRIP // 4}.get(step, 0)


def folds(width):
    return LANES // (2 * width) if width else 0


def folded(length, width):
    return length // folds(width) if width else 0


def kept_lanes(shape, width):
    lane = lane_of(shape)
    return (lane < width) | (lane >= LANES - width)


def fold(pieces, width):
    total = None
    for turn, piece in enumerate(pieces):
        piece = jnp.where(kept_lanes(piece.shape, width), piece, 0.0)
        if turn:
            piece = pltpu.roll(piece, 2 * width * turn, 1)
        total = piece if total is None else total + piece
    return total


def unfold(both, turn, width):
    if turn:
        both = pltpu.roll(both, LANES - 2 * width * turn, 1)
    return jnp.where(kept_lanes(both.shape, width), both, 0.0)


def write_faces(width, ids, main, side, z_even, z_odd, x_even, x_odd):
    z_parity, x_parity = ids[0] & 1, ids[1] & 1
    depth, rows, _ = main.shape
    count = folds(width)
    for face, start in (
        (z_even, (depth - RADIUS) * (1 - z_parity)),
        (z_odd, (depth - RADIUS) * z_parity),
    ):
        face[pl.ds(0, RADIUS)] = main[pl.ds(start, RADIUS)]
        span = folded(RADIUS, width)
        for plane in range(span):
            face[RADIUS + plane] = fold(
                [side[start + plane + span * turn] for turn in range(count)], width
            )
    for face, start in (
        (x_even, (rows - RADIUS) * (1 - x_parity)),
        (x_odd, (rows - RADIUS) * x_parity),
    ):
        start = pl.multiple_of(start, RADIUS)
        face[pl.ds(0, depth)] = main[:, pl.ds(start, RADIUS), :]
        span = folded(depth, width)
        for plane in range(span):
            face[depth + plane] = fold(
                [side[plane + span * turn, pl.ds(start, RADIUS), :] for turn in range(count)],
                width,
            )


def strip_unpack_kernel(
    ids, even, odd, wave, wave_side, older_side, stiff_side, z_even, z_odd, x_even, x_odd
):
    parity = ids[2] & 1
    quarters = LANES // STRIP
    quarter = lane_of(wave.shape[1:]) // STRIP
    from_even = quarter == 3 * parity
    from_odd = quarter == 3 * (1 - parity)
    chunks = wave.shape[0] // quarters
    for number, side in enumerate((wave_side, older_side, stiff_side)):
        for chunk in range(chunks):
            one, two = even[number * chunks + chunk], odd[number * chunks + chunk]
            for turn in range(quarters):
                back = (LANES - STRIP * turn) % LANES
                first = pltpu.roll(one, back, 1) if back else one
                second = pltpu.roll(two, back, 1) if back else two
                side[quarters * chunk + turn] = jnp.where(
                    from_even, first, jnp.where(from_odd, second, 0.0)
                )
    write_faces(STRIP, ids, wave, wave_side, z_even, z_odd, x_even, x_odd)


def fill(width, ids, wave, side, z_even, z_odd, x_even, x_odd, z_ext, x_ext):
    z_parity, x_parity = ids[0] & 1, ids[1] & 1
    depth, rows, _ = wave.shape
    count = folds(width)
    for part, field in enumerate((wave, side) if width else (wave,)):
        z_ext[part, pl.ds(RADIUS, depth)] = field[...]
        x_ext[part, :, pl.ds(RADIUS, rows), :] = field[...]
    pair = z_even.at[1 - z_parity]
    for face, start in (
        (pair, (depth + RADIUS) * (1 - z_parity)),
        (z_odd, (depth + RADIUS) * z_parity),
    ):
        z_ext[0, pl.ds(start, RADIUS)] = face[pl.ds(0, RADIUS)]
        span = folded(RADIUS, width)
        for plane in range(span):
            both = face[RADIUS + plane]
            for turn in range(count):
                z_ext[1, start + plane + span * turn] = unfold(both, turn, width)
    for face, start in (
        (x_even, (rows + RADIUS) * (1 - x_parity)),
        (x_odd, (rows + RADIUS) * x_parity),
    ):
        start = pl.multiple_of(start, RADIUS)
        x_ext[0, :, pl.ds(start, RADIUS), :] = face[pl.ds(0, depth)]
        span = folded(depth, width)
        for plane in range(span):
            both = face[depth + plane]
            for turn in range(count):
                x_ext[1, plane + span * turn, pl.ds(start, RADIUS), :] = unfold(both, turn, width)


def advance(step, ids, wave, side, older, older_side, stiff, stiff_side, forward, image_in,
            planes, band_high, band_low, fresh, fresh_side, image, z_ext, x_ext, y_terms):
    depth, rows, _ = wave.shape
    last = step == STEPS - 1
    width = LANES if last else 2 * LANES
    both = jnp.concatenate(
        [wave[...].reshape(depth * rows, LANES), side[...].reshape(depth * rows, LANES)], axis=1
    )
    high = both.astype(BF16)
    low = (both - high.astype(F32)).astype(BF16)
    matrix, rest = band_high[:, :width], band_low[:, :width]
    y_terms[:, :width] = (
        jnp.dot(high, matrix, preferred_element_type=F32)
        + jnp.dot(low, matrix, preferred_element_type=F32)
        + jnp.dot(high, rest, preferred_element_type=F32)
    )

    def one(z, part, field, before, speed, target):
        column = x_ext[part, z]
        turned = [None] + [
            pltpu.roll(column, rows + 2 * RADIUS - offset, 0) for offset in range(1, RADIUS)
        ]
        total = y_terms[z * rows : (z + 1) * rows, part * LANES : (part + 1) * LANES]
        for offset in range(1, RADIUS + 1):
            near = z_ext[part, RADIUS + z + offset] + z_ext[part, RADIUS + z - offset]
            if offset < RADIUS:
                near = near + turned[offset][RADIUS : RADIUS + rows]
                near = near + turned[RADIUS - offset][:rows]
            else:
                near = near + column[2 * RADIUS :] + column[:rows]
            total = total + WEIGHTS[offset - 1] * near
        if z == 0:
            total = total + planes[STEPS * part + step]
        value = 2.0 * field[z] - before[z] + speed[z] * total
        target[z] = value
        return value

    for z in range(depth):
        value = one(z, 0, wave, older, stiff, fresh)
        product = forward[step, z].astype(F32) * value
        if step:
            product = product + image_in[z]
        if last:
            product = product * muting(ids, z, depth, rows)
        image[z] = product
        if not last:
            one(z, 1, side, older_side, stiff_side, fresh_side)


def muting(ids, z, depth, rows):
    gap_z = (ids[0] * depth + z).astype(F32)
    gap_x = (
        ids[1] * rows + lax.broadcasted_iota(jnp.int32, (rows, LANES), 0) - ids[3]
    ).astype(F32)
    gap_y = (ids[2] * LANES + lane_of((rows, LANES)) - ids[4]).astype(F32)
    distance = gap_z * gap_z + gap_x * gap_x + gap_y * gap_y
    return jnp.minimum(1.0, distance / 576.0)


def step_kernel(step, ids, x_odd_in, x_even_in, z_odd_in, z_even_in, wave, side, older,
                older_side, stiff, stiff_side, forward, band_high, band_low, *rest):
    image_in = None
    if step:
        planes, image_in, *rest = rest
    else:
        planes, *rest = rest
        face = z_even_in.shape[1] - 2 * STEPS
        both = z_even_in[0, pl.ds(face, 2 * STEPS)] + z_even_in[1, pl.ds(face, 2 * STEPS)]
        planes[...] = jnp.where(ids[0] == 0, both, 0.0)
    last = step == STEPS - 1
    if last:
        image, fresh, z_ext, x_ext, y_terms = rest
        fresh_side = None
    else:
        (image, fresh, fresh_side, z_even, z_odd, x_even, x_odd, z_ext, x_ext, y_terms) = rest
    fill(strip_width(step), ids, wave, side, z_even_in, z_odd_in, x_even_in, x_odd_in, z_ext, x_ext)
    advance(step, ids, wave, side, older, older_side, stiff, stiff_side, forward, image_in,
            planes, band_high, band_low, fresh, fresh_side, image, z_ext, x_ext, y_terms)
    if not last:
        write_faces(strip_width(step + 1), ids, fresh, fresh_side, z_even, z_odd, x_even, x_odd)


def swap(block, axis, parity):
    count = lax.axis_size(axis)
    pairs = []
    for left in range(parity, count - 1, 2):
        pairs += [(left, left + 1), (left + 1, left)]
    return lax.ppermute(block, axis, pairs)


def pair_gather(block, axis, parity):
    count = lax.axis_size(axis)
    groups = [
        [(2 * pair + parity) % count, (2 * pair + parity + 1) % count]
        for pair in range(count // 2)
    ]
    return lax.all_gather(block, axis, axis=0, tiled=False, axis_index_groups=groups)


def exchange(faces):
    z_even, z_odd, x_even, x_odd = faces
    z_odd = swap(z_odd, "gz", 1)
    x_even = swap(x_even, "gx", 0)
    x_odd = swap(x_odd, "gx", 1)
    z_even = pair_gather(z_even, "gz", 0)
    return z_even, z_odd, x_even, x_odd


def on_device(
    stiffness, older_wave, wave_now, forward_wave, residuals, owners, receivers, source_cell
):
    depth, rows, cols = wave_now.shape
    span_x, span_y, span_z = (lax.axis_size(axis) for axis in ("gx", "gy", "gz"))
    tiles = span_x * span_y
    total_y = cols * span_y
    ids = jnp.stack(
        [
            lax.axis_index("gz"),
            lax.axis_index("gx"),
            lax.axis_index("gy"),
            source_cell[0] // total_y,
            source_cell[0] % total_y,
        ]
    ).astype(jnp.int32)
    band_high, band_low = (jnp.asarray(part) for part in band())
    block = shaped(depth, rows, LANES)

    def faces_out(step):
        width = strip_width(step)
        z_face = shaped(RADIUS + folded(RADIUS, width), rows, LANES)
        x_face = shaped(depth + folded(depth, width), RADIUS, LANES)
        return [z_face, z_face, x_face, x_face]

    strips = shaped(3 * depth * STRIP // LANES, rows, LANES)
    packets, even, odd = call(
        functools.partial(prepare_kernel, span_y, tiles),
        [shaped(tiles, LANES), strips, strips],
        [ids, residuals, owners.reshape(1, -1), receivers.reshape(1, -1), wave_now, older_wave,
         stiffness],
        in_specs=[smem()] + [pl.BlockSpec()] * 6,
        grant=60,
    )
    packets = lax.all_to_all(packets, ("gx", "gy"), 0, 0, tiled=True)
    packets, even, odd = lax.optimization_barrier((packets, even, odd))
    even, odd = (swap(strip, "gy", parity) for parity, strip in enumerate((even, odd)))
    side, older_side, stiff_side, *faces = call(
        strip_unpack_kernel,
        [block] * 3 + faces_out(0),
        [ids, even, odd, wave_now],
    )
    cores = 2
    packets = [packets] + [
        lax.ppermute(packets, "gz", [(chip + core, core) for core in range(cores)])
        for chip in range(cores, span_z, cores)
    ]
    face = faces[0].shape[0]
    faces[0] = call(
        functools.partial(plane_kernel, face, rows),
        shaped(face + 2 * STEPS, rows, LANES),
        [ids, faces[0], *packets],
        scratch=[pltpu.VMEM((LANES, span_z // cores * tiles), F32)],
    )

    scratch = [
        pltpu.VMEM((2, depth + 2 * RADIUS, rows, LANES), F32),
        pltpu.VMEM((2, depth, rows + 2 * RADIUS, LANES), F32),
        pltpu.VMEM((depth * rows, 2 * LANES), F32),
    ]
    wave, older = wave_now, older_wave
    image = None
    for step in range(STEPS):
        faces = exchange(faces)
        ins = [ids, *faces[::-1], wave, side, older, older_side, stiffness, stiff_side, forward_wave,
               band_high, band_low]
        outs = [block, block]
        if step:
            ins += [planes, image]
        else:
            outs = [shaped(2 * STEPS, rows, LANES)] + outs
        if step < STEPS - 1:
            outs += [block] + faces_out(step + 1)
        rest = call(functools.partial(step_kernel, step), outs, ins, scratch)
        if not step:
            planes, *rest = rest
        image, fresh, *rest = rest
        older, wave = wave, fresh
        if step < STEPS - 1:
            older_side, side = side, rest[0]
            faces = rest[1:]
    return image, older, wave


def solution(mesh):
    in_specs = (
        P("gz", "gx", "gy"),
        P("gz", "gx", "gy"),
        P("gz", "gx", "gy"),
        P(None, "gz", "gx", "gy"),
        P(None, ("gx", "gy", "gz")),
        P(("gx", "gy", "gz"), None),
        P(("gx", "gy", "gz")),
        P(),
    )
    out_specs = (P("gz", "gx", "gy"), P("gz", "gx", "gy"), P("gz", "gx", "gy"))
    return jax.shard_map(
        on_device, mesh=mesh, in_specs=in_specs, out_specs=out_specs, check_vma=False
    )
```

```python
import functools
import math

import jax
import jax.numpy as jnp
import numpy as np
from jax import lax
from jax.experimental import pallas as pl
from jax.experimental.pallas import tpu as pltpu
from jax.sharding import PartitionSpec as P

STEPS = 4
RADIUS = 8
LANES = 128
STRIP = 32
CAP = 8
SLOTS = 3 * CAP
F32 = jnp.float32
BF16 = jnp.bfloat16


def stencil_weights():
    window = [math.cos(math.pi * offset / 20.0) for offset in range(1, RADIUS + 1)]
    alternating = sum(
        ((-1.0) ** (offset + 1) * window[offset - 1] for offset in range(1, RADIUS + 1))
    )
    factor = 1.0 / (2.0 * alternating)
    weights = []
    for offset in range(1, RADIUS + 1):
        weights.append(
            factor * 2.0 * (-1.0) ** (offset + 1) * window[offset - 1] / (offset * offset)
        )
    return (weights, -2.0 * sum(weights))


WEIGHTS, CENTER = stencil_weights()


def band():
    size = 2 * LANES
    matrix = np.zeros((size, size), np.float64)
    for column in range(size):
        matrix[column, column] = 3.0 * CENTER
        for offset in range(1, RADIUS + 1):
            matrix[(column + offset) % size, column] = WEIGHTS[offset - 1]
            matrix[(column - offset) % size, column] = WEIGHTS[offset - 1]
    matrix = matrix.astype(np.float32)
    high = matrix.astype(jnp.bfloat16)
    low = (matrix - high.astype(np.float32)).astype(jnp.bfloat16)
    return high, low


def lane_of(shape):
    return lax.broadcasted_iota(jnp.int32, shape, len(shape) - 1)


def vmem():
    return pl.BlockSpec(memory_space=pltpu.VMEM)


def smem():
    return pl.BlockSpec(memory_space=pltpu.SMEM)


def call(body, outs, ins, scratch=(), in_specs=None, grant=32):
    return pl.pallas_call(
        body,
        out_shape=outs,
        in_specs=in_specs or [smem()] + [vmem()] * (len(ins) - 1),
        out_specs=jax.tree.map(lambda _: vmem(), outs),
        scratch_shapes=list(scratch),
        compiler_params=pltpu.CompilerParams(vmem_limit_bytes=grant * 1024 * 1024),
        cost_estimate=pl.CostEstimate(flops=1_000_000, bytes_accessed=2_000_000, transcendentals=0),
    )(*ins)


def shaped(*shape):
    return jax.ShapeDtypeStruct(shape, F32)


def split3(value):
    high = value.astype(BF16)
    rest = value - high.astype(F32)
    middle = rest.astype(BF16)
    return high, middle, (rest - middle.astype(F32)).astype(BF16)


def dot_nt(left, right):
    return lax.dot_general(left, right, (((1,), (1,)), ((), ())), preferred_element_type=F32)


def prepare_kernel(span_y, tiles, ids, residuals, owners, cells, wave, older, stiff, packets,
                   even, odd):
    pack_slots(span_y, tiles, residuals, owners, cells, packets)
    pack_strips(ids, wave, older, stiff, even, odd)


def pack_slots(span_y, tiles, residuals, owner_row, cell_row, out):
    rows = residuals.shape[1]
    owner = owner_row[...]
    owner_column = jnp.transpose(jnp.broadcast_to(owner.astype(F32), (rows, rows)))
    earlier = (owner_column.astype(jnp.int32) == owner) & (
        lax.broadcasted_iota(jnp.int32, (rows, rows), 0)
        < lax.broadcasted_iota(jnp.int32, (rows, rows), 1)
    )
    rank = jnp.sum(earlier.astype(jnp.int32), axis=0, keepdims=True)
    cell = cell_row[...]
    along = cell & (LANES - 1)
    fields = [residuals[pl.ds(field, 1), :] for field in range(STEPS)] + [cell.astype(F32)]
    stacked = jnp.concatenate(
        [jnp.broadcast_to(field, (SLOTS, rows)) for field in fields]
        + [jnp.zeros((LANES - SLOTS * len(fields), rows), F32)],
        axis=0,
    )
    line = lax.broadcasted_iota(jnp.int32, (LANES, rows), 0)
    slot = line - SLOTS * (line // SLOTS)
    tile = lax.broadcasted_iota(jnp.int32, (tiles, rows), 0)
    place = tile & (span_y - 1)
    total = jnp.zeros((tiles, LANES), F32)
    for group in range(3):
        named = owner == tile + (group - 1)
        wanted = slot == rank + CAP * group
        if group == 0:
            named = named & (place != 0)
            wanted = wanted & (along >= LANES - STRIP)
        if group == 2:
            named = named & (place != span_y - 1)
            wanted = wanted & (along < STRIP)
        chosen = named.astype(F32).astype(BF16)
        for part in split3(jnp.where(wanted, stacked, 0.0)):
            total = total + dot_nt(chosen, part)
    out[...] = total


def plane_kernel(face, rows, ids, z_even, *refs):
    *packets, out, turned = refs
    out[pl.ds(0, face)] = z_even[...]
    out[pl.ds(face, 2 * STEPS)] = jnp.zeros((2 * STEPS, rows, LANES), F32)

    @pl.when(ids[0] < 2)
    def _():
        count = turned.shape[1]
        share = count // len(packets)
        for number, packet in enumerate(packets):
            turned[:, share * number : share * (number + 1)] = jnp.transpose(packet[...])
        line = lax.broadcasted_iota(jnp.int32, (rows, count), 0)
        spot = lax.broadcasted_iota(jnp.int32, (LANES, count), 0)

        def product(slot):
            cell = turned[pl.ds(SLOTS * STEPS + slot, 1), :].astype(jnp.int32)
            hit = (cell >> 7) == line
            highs, lows = [], []
            for step in range(STEPS):
                value = turned[pl.ds(SLOTS * step + slot, 1), :]
                high = value.astype(BF16).astype(F32)
                highs.append(jnp.where(hit, high, 0.0))
                lows.append(jnp.where(hit, value - high, 0.0))
            left = jnp.concatenate(highs + lows, axis=0).astype(BF16)
            right = jnp.where((cell & (LANES - 1)) == spot, 1.0, 0.0).astype(BF16)
            both = dot_nt(left, right)
            return both[: STEPS * rows] + both[STEPS * rows :]

        for part, groups in enumerate(((1,), (0, 2))):
            total = None
            for slot in [CAP * group + rank for group in groups for rank in range(CAP)]:
                total = product(slot) if total is None else total + product(slot)
            out[pl.ds(face + STEPS * part, STEPS)] = total.reshape(STEPS, rows, LANES)


def pack_strips(ids, wave, older, stiff, even, odd):
    parity = ids[2] & 1
    quarter = lane_of(wave.shape[1:]) // STRIP
    low, high = quarter == 0, quarter == 3
    quarters = LANES // STRIP
    for number, field in enumerate((wave, older, stiff)):
        for chunk in range(field.shape[0] // quarters):
            lows = highs = None
            for turn in range(quarters):
                value = field[quarters * chunk + turn]
                one = jnp.where(low, value, 0.0)
                two = jnp.where(high, value, 0.0)
                if turn:
                    one = pltpu.roll(one, STRIP * turn, 1)
                    two = pltpu.roll(two, STRIP * turn, 1)
                lows = one if lows is None else lows + one
                highs = two if highs is None else highs + two
            place = number * (field.shape[0] // quarters) + chunk
            even[place] = jnp.where(parity == 0, highs, lows)
            odd[place] = jnp.where(parity == 0, lows, highs)


def strip_width(step):
    return {0: STRIP, 1: STRIP // 2, 2: STRIP // 4}.get(step, 0)


def folds(width):
    return LANES // (2 * width) if width else 0


def folded(length, width):
    return length // folds(width) if width else 0


def kept_lanes(shape, width):
    lane = lane_of(shape)
    return (lane < width) | (lane >= LANES - width)


def fold(pieces, width):
    total = None
    for turn, piece in enumerate(pieces):
        piece = jnp.where(kept_lanes(piece.shape, width), piece, 0.0)
        if turn:
            piece = pltpu.roll(piece, 2 * width * turn, 1)
        total = piece if total is None else total + piece
    return total


def unfold(both, turn, width):
    if turn:
        both = pltpu.roll(both, LANES - 2 * width * turn, 1)
    return jnp.where(kept_lanes(both.shape, width), both, 0.0)


def write_faces(width, ids, main, side, z_even, z_odd, x_even, x_odd):
    z_parity, x_parity = ids[0] & 1, ids[1] & 1
    depth, rows, _ = main.shape
    count = folds(width)
    for face, start in (
        (z_even, (depth - RADIUS) * (1 - z_parity)),
        (z_odd, (depth - RADIUS) * z_parity),
    ):
        face[pl.ds(0, RADIUS)] = main[pl.ds(start, RADIUS)]
        span = folded(RADIUS, width)
        for plane in range(span):
            face[RADIUS + plane] = fold(
                [side[start + plane + span * turn] for turn in range(count)], width
            )
    for face, start in (
        (x_even, (rows - RADIUS) * (1 - x_parity)),
        (x_odd, (rows - RADIUS) * x_parity),
    ):
        start = pl.multiple_of(start, RADIUS)
        face[pl.ds(0, depth)] = main[:, pl.ds(start, RADIUS), :]
        span = folded(depth, width)
        for plane in range(span):
            face[depth + plane] = fold(
                [side[plane + span * turn, pl.ds(start, RADIUS), :] for turn in range(count)],
                width,
            )


def strip_unpack_kernel(
    ids, even, odd, wave, wave_side, older_side, stiff_side, z_even, z_odd, x_even, x_odd
):
    parity = ids[2] & 1
    quarters = LANES // STRIP
    quarter = lane_of(wave.shape[1:]) // STRIP
    from_even = quarter == 3 * parity
    from_odd = quarter == 3 * (1 - parity)
    chunks = wave.shape[0] // quarters
    for number, side in enumerate((wave_side, older_side, stiff_side)):
        for chunk in range(chunks):
            one, two = even[number * chunks + chunk], odd[number * chunks + chunk]
            for turn in range(quarters):
                back = (LANES - STRIP * turn) % LANES
                first = pltpu.roll(one, back, 1) if back else one
                second = pltpu.roll(two, back, 1) if back else two
                side[quarters * chunk + turn] = jnp.where(
                    from_even, first, jnp.where(from_odd, second, 0.0)
                )
    write_faces(STRIP, ids, wave, wave_side, z_even, z_odd, x_even, x_odd)


def fill(width, ids, z_even, z_odd, x_even, x_odd, z_halo, x_halo):
    z_parity, x_parity = ids[0] & 1, ids[1] & 1
    depth = x_halo.shape[1]
    count = folds(width)
    pair = z_even.at[1 - z_parity]
    for face, start in ((pair, RADIUS * (1 - z_parity)), (z_odd, RADIUS * z_parity)):
        z_halo[0, pl.ds(start, RADIUS)] = face[pl.ds(0, RADIUS)]
        span = folded(RADIUS, width)
        for plane in range(span):
            both = face[RADIUS + plane]
            for turn in range(count):
                z_halo[1, start + plane + span * turn] = unfold(both, turn, width)
    for face, start in ((x_even, RADIUS * (1 - x_parity)), (x_odd, RADIUS * x_parity)):
        start = pl.multiple_of(start, RADIUS)
        x_halo[0, :, pl.ds(start, RADIUS), :] = face[pl.ds(0, depth)]
        span = folded(depth, width)
        for plane in range(span):
            both = face[depth + plane]
            for turn in range(count):
                x_halo[1, plane + span * turn, pl.ds(start, RADIUS), :] = unfold(both, turn, width)


def own_kernel(last, wave, side, band_high, band_low, *rest):
    *outs, y_terms = rest
    depth, rows, _ = wave.shape
    width = LANES * len(outs)
    both = jnp.concatenate(
        [wave[...].reshape(depth * rows, LANES), side[...].reshape(depth * rows, LANES)], axis=1
    )
    high = both.astype(BF16)
    low = (both - high.astype(F32)).astype(BF16)
    matrix, remainder = band_high[:, :width], band_low[:, :width]
    y_terms[:, :width] = (
        jnp.dot(high, matrix, preferred_element_type=F32)
        + jnp.dot(low, matrix, preferred_element_type=F32)
        + jnp.dot(high, remainder, preferred_element_type=F32)
    )
    beyond = jnp.zeros((RADIUS, LANES), F32)
    for z in range(depth):
        for part, (field, out) in enumerate(zip((wave, side), outs)):
            column = jnp.concatenate([beyond, field[z], beyond], axis=0)
            turned = [None] + [
                pltpu.roll(column, rows + 2 * RADIUS - offset, 0) for offset in range(1, RADIUS)
            ]
            total = y_terms[z * rows : (z + 1) * rows, part * LANES : (part + 1) * LANES]
            for offset in range(1, RADIUS + 1):
                if offset < RADIUS:
                    near = turned[offset][RADIUS : RADIUS + rows] + turned[RADIUS - offset][:rows]
                else:
                    near = column[2 * RADIUS :] + column[:rows]
                if z + offset < depth:
                    near = near + field[z + offset]
                if z >= offset:
                    near = near + field[z - offset]
                total = total + WEIGHTS[offset - 1] * near
            out[z] = total


def advance(step, ids, wave, side, older, older_side, stiff, stiff_side, forward, image_in,
            planes, own, own_side, fresh, fresh_side, image, z_halo, x_halo):
    depth, rows, _ = wave.shape
    last = step == STEPS - 1
    line = lax.broadcasted_iota(jnp.int32, (RADIUS, LANES), 0)
    before_tile = [
        jnp.where(line < offset, WEIGHTS[offset - 1], 0.0) for offset in range(1, RADIUS + 1)
    ]
    behind_tile = [
        jnp.where(line >= RADIUS - offset, WEIGHTS[offset - 1], 0.0)
        for offset in range(1, RADIUS + 1)
    ]
    between = jnp.zeros((rows - 2 * RADIUS, LANES), F32)

    def one(z, part, partial, field, previous, speed, target):
        total = partial[z]
        first = last_rows = None
        head, tail = x_halo[part, z, :RADIUS], x_halo[part, z, RADIUS:]
        for offset in range(1, RADIUS + 1):
            if z < offset:
                total = total + WEIGHTS[offset - 1] * z_halo[part, RADIUS + z - offset]
            if z + offset >= depth:
                total = total + WEIGHTS[offset - 1] * z_halo[part, RADIUS + z + offset - depth]
            above = pltpu.roll(head, offset, 0) if offset < RADIUS else head
            below = pltpu.roll(tail, RADIUS - offset, 0) if offset < RADIUS else tail
            above = before_tile[offset - 1] * above
            below = behind_tile[offset - 1] * below
            first = above if first is None else first + above
            last_rows = below if last_rows is None else last_rows + below
        total = total + jnp.concatenate([first, between, last_rows], axis=0)
        if z == 0:
            total = total + planes[STEPS * part + step]
        value = 2.0 * field[z] - previous[z] + speed[z] * total
        target[z] = value
        return value

    for z in range(depth):
        value = one(z, 0, own, wave, older, stiff, fresh)
        product = forward[step, z].astype(F32) * value
        if step:
            product = product + image_in[z]
        if last:
            product = product * muting(ids, z, depth, rows)
        image[z] = product
        if not last:
            one(z, 1, own_side, side, older_side, stiff_side, fresh_side)


def muting(ids, z, depth, rows):
    gap_z = (ids[0] * depth + z).astype(F32)
    gap_x = (
        ids[1] * rows + lax.broadcasted_iota(jnp.int32, (rows, LANES), 0) - ids[3]
    ).astype(F32)
    gap_y = (ids[2] * LANES + lane_of((rows, LANES)) - ids[4]).astype(F32)
    distance = gap_z * gap_z + gap_x * gap_x + gap_y * gap_y
    return jnp.minimum(1.0, distance / 576.0)


def step_kernel(step, ids, x_odd_in, x_even_in, z_odd_in, z_even_in, wave, side, older,
                older_side, stiff, stiff_side, forward, own, *rest):
    last = step == STEPS - 1
    own_side = image_in = None
    if not last:
        own_side, *rest = rest
    if step:
        planes, image_in, *rest = rest
    else:
        planes, *rest = rest
        face = z_even_in.shape[1] - 2 * STEPS
        both = z_even_in[0, pl.ds(face, 2 * STEPS)] + z_even_in[1, pl.ds(face, 2 * STEPS)]
        planes[...] = jnp.where(ids[0] == 0, both, 0.0)
    if last:
        image, fresh, z_halo, x_halo = rest
        fresh_side = None
    else:
        image, fresh, fresh_side, z_even, z_odd, x_even, x_odd, z_halo, x_halo = rest
    fill(strip_width(step), ids, z_even_in, z_odd_in, x_even_in, x_odd_in, z_halo, x_halo)
    advance(step, ids, wave, side, older, older_side, stiff, stiff_side, forward, image_in,
            planes, own, own_side, fresh, fresh_side, image, z_halo, x_halo)
    if not last:
        write_faces(strip_width(step + 1), ids, fresh, fresh_side, z_even, z_odd, x_even, x_odd)


def swap(block, axis, parity):
    count = lax.axis_size(axis)
    pairs = []
    for left in range(parity, count - 1, 2):
        pairs += [(left, left + 1), (left + 1, left)]
    return lax.ppermute(block, axis, pairs)


def pair_gather(block, axis, parity):
    count = lax.axis_size(axis)
    groups = [
        [(2 * pair + parity) % count, (2 * pair + parity + 1) % count]
        for pair in range(count // 2)
    ]
    return lax.all_gather(block, axis, axis=0, tiled=False, axis_index_groups=groups)


def exchange(faces):
    z_even, z_odd, x_even, x_odd = faces
    z_odd = swap(z_odd, "gz", 1)
    x_even = swap(x_even, "gx", 0)
    x_odd = swap(x_odd, "gx", 1)
    z_even = pair_gather(z_even, "gz", 0)
    return z_even, z_odd, x_even, x_odd


def on_device(
    stiffness, older_wave, wave_now, forward_wave, residuals, owners, receivers, source_cell
):
    depth, rows, cols = wave_now.shape
    span_x, span_y, span_z = (lax.axis_size(axis) for axis in ("gx", "gy", "gz"))
    tiles = span_x * span_y
    total_y = cols * span_y
    ids = jnp.stack(
        [
            lax.axis_index("gz"),
            lax.axis_index("gx"),
            lax.axis_index("gy"),
            source_cell[0] // total_y,
            source_cell[0] % total_y,
        ]
    ).astype(jnp.int32)
    band_high, band_low = (jnp.asarray(part) for part in band())
    block = shaped(depth, rows, LANES)

    def faces_out(step):
        width = strip_width(step)
        z_face = shaped(RADIUS + folded(RADIUS, width), rows, LANES)
        x_face = shaped(depth + folded(depth, width), RADIUS, LANES)
        return [z_face, z_face, x_face, x_face]

    strips = shaped(3 * depth * STRIP // LANES, rows, LANES)
    packets, even, odd = call(
        functools.partial(prepare_kernel, span_y, tiles),
        [shaped(tiles, LANES), strips, strips],
        [ids, residuals, owners.reshape(1, -1), receivers.reshape(1, -1), wave_now, older_wave,
         stiffness],
        in_specs=[smem()] + [pl.BlockSpec()] * 6,
        grant=60,
    )
    packets = lax.all_to_all(packets, ("gx", "gy"), 0, 0, tiled=True)
    packets, even, odd = lax.optimization_barrier((packets, even, odd))
    even, odd = (swap(strip, "gy", parity) for parity, strip in enumerate((even, odd)))
    side, older_side, stiff_side, *faces = call(
        strip_unpack_kernel,
        [block] * 3 + faces_out(0),
        [ids, even, odd, wave_now],
    )
    cores = 2
    packets = [packets] + [
        lax.ppermute(packets, "gz", [(chip + core, core) for core in range(cores)])
        for chip in range(cores, span_z, cores)
    ]
    face = faces[0].shape[0]
    faces[0] = call(
        functools.partial(plane_kernel, face, rows),
        shaped(face + 2 * STEPS, rows, LANES),
        [ids, faces[0], *packets],
        scratch=[pltpu.VMEM((LANES, span_z // cores * tiles), F32)],
    )

    scratch = [
        pltpu.VMEM((2, 2 * RADIUS, rows, LANES), F32),
        pltpu.VMEM((2, depth, 2 * RADIUS, LANES), F32),
    ]
    wave, older = wave_now, older_wave
    image = None
    for step in range(STEPS):
        last = step == STEPS - 1
        own = call(
            functools.partial(own_kernel, last),
            [block] if last else [block, block],
            [wave, side, band_high, band_low],
            scratch=[pltpu.VMEM((depth * rows, 2 * LANES), F32)],
            in_specs=[vmem()] * 4,
        )
        faces = exchange(faces)
        ins = [ids, *faces[::-1], wave, side, older, older_side, stiffness, stiff_side, forward_wave,
               *own]
        outs = [block, block]
        if step:
            ins += [planes, image]
        else:
            outs = [shaped(2 * STEPS, rows, LANES)] + outs
        if not last:
            outs += [block] + faces_out(step + 1)
        rest = call(functools.partial(step_kernel, step), outs, ins, scratch)
        if not step:
            planes, *rest = rest
        image, fresh, *rest = rest
        older, wave = wave, fresh
        if not last:
            older_side, side = side, rest[0]
            faces = rest[1:]
    return image, older, wave


def solution(mesh):
    in_specs = (
        P("gz", "gx", "gy"),
        P("gz", "gx", "gy"),
        P("gz", "gx", "gy"),
        P(None, "gz", "gx", "gy"),
        P(None, ("gx", "gy", "gz")),
        P(("gx", "gy", "gz"), None),
        P(("gx", "gy", "gz")),
        P(),
    )
    out_specs = (P("gz", "gx", "gy"), P("gz", "gx", "gy"), P("gz", "gx", "gy"))
    return jax.shard_map(
        on_device, mesh=mesh, in_specs=in_specs, out_specs=out_specs, check_vma=False
    )
```

```python
import functools
import math

import jax
import jax.numpy as jnp
import numpy as np
from jax import lax
from jax.experimental import pallas as pl
from jax.experimental.pallas import tpu as pltpu
from jax.sharding import PartitionSpec as P

STEPS = 4
RADIUS = 8
LANES = 128
STRIP = 32
CAP = 8
CHUNK = 4
SLOTS = 3 * CAP
F32 = jnp.float32
BF16 = jnp.bfloat16


def stencil_weights():
    window = [math.cos(math.pi * offset / 20.0) for offset in range(1, RADIUS + 1)]
    alternating = sum(
        ((-1.0) ** (offset + 1) * window[offset - 1] for offset in range(1, RADIUS + 1))
    )
    factor = 1.0 / (2.0 * alternating)
    weights = []
    for offset in range(1, RADIUS + 1):
        weights.append(
            factor * 2.0 * (-1.0) ** (offset + 1) * window[offset - 1] / (offset * offset)
        )
    return (weights, -2.0 * sum(weights))


WEIGHTS, CENTER = stencil_weights()


def band():
    size = 2 * LANES
    matrix = np.zeros((size, size), np.float64)
    for column in range(size):
        matrix[column, column] = 3.0 * CENTER
        for offset in range(1, RADIUS + 1):
            matrix[(column + offset) % size, column] = WEIGHTS[offset - 1]
            matrix[(column - offset) % size, column] = WEIGHTS[offset - 1]
    matrix = matrix.astype(np.float32)
    high = matrix.astype(jnp.bfloat16)
    low = (matrix - high.astype(np.float32)).astype(jnp.bfloat16)
    return high, low


def lane_of(shape):
    return lax.broadcasted_iota(jnp.int32, shape, len(shape) - 1)


def vmem():
    return pl.BlockSpec(memory_space=pltpu.VMEM)


def smem():
    return pl.BlockSpec(memory_space=pltpu.SMEM)


def call(body, outs, ins, scratch=(), in_specs=None, grant=32, out_specs=None):
    return pl.pallas_call(
        body,
        out_shape=outs,
        in_specs=in_specs or [smem()] + [vmem()] * (len(ins) - 1),
        out_specs=out_specs or jax.tree.map(lambda _: vmem(), outs),
        scratch_shapes=list(scratch),
        compiler_params=pltpu.CompilerParams(vmem_limit_bytes=grant * 1024 * 1024),
        cost_estimate=pl.CostEstimate(flops=1_000_000, bytes_accessed=2_000_000, transcendentals=0),
    )(*ins)


def shaped(*shape):
    return jax.ShapeDtypeStruct(shape, F32)


def split3(value):
    high = value.astype(BF16)
    rest = value - high.astype(F32)
    middle = rest.astype(BF16)
    return high, middle, (rest - middle.astype(F32)).astype(BF16)


def dot_nt(left, right):
    return lax.dot_general(left, right, (((1,), (1,)), ((), ())), preferred_element_type=F32)


def prepare_kernel(span_y, tiles, ids, residuals, owners, cells, wave, older, stiff, packets,
                   even, odd, held, sems):
    copies = [
        pltpu.make_async_copy(field, held.at[number], sems.at[number])
        for number, field in enumerate((wave, older, stiff))
    ]
    for copy in copies:
        copy.start()
    pack_slots(span_y, tiles, residuals, owners, cells, packets)
    for copy in copies:
        copy.wait()
    pack_strips(ids, held.at[0], held.at[1], held.at[2], even, odd)


def pack_slots(span_y, tiles, residuals, owner_row, cell_row, out):
    rows = residuals.shape[1]
    owner = owner_row[...]
    owner_column = jnp.transpose(jnp.broadcast_to(owner.astype(F32), (rows, rows)))
    earlier = (owner_column.astype(jnp.int32) == owner) & (
        lax.broadcasted_iota(jnp.int32, (rows, rows), 0)
        < lax.broadcasted_iota(jnp.int32, (rows, rows), 1)
    )
    rank = jnp.sum(earlier.astype(jnp.int32), axis=0, keepdims=True)
    cell = cell_row[...]
    along = cell & (LANES - 1)
    fields = [residuals[pl.ds(field, 1), :] for field in range(STEPS)] + [cell.astype(F32)]
    stacked = jnp.concatenate(
        [jnp.broadcast_to(field, (SLOTS, rows)) for field in fields]
        + [jnp.zeros((LANES - SLOTS * len(fields), rows), F32)],
        axis=0,
    )
    line = lax.broadcasted_iota(jnp.int32, (LANES, rows), 0)
    slot = line - SLOTS * (line // SLOTS)
    tile = lax.broadcasted_iota(jnp.int32, (tiles, rows), 0)
    place = tile & (span_y - 1)
    total = jnp.zeros((tiles, LANES), F32)
    for group in range(3):
        named = owner == tile + (group - 1)
        wanted = slot == rank + CAP * group
        if group == 0:
            named = named & (place != 0)
            wanted = wanted & (along >= LANES - STRIP)
        if group == 2:
            named = named & (place != span_y - 1)
            wanted = wanted & (along < STRIP)
        chosen = named.astype(F32).astype(BF16)
        for part in split3(jnp.where(wanted, stacked, 0.0)):
            total = total + dot_nt(chosen, part)
    out[...] = total


def plane_kernel(face, rows, ids, z_even, *refs):
    *packets, out, turned = refs
    out[pl.ds(0, face)] = z_even[...]
    out[pl.ds(face, 2 * STEPS)] = jnp.zeros((2 * STEPS, rows, LANES), F32)

    @pl.when(ids[0] < 2)
    def _():
        count = turned.shape[1]
        share = count // len(packets)
        for number, packet in enumerate(packets):
            turned[:, share * number : share * (number + 1)] = jnp.transpose(packet[...])
        line = lax.broadcasted_iota(jnp.int32, (rows, count), 0)
        spot = lax.broadcasted_iota(jnp.int32, (LANES, count), 0)

        def product(slot):
            cell = turned[pl.ds(SLOTS * STEPS + slot, 1), :].astype(jnp.int32)
            hit = (cell >> 7) == line
            highs, lows = [], []
            for step in range(STEPS):
                value = turned[pl.ds(SLOTS * step + slot, 1), :]
                high = value.astype(BF16).astype(F32)
                highs.append(jnp.where(hit, high, 0.0))
                lows.append(jnp.where(hit, value - high, 0.0))
            left = jnp.concatenate(highs + lows, axis=0).astype(BF16)
            right = jnp.where((cell & (LANES - 1)) == spot, 1.0, 0.0).astype(BF16)
            both = dot_nt(left, right)
            return both[: STEPS * rows] + both[STEPS * rows :]

        for part, groups in enumerate(((1,), (0, 2))):
            total = None
            for slot in [CAP * group + rank for group in groups for rank in range(CAP)]:
                total = product(slot) if total is None else total + product(slot)
            out[pl.ds(face + STEPS * part, STEPS)] = total.reshape(STEPS, rows, LANES)


def pack_strips(ids, wave, older, stiff, even, odd):
    parity = ids[2] & 1
    quarter = lane_of(wave.shape[1:]) // STRIP
    low, high = quarter == 0, quarter == 3
    quarters = LANES // STRIP
    for number, field in enumerate((wave, older, stiff)):
        for chunk in range(field.shape[0] // quarters):
            lows = highs = None
            for turn in range(quarters):
                value = field[quarters * chunk + turn]
                one = jnp.where(low, value, 0.0)
                two = jnp.where(high, value, 0.0)
                if turn:
                    one = pltpu.roll(one, STRIP * turn, 1)
                    two = pltpu.roll(two, STRIP * turn, 1)
                lows = one if lows is None else lows + one
                highs = two if highs is None else highs + two
            place = number * (field.shape[0] // quarters) + chunk
            even[place] = jnp.where(parity == 0, highs, lows)
            odd[place] = jnp.where(parity == 0, lows, highs)


def strip_width(step):
    return {0: STRIP, 1: STRIP // 2, 2: STRIP // 4}.get(step, 0)


def folds(width):
    return LANES // (2 * width) if width else 0


def folded(length, width):
    return length // folds(width) if width else 0


def kept_lanes(shape, width):
    lane = lane_of(shape)
    return (lane < width) | (lane >= LANES - width)


def fold(pieces, width):
    total = None
    for turn, piece in enumerate(pieces):
        piece = jnp.where(kept_lanes(piece.shape, width), piece, 0.0)
        if turn:
            piece = pltpu.roll(piece, 2 * width * turn, 1)
        total = piece if total is None else total + piece
    return total


def unfold(both, turn, width):
    if turn:
        both = pltpu.roll(both, LANES - 2 * width * turn, 1)
    return jnp.where(kept_lanes(both.shape, width), both, 0.0)


def write_faces(width, ids, main, side, z_even, z_odd, x_even, x_odd):
    z_parity, x_parity = ids[0] & 1, ids[1] & 1
    depth, rows, _ = main.shape
    count = folds(width)
    for face, start in (
        (z_even, (depth - RADIUS) * (1 - z_parity)),
        (z_odd, (depth - RADIUS) * z_parity),
    ):
        face[pl.ds(0, RADIUS)] = main[pl.ds(start, RADIUS)]
        span = folded(RADIUS, width)
        for plane in range(span):
            face[RADIUS + plane] = fold(
                [side[start + plane + span * turn] for turn in range(count)], width
            )
    for face, start in (
        (x_even, (rows - RADIUS) * (1 - x_parity)),
        (x_odd, (rows - RADIUS) * x_parity),
    ):
        start = pl.multiple_of(start, RADIUS)
        face[pl.ds(0, depth)] = main[:, pl.ds(start, RADIUS), :]
        span = folded(depth, width)
        for plane in range(span):
            face[depth + plane] = fold(
                [side[plane + span * turn, pl.ds(start, RADIUS), :] for turn in range(count)],
                width,
            )


def strip_unpack_kernel(
    ids, even, odd, wave, wave_side, older_side, stiff_side, z_even, z_odd, x_even, x_odd
):
    parity = ids[2] & 1
    quarters = LANES // STRIP
    quarter = lane_of(wave.shape[1:]) // STRIP
    from_even = quarter == 3 * parity
    from_odd = quarter == 3 * (1 - parity)
    chunks = wave.shape[0] // quarters
    for number, side in enumerate((wave_side, older_side, stiff_side)):
        for chunk in range(chunks):
            one, two = even[number * chunks + chunk], odd[number * chunks + chunk]
            for turn in range(quarters):
                back = (LANES - STRIP * turn) % LANES
                first = pltpu.roll(one, back, 1) if back else one
                second = pltpu.roll(two, back, 1) if back else two
                side[quarters * chunk + turn] = jnp.where(
                    from_even, first, jnp.where(from_odd, second, 0.0)
                )
    write_faces(STRIP, ids, wave, wave_side, z_even, z_odd, x_even, x_odd)


def fill(width, ids, z_even, z_odd, x_even, x_odd, z_halo, x_halo):
    z_parity, x_parity = ids[0] & 1, ids[1] & 1
    depth = x_halo.shape[1]
    count = folds(width)
    pair = z_even.at[1 - z_parity]
    for face, start in ((pair, RADIUS * (1 - z_parity)), (z_odd, RADIUS * z_parity)):
        z_halo[0, pl.ds(start, RADIUS)] = face[pl.ds(0, RADIUS)]
        span = folded(RADIUS, width)
        for plane in range(span):
            both = face[RADIUS + plane]
            for turn in range(count):
                z_halo[1, start + plane + span * turn] = unfold(both, turn, width)
    for face, start in ((x_even, RADIUS * (1 - x_parity)), (x_odd, RADIUS * x_parity)):
        start = pl.multiple_of(start, RADIUS)
        x_halo[0, :, pl.ds(start, RADIUS), :] = face[pl.ds(0, depth)]
        span = folded(depth, width)
        for plane in range(span):
            both = face[depth + plane]
            for turn in range(count):
                x_halo[1, plane + span * turn, pl.ds(start, RADIUS), :] = unfold(both, turn, width)


def own_kernel(last, wave, side, band_high, band_low, *rest):
    *outs, y_terms = rest
    depth, rows, _ = wave.shape
    if last:
        outs, kept = outs[:1], outs[1]
        kept[...] = wave[...]
    width = LANES * len(outs)
    both = jnp.concatenate(
        [wave[...].reshape(depth * rows, LANES), side[...].reshape(depth * rows, LANES)], axis=1
    )
    high = both.astype(BF16)
    low = (both - high.astype(F32)).astype(BF16)
    matrix, remainder = band_high[:, :width], band_low[:, :width]
    y_terms[:, :width] = (
        jnp.dot(high, matrix, preferred_element_type=F32)
        + jnp.dot(low, matrix, preferred_element_type=F32)
        + jnp.dot(high, remainder, preferred_element_type=F32)
    )
    beyond = jnp.zeros((RADIUS, LANES), F32)
    for z in range(depth):
        for part, (field, out) in enumerate(zip((wave, side), outs)):
            column = jnp.concatenate([beyond, field[z], beyond], axis=0)
            turned = [None] + [
                pltpu.roll(column, rows + 2 * RADIUS - offset, 0) for offset in range(1, RADIUS)
            ]
            total = y_terms[z * rows : (z + 1) * rows, part * LANES : (part + 1) * LANES]
            for offset in range(1, RADIUS + 1):
                if offset < RADIUS:
                    near = turned[offset][RADIUS : RADIUS + rows] + turned[RADIUS - offset][:rows]
                else:
                    near = column[2 * RADIUS :] + column[:rows]
                if z + offset < depth:
                    near = near + field[z + offset]
                if z >= offset:
                    near = near + field[z - offset]
                total = total + WEIGHTS[offset - 1] * near
            out[z] = total


def advance(step, shot, ids, wave, side, older, older_side, stiff, stiff_side, forward, image_in,
            planes, own, own_side, fresh, fresh_side, image, z_halo, x_halo, done=None):
    depth, rows, _ = wave.shape
    last = step == STEPS - 1
    line = lax.broadcasted_iota(jnp.int32, (RADIUS, LANES), 0)
    before_tile = [
        jnp.where(line < offset, WEIGHTS[offset - 1], 0.0) for offset in range(1, RADIUS + 1)
    ]
    behind_tile = [
        jnp.where(line >= RADIUS - offset, WEIGHTS[offset - 1], 0.0)
        for offset in range(1, RADIUS + 1)
    ]
    between = jnp.zeros((rows - 2 * RADIUS, LANES), F32)

    def one(z, part, partial, field, previous, speed, target):
        total = partial[z]
        first = last_rows = None
        head, tail = x_halo[part, z, :RADIUS], x_halo[part, z, RADIUS:]
        for offset in range(1, RADIUS + 1):
            if z < offset:
                total = total + WEIGHTS[offset - 1] * z_halo[part, RADIUS + z - offset]
            if z + offset >= depth:
                total = total + WEIGHTS[offset - 1] * z_halo[part, RADIUS + z + offset - depth]
            above = pltpu.roll(head, offset, 0) if offset < RADIUS else head
            below = pltpu.roll(tail, RADIUS - offset, 0) if offset < RADIUS else tail
            above = before_tile[offset - 1] * above
            below = behind_tile[offset - 1] * below
            first = above if first is None else first + above
            last_rows = below if last_rows is None else last_rows + below
        total = total + jnp.concatenate([first, between, last_rows], axis=0)
        if z == 0:
            total = total + planes[STEPS * part + step]
        value = 2.0 * field[z] - previous[z] + speed[z] * total
        target[z] = value
        return value

    for z in range(depth):
        value = one(z, 0, own, wave, older, stiff, fresh)
        product = forward[step, z].astype(F32) * value
        if step:
            product = product + image_in[z]
        if last:
            product = product * muting(ids, *shot, z, depth, rows)
        image[z] = product
        if done is not None:
            done(z)
        if not last:
            one(z, 1, own_side, side, older_side, stiff_side, fresh_side)


def muting(ids, shot_x, shot_y, z, depth, rows):
    gap_z = (ids[0] * depth + z).astype(F32)
    gap_x = (
        ids[1] * rows + lax.broadcasted_iota(jnp.int32, (rows, LANES), 0) - shot_x
    ).astype(F32)
    gap_y = (ids[2] * LANES + lane_of((rows, LANES)) - shot_y).astype(F32)
    distance = gap_z * gap_z + gap_x * gap_x + gap_y * gap_y
    return jnp.minimum(1.0, distance / 576.0)


def step_kernel(step, total_y, ids, x_odd_in, x_even_in, z_odd_in, z_even_in, wave, side, older,
                older_side, stiff, stiff_side, forward, own, *rest):
    last = step == STEPS - 1
    own_side = image_in = None
    if not last:
        own_side, *rest = rest
    if step:
        planes, image_in, *rest = rest
    else:
        planes, *rest = rest
        face = z_even_in.shape[1] - 2 * STEPS
        both = z_even_in[0, pl.ds(face, 2 * STEPS)] + z_even_in[1, pl.ds(face, 2 * STEPS)]
        planes[...] = jnp.where(ids[0] == 0, both, 0.0)
    shot = done = None
    copies = []
    if last:
        (source, image_out, wave_out, z_halo, x_halo, image, fresh, sems) = rest
        fresh_side = None
        shot = (lax.div(source[0], total_y), lax.rem(source[0], total_y))

        def done(z):
            if (z + 1) % CHUNK:
                return
            chunk = pl.ds(z + 1 - CHUNK, CHUNK)
            for number, (held, out) in enumerate(((image, image_out), (fresh, wave_out))):
                copies.append(
                    pltpu.make_async_copy(
                        held.at[chunk], out.at[chunk], sems.at[number, z // CHUNK]
                    )
                )
                copies[-1].start()

    else:
        image, fresh, fresh_side, z_even, z_odd, x_even, x_odd, z_halo, x_halo = rest
    fill(strip_width(step), ids, z_even_in, z_odd_in, x_even_in, x_odd_in, z_halo, x_halo)
    advance(step, shot, ids, wave, side, older, older_side, stiff, stiff_side, forward, image_in,
            planes, own, own_side, fresh, fresh_side, image, z_halo, x_halo, done)
    for copy in copies:
        copy.wait()
    if not last:
        write_faces(strip_width(step + 1), ids, fresh, fresh_side, z_even, z_odd, x_even, x_odd)


def swap(block, axis, parity):
    count = lax.axis_size(axis)
    pairs = []
    for left in range(parity, count - 1, 2):
        pairs += [(left, left + 1), (left + 1, left)]
    return lax.ppermute(block, axis, pairs)


def pair_gather(block, axis, parity):
    count = lax.axis_size(axis)
    groups = [
        [(2 * pair + parity) % count, (2 * pair + parity + 1) % count]
        for pair in range(count // 2)
    ]
    return lax.all_gather(block, axis, axis=0, tiled=False, axis_index_groups=groups)


def exchange(faces):
    z_even, z_odd, x_even, x_odd = faces
    z_odd = swap(z_odd, "gz", 1)
    x_even = swap(x_even, "gx", 0)
    x_odd = swap(x_odd, "gx", 1)
    z_even = pair_gather(z_even, "gz", 0)
    return z_even, z_odd, x_even, x_odd


def on_device(
    stiffness, older_wave, wave_now, forward_wave, residuals, owners, receivers, source_cell
):
    depth, rows, cols = wave_now.shape
    span_x, span_y, span_z = (lax.axis_size(axis) for axis in ("gx", "gy", "gz"))
    tiles = span_x * span_y
    ids = jnp.stack(
        [
            lax.axis_index("gz"),
            lax.axis_index("gx"),
            lax.axis_index("gy"),
        ]
    ).astype(jnp.int32)
    band_high, band_low = (jnp.asarray(part) for part in band())
    block = shaped(depth, rows, LANES)

    def faces_out(step):
        width = strip_width(step)
        z_face = shaped(RADIUS + folded(RADIUS, width), rows, LANES)
        x_face = shaped(depth + folded(depth, width), RADIUS, LANES)
        return [z_face, z_face, x_face, x_face]

    strips = shaped(3 * depth * STRIP // LANES, rows, LANES)
    packets, even, odd = call(
        functools.partial(prepare_kernel, span_y, tiles),
        [shaped(tiles, LANES), strips, strips],
        [ids, residuals, owners.reshape(1, -1), receivers.reshape(1, -1), wave_now, older_wave,
         stiffness],
        scratch=[pltpu.VMEM((3, depth, rows, LANES), F32), pltpu.SemaphoreType.DMA((3,))],
        in_specs=[smem()] + [pl.BlockSpec()] * 3 + [pl.BlockSpec(memory_space=pl.ANY)] * 3,
        grant=60,
    )
    packets = lax.all_to_all(packets, ("gx", "gy"), 0, 0, tiled=True)
    packets, even, odd = lax.optimization_barrier((packets, even, odd))
    even, odd = (swap(strip, "gy", parity) for parity, strip in enumerate((even, odd)))
    side, older_side, stiff_side, *faces = call(
        strip_unpack_kernel,
        [block] * 3 + faces_out(0),
        [ids, even, odd, wave_now],
    )
    cores = 2
    packets = [packets] + [
        lax.ppermute(packets, "gz", [(chip + core, core) for core in range(cores)])
        for chip in range(cores, span_z, cores)
    ]
    face = faces[0].shape[0]
    faces[0] = call(
        functools.partial(plane_kernel, face, rows),
        shaped(face + 2 * STEPS, rows, LANES),
        [ids, faces[0], *packets],
        scratch=[pltpu.VMEM((LANES, span_z // cores * tiles), F32)],
    )

    scratch = [
        pltpu.VMEM((2, 2 * RADIUS, rows, LANES), F32),
        pltpu.VMEM((2, depth, 2 * RADIUS, LANES), F32),
    ]
    wave, older = wave_now, older_wave
    image = None
    for step in range(STEPS):
        last = step == STEPS - 1
        own = call(
            functools.partial(own_kernel, last),
            [block, block],
            [wave, side, band_high, band_low],
            scratch=[pltpu.VMEM((depth * rows, 2 * LANES), F32)],
            in_specs=[vmem()] * 4,
        )
        if last:
            *own, last_older = own
        faces = exchange(faces)
        ins = [ids, *faces[::-1], wave, side, older, older_side, stiffness, stiff_side, forward_wave,
               *own]
        outs = [block, block]
        if step:
            ins += [planes, image]
        else:
            outs = [shaped(2 * STEPS, rows, LANES)] + outs
        if not last:
            outs += [block] + faces_out(step + 1)
        room, in_specs, out_specs = scratch, None, None
        if last:
            ins.append(source_cell)
            in_specs = [smem()] + [vmem()] * (len(ins) - 2) + [smem()]
            out_specs = [pl.BlockSpec(memory_space=pl.ANY)] * 2
            held = pltpu.VMEM((depth, rows, LANES), F32)
            room = scratch + [held, held, pltpu.SemaphoreType.DMA((2, depth // CHUNK))]
        rest = call(
            functools.partial(step_kernel, step, cols * span_y), outs, ins, room, in_specs,
            out_specs=out_specs,
        )
        if not step:
            planes, *rest = rest
        image, fresh, *rest = rest
        older, wave = wave, fresh
        if not last:
            older_side, side = side, rest[0]
            faces = rest[1:]
    return image, last_older, wave


def solution(mesh):
    in_specs = (
        P("gz", "gx", "gy"),
        P("gz", "gx", "gy"),
        P("gz", "gx", "gy"),
        P(None, "gz", "gx", "gy"),
        P(None, ("gx", "gy", "gz")),
        P(("gx", "gy", "gz"), None),
        P(("gx", "gy", "gz")),
        P(),
    )
    out_specs = (P("gz", "gx", "gy"), P("gz", "gx", "gy"), P("gz", "gx", "gy"))
    return jax.shard_map(
        on_device, mesh=mesh, in_specs=in_specs, out_specs=out_specs, check_vma=False
    )
```

```python
import functools
import math

import jax
import jax.numpy as jnp
import numpy as np
from jax import lax
from jax.experimental import pallas as pl
from jax.experimental.pallas import tpu as pltpu
from jax.sharding import PartitionSpec as P

STEPS = 4
RADIUS = 8
LANES = 128
STRIP = 32
CAP = 8
CHUNK = 4
SLOTS = 3 * CAP
F32 = jnp.float32
BF16 = jnp.bfloat16


def stencil_weights():
    window = [math.cos(math.pi * offset / 20.0) for offset in range(1, RADIUS + 1)]
    alternating = sum(
        ((-1.0) ** (offset + 1) * window[offset - 1] for offset in range(1, RADIUS + 1))
    )
    factor = 1.0 / (2.0 * alternating)
    weights = []
    for offset in range(1, RADIUS + 1):
        weights.append(
            factor * 2.0 * (-1.0) ** (offset + 1) * window[offset - 1] / (offset * offset)
        )
    return (weights, -2.0 * sum(weights))


WEIGHTS, CENTER = stencil_weights()


def band():
    size = 2 * LANES
    matrix = np.zeros((size, size), np.float64)
    for column in range(size):
        matrix[column, column] = 3.0 * CENTER
        for offset in range(1, RADIUS + 1):
            matrix[(column + offset) % size, column] = WEIGHTS[offset - 1]
            matrix[(column - offset) % size, column] = WEIGHTS[offset - 1]
    matrix = matrix.astype(np.float32)
    high = matrix.astype(jnp.bfloat16)
    low = (matrix - high.astype(np.float32)).astype(jnp.bfloat16)
    return high, low


def lane_of(shape):
    return lax.broadcasted_iota(jnp.int32, shape, len(shape) - 1)


def vmem():
    return pl.BlockSpec(memory_space=pltpu.VMEM)


def smem():
    return pl.BlockSpec(memory_space=pltpu.SMEM)


def call(body, outs, ins, scratch=(), in_specs=None, grant=32, out_specs=None):
    return pl.pallas_call(
        body,
        out_shape=outs,
        in_specs=in_specs or [smem()] + [vmem()] * (len(ins) - 1),
        out_specs=out_specs or jax.tree.map(lambda _: vmem(), outs),
        scratch_shapes=list(scratch),
        compiler_params=pltpu.CompilerParams(vmem_limit_bytes=grant * 1024 * 1024),
        cost_estimate=pl.CostEstimate(flops=1_000_000, bytes_accessed=2_000_000, transcendentals=0),
    )(*ins)


def shaped(*shape):
    return jax.ShapeDtypeStruct(shape, F32)


def split3(value):
    high = value.astype(BF16)
    rest = value - high.astype(F32)
    middle = rest.astype(BF16)
    return high, middle, (rest - middle.astype(F32)).astype(BF16)


def dot_nt(left, right):
    return lax.dot_general(left, right, (((1,), (1,)), ((), ())), preferred_element_type=F32)


def prepare_kernel(span_y, tiles, ids, residuals, owners, cells, wave, older, stiff, packets,
                   even, odd):
    pack_slots(span_y, tiles, residuals, owners, cells, packets)
    pack_strips(ids, wave, older, stiff, even, odd)


def pack_slots(span_y, tiles, residuals, owner_row, cell_row, out):
    rows = residuals.shape[1]
    owner = owner_row[...]
    owner_column = jnp.transpose(jnp.broadcast_to(owner.astype(F32), (rows, rows)))
    earlier = (owner_column.astype(jnp.int32) == owner) & (
        lax.broadcasted_iota(jnp.int32, (rows, rows), 0)
        < lax.broadcasted_iota(jnp.int32, (rows, rows), 1)
    )
    rank = jnp.sum(earlier.astype(jnp.int32), axis=0, keepdims=True)
    cell = cell_row[...]
    along = cell & (LANES - 1)
    fields = [residuals[pl.ds(field, 1), :] for field in range(STEPS)] + [cell.astype(F32)]
    stacked = jnp.concatenate(
        [jnp.broadcast_to(field, (SLOTS, rows)) for field in fields]
        + [jnp.zeros((LANES - SLOTS * len(fields), rows), F32)],
        axis=0,
    )
    line = lax.broadcasted_iota(jnp.int32, (LANES, rows), 0)
    slot = line - SLOTS * (line // SLOTS)
    tile = lax.broadcasted_iota(jnp.int32, (tiles, rows), 0)
    place = tile & (span_y - 1)
    total = jnp.zeros((tiles, LANES), F32)
    for group in range(3):
        named = owner == tile + (group - 1)
        wanted = slot == rank + CAP * group
        if group == 0:
            named = named & (place != 0)
            wanted = wanted & (along >= LANES - STRIP)
        if group == 2:
            named = named & (place != span_y - 1)
            wanted = wanted & (along < STRIP)
        chosen = named.astype(F32).astype(BF16)
        for part in split3(jnp.where(wanted, stacked, 0.0)):
            total = total + dot_nt(chosen, part)
    out[...] = total


def plane_kernel(face, rows, ids, z_even, *refs):
    *packets, out, turned = refs
    out[pl.ds(0, face)] = z_even[...]
    out[pl.ds(face, 2 * STEPS)] = jnp.zeros((2 * STEPS, rows, LANES), F32)

    @pl.when(ids[0] < 2)
    def _():
        count = turned.shape[1]
        share = count // len(packets)
        for number, packet in enumerate(packets):
            turned[:, share * number : share * (number + 1)] = jnp.transpose(packet[...])
        line = lax.broadcasted_iota(jnp.int32, (rows, count), 0)
        spot = lax.broadcasted_iota(jnp.int32, (LANES, count), 0)

        def product(slot):
            cell = turned[pl.ds(SLOTS * STEPS + slot, 1), :].astype(jnp.int32)
            hit = (cell >> 7) == line
            highs, lows = [], []
            for step in range(STEPS):
                value = turned[pl.ds(SLOTS * step + slot, 1), :]
                high = value.astype(BF16).astype(F32)
                highs.append(jnp.where(hit, high, 0.0))
                lows.append(jnp.where(hit, value - high, 0.0))
            left = jnp.concatenate(highs + lows, axis=0).astype(BF16)
            right = jnp.where((cell & (LANES - 1)) == spot, 1.0, 0.0).astype(BF16)
            both = dot_nt(left, right)
            return both[: STEPS * rows] + both[STEPS * rows :]

        for part, groups in enumerate(((1,), (0, 2))):
            total = None
            for slot in [CAP * group + rank for group in groups for rank in range(CAP)]:
                total = product(slot) if total is None else total + product(slot)
            out[pl.ds(face + STEPS * part, STEPS)] = total.reshape(STEPS, rows, LANES)


def pack_strips(ids, wave, older, stiff, even, odd):
    parity = ids[2] & 1
    quarter = lane_of(wave.shape[1:]) // STRIP
    low, high = quarter == 0, quarter == 3
    quarters = LANES // STRIP
    for number, field in enumerate((wave, older, stiff)):
        for chunk in range(field.shape[0] // quarters):
            lows = highs = None
            for turn in range(quarters):
                value = field[quarters * chunk + turn]
                one = jnp.where(low, value, 0.0)
                two = jnp.where(high, value, 0.0)
                if turn:
                    one = pltpu.roll(one, STRIP * turn, 1)
                    two = pltpu.roll(two, STRIP * turn, 1)
                lows = one if lows is None else lows + one
                highs = two if highs is None else highs + two
            place = number * (field.shape[0] // quarters) + chunk
            even[place] = jnp.where(parity == 0, highs, lows)
            odd[place] = jnp.where(parity == 0, lows, highs)


def strip_width(step):
    return {0: STRIP, 1: STRIP // 2, 2: STRIP // 4}.get(step, 0)


def folds(width):
    return LANES // (2 * width) if width else 0


def folded(length, width):
    return length // folds(width) if width else 0


def kept_lanes(shape, width):
    lane = lane_of(shape)
    return (lane < width) | (lane >= LANES - width)


def fold(pieces, width):
    total = None
    for turn, piece in enumerate(pieces):
        piece = jnp.where(kept_lanes(piece.shape, width), piece, 0.0)
        if turn:
            piece = pltpu.roll(piece, 2 * width * turn, 1)
        total = piece if total is None else total + piece
    return total


def unfold(both, turn, width):
    if turn:
        both = pltpu.roll(both, LANES - 2 * width * turn, 1)
    return jnp.where(kept_lanes(both.shape, width), both, 0.0)


def write_faces(width, ids, main, side, z_even, z_odd, x_even, x_odd):
    z_parity, x_parity = ids[0] & 1, ids[1] & 1
    depth, rows, _ = main.shape
    count = folds(width)
    for face, start in (
        (z_even, (depth - RADIUS) * (1 - z_parity)),
        (z_odd, (depth - RADIUS) * z_parity),
    ):
        face[pl.ds(0, RADIUS)] = main[pl.ds(start, RADIUS)]
        span = folded(RADIUS, width)
        for plane in range(span):
            face[RADIUS + plane] = fold(
                [side[start + plane + span * turn] for turn in range(count)], width
            )
    for face, start in (
        (x_even, (rows - RADIUS) * (1 - x_parity)),
        (x_odd, (rows - RADIUS) * x_parity),
    ):
        start = pl.multiple_of(start, RADIUS)
        face[pl.ds(0, depth)] = main[:, pl.ds(start, RADIUS), :]
        span = folded(depth, width)
        for plane in range(span):
            face[depth + plane] = fold(
                [side[plane + span * turn, pl.ds(start, RADIUS), :] for turn in range(count)],
                width,
            )


def strip_unpack_kernel(
    ids, even, odd, wave, wave_side, older_side, stiff_side, z_even, z_odd, x_even, x_odd
):
    parity = ids[2] & 1
    quarters = LANES // STRIP
    quarter = lane_of(wave.shape[1:]) // STRIP
    from_even = quarter == 3 * parity
    from_odd = quarter == 3 * (1 - parity)
    chunks = wave.shape[0] // quarters
    for number, side in enumerate((wave_side, older_side, stiff_side)):
        for chunk in range(chunks):
            one = even[1 - parity, number * chunks + chunk]
            two = odd[number * chunks + chunk]
            for turn in range(quarters):
                back = (LANES - STRIP * turn) % LANES
                first = pltpu.roll(one, back, 1) if back else one
                second = pltpu.roll(two, back, 1) if back else two
                side[quarters * chunk + turn] = jnp.where(
                    from_even, first, jnp.where(from_odd, second, 0.0)
                )
    write_faces(STRIP, ids, wave, wave_side, z_even, z_odd, x_even, x_odd)


def fill(width, ids, z_even, z_odd, x_even, x_odd, z_halo, x_halo):
    z_parity, x_parity = ids[0] & 1, ids[1] & 1
    depth = x_halo.shape[1]
    count = folds(width)
    pair = z_even.at[1 - z_parity]
    for face, start in ((pair, RADIUS * (1 - z_parity)), (z_odd, RADIUS * z_parity)):
        z_halo[0, pl.ds(start, RADIUS)] = face[pl.ds(0, RADIUS)]
        span = folded(RADIUS, width)
        for plane in range(span):
            both = face[RADIUS + plane]
            for turn in range(count):
                z_halo[1, start + plane + span * turn] = unfold(both, turn, width)
    for face, start in ((x_even, RADIUS * (1 - x_parity)), (x_odd, RADIUS * x_parity)):
        start = pl.multiple_of(start, RADIUS)
        x_halo[0, :, pl.ds(start, RADIUS), :] = face[pl.ds(0, depth)]
        span = folded(depth, width)
        for plane in range(span):
            both = face[depth + plane]
            for turn in range(count):
                x_halo[1, plane + span * turn, pl.ds(start, RADIUS), :] = unfold(both, turn, width)


def own_kernel(last, wave, side, band_high, band_low, *rest):
    *outs, y_terms = rest
    depth, rows, _ = wave.shape
    if last:
        outs, kept = outs[:1], outs[1]
        kept[...] = wave[...]
    width = LANES * len(outs)
    both = jnp.concatenate(
        [wave[...].reshape(depth * rows, LANES), side[...].reshape(depth * rows, LANES)], axis=1
    )
    high = both.astype(BF16)
    low = (both - high.astype(F32)).astype(BF16)
    matrix, remainder = band_high[:, :width], band_low[:, :width]
    y_terms[:, :width] = (
        jnp.dot(high, matrix, preferred_element_type=F32)
        + jnp.dot(low, matrix, preferred_element_type=F32)
        + jnp.dot(high, remainder, preferred_element_type=F32)
    )
    beyond = jnp.zeros((RADIUS, LANES), F32)
    for z in range(depth):
        for part, (field, out) in enumerate(zip((wave, side), outs)):
            column = jnp.concatenate([beyond, field[z], beyond], axis=0)
            turned = [None] + [
                pltpu.roll(column, rows + 2 * RADIUS - offset, 0) for offset in range(1, RADIUS)
            ]
            total = y_terms[z * rows : (z + 1) * rows, part * LANES : (part + 1) * LANES]
            for offset in range(1, RADIUS + 1):
                if offset < RADIUS:
                    near = turned[offset][RADIUS : RADIUS + rows] + turned[RADIUS - offset][:rows]
                else:
                    near = column[2 * RADIUS :] + column[:rows]
                if z + offset < depth:
                    near = near + field[z + offset]
                if z >= offset:
                    near = near + field[z - offset]
                total = total + WEIGHTS[offset - 1] * near
            out[z] = total


def advance(step, shot, ids, wave, side, older, older_side, stiff, stiff_side, forward, image_in,
            planes, own, own_side, fresh, fresh_side, image, z_halo, x_halo, done=None):
    depth, rows, _ = wave.shape
    last = step == STEPS - 1
    line = lax.broadcasted_iota(jnp.int32, (RADIUS, LANES), 0)
    before_tile = [
        jnp.where(line < offset, WEIGHTS[offset - 1], 0.0) for offset in range(1, RADIUS + 1)
    ]
    behind_tile = [
        jnp.where(line >= RADIUS - offset, WEIGHTS[offset - 1], 0.0)
        for offset in range(1, RADIUS + 1)
    ]
    between = jnp.zeros((rows - 2 * RADIUS, LANES), F32)

    def one(z, part, partial, field, previous, speed, target):
        total = partial[z]
        first = last_rows = None
        head, tail = x_halo[part, z, :RADIUS], x_halo[part, z, RADIUS:]
        for offset in range(1, RADIUS + 1):
            if z < offset:
                total = total + WEIGHTS[offset - 1] * z_halo[part, RADIUS + z - offset]
            if z + offset >= depth:
                total = total + WEIGHTS[offset - 1] * z_halo[part, RADIUS + z + offset - depth]
            above = pltpu.roll(head, offset, 0) if offset < RADIUS else head
            below = pltpu.roll(tail, RADIUS - offset, 0) if offset < RADIUS else tail
            above = before_tile[offset - 1] * above
            below = behind_tile[offset - 1] * below
            first = above if first is None else first + above
            last_rows = below if last_rows is None else last_rows + below
        total = total + jnp.concatenate([first, between, last_rows], axis=0)
        if z == 0:
            total = total + planes[STEPS * part + step]
        value = 2.0 * field[z] - previous[z] + speed[z] * total
        target[z] = value
        return value

    for z in range(depth):
        value = one(z, 0, own, wave, older, stiff, fresh)
        product = forward[step, z].astype(F32) * value
        if step:
            product = product + image_in[z]
        if last:
            product = product * muting(ids, *shot, z, depth, rows)
        image[z] = product
        if done is not None:
            done(z)
        if not last:
            one(z, 1, own_side, side, older_side, stiff_side, fresh_side)


def muting(ids, shot_x, shot_y, z, depth, rows):
    gap_z = (ids[0] * depth + z).astype(F32)
    gap_x = (
        ids[1] * rows + lax.broadcasted_iota(jnp.int32, (rows, LANES), 0) - shot_x
    ).astype(F32)
    gap_y = (ids[2] * LANES + lane_of((rows, LANES)) - shot_y).astype(F32)
    distance = gap_z * gap_z + gap_x * gap_x + gap_y * gap_y
    return jnp.minimum(1.0, distance / 576.0)


def step_kernel(step, total_y, ids, x_odd_in, x_even_in, z_odd_in, z_even_in, wave, side, older,
                older_side, stiff, stiff_side, forward, own, *rest):
    last = step == STEPS - 1
    own_side = image_in = None
    if not last:
        own_side, *rest = rest
    if step:
        planes, image_in, *rest = rest
    else:
        planes, *rest = rest
        face = z_even_in.shape[1] - 2 * STEPS
        both = z_even_in[0, pl.ds(face, 2 * STEPS)] + z_even_in[1, pl.ds(face, 2 * STEPS)]
        planes[...] = jnp.where(ids[0] == 0, both, 0.0)
    shot = done = None
    copies = []
    if last:
        (source, image_out, wave_out, z_halo, x_halo, image, fresh, sems) = rest
        fresh_side = None
        shot = (lax.div(source[0], total_y), lax.rem(source[0], total_y))

        def done(z):
            if (z + 1) % CHUNK:
                return
            chunk = pl.ds(z + 1 - CHUNK, CHUNK)
            for number, (held, out) in enumerate(((image, image_out), (fresh, wave_out))):
                copies.append(
                    pltpu.make_async_copy(
                        held.at[chunk], out.at[chunk], sems.at[number, z // CHUNK]
                    )
                )
                copies[-1].start()

    else:
        image, fresh, fresh_side, z_even, z_odd, x_even, x_odd, z_halo, x_halo = rest
    fill(strip_width(step), ids, z_even_in, z_odd_in, x_even_in, x_odd_in, z_halo, x_halo)
    advance(step, shot, ids, wave, side, older, older_side, stiff, stiff_side, forward, image_in,
            planes, own, own_side, fresh, fresh_side, image, z_halo, x_halo, done)
    for copy in copies:
        copy.wait()
    if not last:
        write_faces(strip_width(step + 1), ids, fresh, fresh_side, z_even, z_odd, x_even, x_odd)


def swap(block, axis, parity):
    count = lax.axis_size(axis)
    pairs = []
    for left in range(parity, count - 1, 2):
        pairs += [(left, left + 1), (left + 1, left)]
    return lax.ppermute(block, axis, pairs)


def pair_gather(block, axis, parity):
    count = lax.axis_size(axis)
    groups = [
        [(2 * pair + parity) % count, (2 * pair + parity + 1) % count]
        for pair in range(count // 2)
    ]
    return lax.all_gather(block, axis, axis=0, tiled=False, axis_index_groups=groups)


def exchange(faces):
    z_even, z_odd, x_even, x_odd = faces
    z_odd = swap(z_odd, "gz", 1)
    x_even = swap(x_even, "gx", 0)
    x_odd = swap(x_odd, "gx", 1)
    z_even = pair_gather(z_even, "gz", 0)
    return z_even, z_odd, x_even, x_odd


def on_device(
    stiffness, older_wave, wave_now, forward_wave, residuals, owners, receivers, source_cell
):
    depth, rows, cols = wave_now.shape
    span_x, span_y, span_z = (lax.axis_size(axis) for axis in ("gx", "gy", "gz"))
    tiles = span_x * span_y
    ids = jnp.stack(
        [
            lax.axis_index("gz"),
            lax.axis_index("gx"),
            lax.axis_index("gy"),
        ]
    ).astype(jnp.int32)
    band_high, band_low = (jnp.asarray(part) for part in band())
    block = shaped(depth, rows, LANES)

    def faces_out(step):
        width = strip_width(step)
        z_face = shaped(RADIUS + folded(RADIUS, width), rows, LANES)
        x_face = shaped(depth + folded(depth, width), RADIUS, LANES)
        return [z_face, z_face, x_face, x_face]

    strips = shaped(3 * depth * STRIP // LANES, rows, LANES)
    packets, even, odd = call(
        functools.partial(prepare_kernel, span_y, tiles),
        [shaped(tiles, LANES), strips, strips],
        [ids, residuals, owners.reshape(1, -1), receivers.reshape(1, -1), wave_now, older_wave,
         stiffness],
        in_specs=[smem()] + [pl.BlockSpec()] * 6,
        grant=60,
    )
    packets = lax.all_to_all(packets, ("gx", "gy"), 0, 0, tiled=True)
    odd = swap(odd, "gy", 1)
    even = pair_gather(even, "gy", 0)
    side, older_side, stiff_side, *faces = call(
        strip_unpack_kernel,
        [block] * 3 + faces_out(0),
        [ids, even, odd, wave_now],
    )
    packets, faces = lax.optimization_barrier((packets, faces))
    cores = 2
    packets = [packets] + [
        lax.ppermute(packets, "gz", [(chip + core, core) for core in range(cores)])
        for chip in range(cores, span_z, cores)
    ]
    face = faces[0].shape[0]
    faces[0] = call(
        functools.partial(plane_kernel, face, rows),
        shaped(face + 2 * STEPS, rows, LANES),
        [ids, faces[0], *packets],
        scratch=[pltpu.VMEM((LANES, span_z // cores * tiles), F32)],
    )

    scratch = [
        pltpu.VMEM((2, 2 * RADIUS, rows, LANES), F32),
        pltpu.VMEM((2, depth, 2 * RADIUS, LANES), F32),
    ]
    wave, older = wave_now, older_wave
    image = None
    for step in range(STEPS):
        last = step == STEPS - 1
        own = call(
            functools.partial(own_kernel, last),
            [block, block],
            [wave, side, band_high, band_low],
            scratch=[pltpu.VMEM((depth * rows, 2 * LANES), F32)],
            in_specs=[vmem()] * 4,
        )
        if last:
            *own, last_older = own
        faces = exchange(faces)
        ins = [ids, *faces[::-1], wave, side, older, older_side, stiffness, stiff_side, forward_wave,
               *own]
        outs = [block, block]
        if step:
            ins += [planes, image]
        else:
            outs = [shaped(2 * STEPS, rows, LANES)] + outs
        if not last:
            outs += [block] + faces_out(step + 1)
        room, in_specs, out_specs = scratch, None, None
        if last:
            ins.append(source_cell)
            in_specs = [smem()] + [vmem()] * (len(ins) - 2) + [smem()]
            out_specs = [pl.BlockSpec(memory_space=pl.ANY)] * 2
            held = pltpu.VMEM((depth, rows, LANES), F32)
            room = scratch + [held, held, pltpu.SemaphoreType.DMA((2, depth // CHUNK))]
        rest = call(
            functools.partial(step_kernel, step, cols * span_y), outs, ins, room, in_specs,
            out_specs=out_specs,
        )
        if not step:
            planes, *rest = rest
        image, fresh, *rest = rest
        older, wave = wave, fresh
        if not last:
            older_side, side = side, rest[0]
            faces = rest[1:]
    return image, last_older, wave


def solution(mesh):
    in_specs = (
        P("gz", "gx", "gy"),
        P("gz", "gx", "gy"),
        P("gz", "gx", "gy"),
        P(None, "gz", "gx", "gy"),
        P(None, ("gx", "gy", "gz")),
        P(("gx", "gy", "gz"), None),
        P(("gx", "gy", "gz")),
        P(),
    )
    out_specs = (P("gz", "gx", "gy"), P("gz", "gx", "gy"), P("gz", "gx", "gy"))
    return jax.shard_map(
        on_device, mesh=mesh, in_specs=in_specs, out_specs=out_specs, check_vma=False
    )
```

```python
import functools
import math

import jax
import jax.numpy as jnp
import numpy as np
from jax import lax
from jax.experimental import pallas as pl
from jax.experimental.pallas import tpu as pltpu
from jax.sharding import PartitionSpec as P

STEPS = 4
RADIUS = 8
LANES = 128
STRIP = 32
CAP = 8
CHUNK = 4
SLOTS = 3 * CAP
F32 = jnp.float32
BF16 = jnp.bfloat16


def stencil_weights():
    window = [math.cos(math.pi * offset / 20.0) for offset in range(1, RADIUS + 1)]
    alternating = sum(
        ((-1.0) ** (offset + 1) * window[offset - 1] for offset in range(1, RADIUS + 1))
    )
    factor = 1.0 / (2.0 * alternating)
    weights = []
    for offset in range(1, RADIUS + 1):
        weights.append(
            factor * 2.0 * (-1.0) ** (offset + 1) * window[offset - 1] / (offset * offset)
        )
    return (weights, -2.0 * sum(weights))


WEIGHTS, CENTER = stencil_weights()


def band():
    size = 2 * LANES
    matrix = np.zeros((size, size), np.float64)
    for column in range(size):
        matrix[column, column] = 3.0 * CENTER
        for offset in range(1, RADIUS + 1):
            matrix[(column + offset) % size, column] = WEIGHTS[offset - 1]
            matrix[(column - offset) % size, column] = WEIGHTS[offset - 1]
    matrix = matrix.astype(np.float32)
    high = matrix.astype(jnp.bfloat16)
    low = (matrix - high.astype(np.float32)).astype(jnp.bfloat16)
    return high, low


def lane_of(shape):
    return lax.broadcasted_iota(jnp.int32, shape, len(shape) - 1)


def vmem():
    return pl.BlockSpec(memory_space=pltpu.VMEM)


def smem():
    return pl.BlockSpec(memory_space=pltpu.SMEM)


def call(body, outs, ins, scratch=(), in_specs=None, grant=32, out_specs=None):
    return pl.pallas_call(
        body,
        out_shape=outs,
        in_specs=in_specs or [vmem()] * len(ins),
        out_specs=out_specs or jax.tree.map(lambda _: vmem(), outs),
        scratch_shapes=list(scratch),
        compiler_params=pltpu.CompilerParams(vmem_limit_bytes=grant * 1024 * 1024),
        cost_estimate=pl.CostEstimate(flops=1_000_000, bytes_accessed=2_000_000, transcendentals=0),
    )(*ins)


def shaped(*shape):
    return jax.ShapeDtypeStruct(shape, F32)


def split3(value):
    high = value.astype(BF16)
    rest = value - high.astype(F32)
    middle = rest.astype(BF16)
    return high, middle, (rest - middle.astype(F32)).astype(BF16)


def dot_nt(left, right):
    return lax.dot_general(left, right, (((1,), (1,)), ((), ())), preferred_element_type=F32)


def place():
    return tuple(lax.axis_index(axis) for axis in ("gz", "gx", "gy"))


def prepare_kernel(span_y, tiles, residuals, owners, cells, wave, older, stiff, packets,
                   even, odd):
    pack_slots(span_y, tiles, residuals, owners, cells, packets)
    pack_strips(place(), wave, older, stiff, even, odd)


def pack_slots(span_y, tiles, residuals, owner_row, cell_row, out):
    rows = residuals.shape[1]
    owner = owner_row[...]
    owner_column = jnp.transpose(jnp.broadcast_to(owner.astype(F32), (rows, rows)))
    earlier = (owner_column.astype(jnp.int32) == owner) & (
        lax.broadcasted_iota(jnp.int32, (rows, rows), 0)
        < lax.broadcasted_iota(jnp.int32, (rows, rows), 1)
    )
    rank = jnp.sum(earlier.astype(jnp.int32), axis=0, keepdims=True)
    cell = cell_row[...]
    along = cell & (LANES - 1)
    fields = [residuals[pl.ds(field, 1), :] for field in range(STEPS)] + [cell.astype(F32)]
    stacked = jnp.concatenate(
        [jnp.broadcast_to(field, (SLOTS, rows)) for field in fields]
        + [jnp.zeros((LANES - SLOTS * len(fields), rows), F32)],
        axis=0,
    )
    line = lax.broadcasted_iota(jnp.int32, (LANES, rows), 0)
    slot = line - SLOTS * (line // SLOTS)
    tile = lax.broadcasted_iota(jnp.int32, (tiles, rows), 0)
    place = tile & (span_y - 1)
    total = jnp.zeros((tiles, LANES), F32)
    for group in range(3):
        named = owner == tile + (group - 1)
        wanted = slot == rank + CAP * group
        if group == 0:
            named = named & (place != 0)
            wanted = wanted & (along >= LANES - STRIP)
        if group == 2:
            named = named & (place != span_y - 1)
            wanted = wanted & (along < STRIP)
        chosen = named.astype(F32).astype(BF16)
        for part in split3(jnp.where(wanted, stacked, 0.0)):
            total = total + dot_nt(chosen, part)
    out[...] = total


def plane_kernel(face, rows, z_even, *refs):
    *packets, out, turned = refs
    out[pl.ds(0, face)] = z_even[...]
    out[pl.ds(face, 2 * STEPS)] = jnp.zeros((2 * STEPS, rows, LANES), F32)

    @pl.when(place()[0] < 2)
    def _():
        count = turned.shape[1]
        share = count // len(packets)
        for number, packet in enumerate(packets):
            turned[:, share * number : share * (number + 1)] = jnp.transpose(packet[...])
        line = lax.broadcasted_iota(jnp.int32, (rows, count), 0)
        spot = lax.broadcasted_iota(jnp.int32, (LANES, count), 0)

        def product(slot):
            cell = turned[pl.ds(SLOTS * STEPS + slot, 1), :].astype(jnp.int32)
            hit = (cell >> 7) == line
            highs, lows = [], []
            for step in range(STEPS):
                value = turned[pl.ds(SLOTS * step + slot, 1), :]
                high = value.astype(BF16).astype(F32)
                highs.append(jnp.where(hit, high, 0.0))
                lows.append(jnp.where(hit, value - high, 0.0))
            left = jnp.concatenate(highs + lows, axis=0).astype(BF16)
            right = jnp.where((cell & (LANES - 1)) == spot, 1.0, 0.0).astype(BF16)
            both = dot_nt(left, right)
            return both[: STEPS * rows] + both[STEPS * rows :]

        for part, groups in enumerate(((1,), (0, 2))):
            total = None
            for slot in [CAP * group + rank for group in groups for rank in range(CAP)]:
                total = product(slot) if total is None else total + product(slot)
            out[pl.ds(face + STEPS * part, STEPS)] = total.reshape(STEPS, rows, LANES)


def pack_strips(ids, wave, older, stiff, even, odd):
    parity = ids[2] & 1
    quarter = lane_of(wave.shape[1:]) // STRIP
    low, high = quarter == 0, quarter == 3
    quarters = LANES // STRIP
    for number, field in enumerate((wave, older, stiff)):
        for chunk in range(field.shape[0] // quarters):
            lows = highs = None
            for turn in range(quarters):
                value = field[quarters * chunk + turn]
                one = jnp.where(low, value, 0.0)
                two = jnp.where(high, value, 0.0)
                if turn:
                    one = pltpu.roll(one, STRIP * turn, 1)
                    two = pltpu.roll(two, STRIP * turn, 1)
                lows = one if lows is None else lows + one
                highs = two if highs is None else highs + two
            place = number * (field.shape[0] // quarters) + chunk
            even[place] = jnp.where(parity == 0, highs, lows)
            odd[place] = jnp.where(parity == 0, lows, highs)


def strip_width(step):
    return {0: STRIP, 1: STRIP // 2, 2: STRIP // 4}.get(step, 0)


def folds(width):
    return LANES // (2 * width) if width else 0


def folded(length, width):
    return length // folds(width) if width else 0


def kept_lanes(shape, width):
    lane = lane_of(shape)
    return (lane < width) | (lane >= LANES - width)


def fold(pieces, width):
    total = None
    for turn, piece in enumerate(pieces):
        piece = jnp.where(kept_lanes(piece.shape, width), piece, 0.0)
        if turn:
            piece = pltpu.roll(piece, 2 * width * turn, 1)
        total = piece if total is None else total + piece
    return total


def unfold(both, turn, width):
    if turn:
        both = pltpu.roll(both, LANES - 2 * width * turn, 1)
    return jnp.where(kept_lanes(both.shape, width), both, 0.0)


def write_faces(width, ids, main, side, z_even, z_odd, x_even, x_odd):
    z_parity, x_parity = ids[0] & 1, ids[1] & 1
    depth, rows, _ = main.shape
    count = folds(width)
    for face, start in (
        (z_even, (depth - RADIUS) * (1 - z_parity)),
        (z_odd, (depth - RADIUS) * z_parity),
    ):
        face[pl.ds(0, RADIUS)] = main[pl.ds(start, RADIUS)]
        span = folded(RADIUS, width)
        for plane in range(span):
            face[RADIUS + plane] = fold(
                [side[start + plane + span * turn] for turn in range(count)], width
            )
    for face, start in (
        (x_even, (rows - RADIUS) * (1 - x_parity)),
        (x_odd, (rows - RADIUS) * x_parity),
    ):
        start = pl.multiple_of(start, RADIUS)
        face[pl.ds(0, depth)] = main[:, pl.ds(start, RADIUS), :]
        span = folded(depth, width)
        for plane in range(span):
            face[depth + plane] = fold(
                [side[plane + span * turn, pl.ds(start, RADIUS), :] for turn in range(count)],
                width,
            )


def strip_unpack_kernel(
    even, odd, wave, wave_side, older_side, stiff_side, z_even, z_odd, x_even, x_odd
):
    ids = place()
    parity = ids[2] & 1
    quarters = LANES // STRIP
    quarter = lane_of(wave.shape[1:]) // STRIP
    from_even = quarter == 3 * parity
    from_odd = quarter == 3 * (1 - parity)
    chunks = wave.shape[0] // quarters
    for number, side in enumerate((wave_side, older_side, stiff_side)):
        for chunk in range(chunks):
            one = even[1 - parity, number * chunks + chunk]
            two = odd[number * chunks + chunk]
            for turn in range(quarters):
                back = (LANES - STRIP * turn) % LANES
                first = pltpu.roll(one, back, 1) if back else one
                second = pltpu.roll(two, back, 1) if back else two
                side[quarters * chunk + turn] = jnp.where(
                    from_even, first, jnp.where(from_odd, second, 0.0)
                )
    write_faces(STRIP, ids, wave, wave_side, z_even, z_odd, x_even, x_odd)


def fill(width, ids, z_even, z_odd, x_even, x_odd, z_halo, x_halo):
    z_parity, x_parity = ids[0] & 1, ids[1] & 1
    depth = x_halo.shape[1]
    count = folds(width)
    pair = z_even.at[1 - z_parity]
    for face, start in ((pair, RADIUS * (1 - z_parity)), (z_odd, RADIUS * z_parity)):
        z_halo[0, pl.ds(start, RADIUS)] = face[pl.ds(0, RADIUS)]
        span = folded(RADIUS, width)
        for plane in range(span):
            both = face[RADIUS + plane]
            for turn in range(count):
                z_halo[1, start + plane + span * turn] = unfold(both, turn, width)
    for face, start in ((x_even, RADIUS * (1 - x_parity)), (x_odd, RADIUS * x_parity)):
        start = pl.multiple_of(start, RADIUS)
        x_halo[0, :, pl.ds(start, RADIUS), :] = face[pl.ds(0, depth)]
        span = folded(depth, width)
        for plane in range(span):
            both = face[depth + plane]
            for turn in range(count):
                x_halo[1, plane + span * turn, pl.ds(start, RADIUS), :] = unfold(both, turn, width)


def own_kernel(last, wave, side, band_high, band_low, *rest):
    *outs, y_terms = rest
    depth, rows, _ = wave.shape
    if last:
        outs, kept = outs[:1], outs[1]
        kept[...] = wave[...]
    width = LANES * len(outs)
    both = jnp.concatenate(
        [wave[...].reshape(depth * rows, LANES), side[...].reshape(depth * rows, LANES)], axis=1
    )
    high = both.astype(BF16)
    low = (both - high.astype(F32)).astype(BF16)
    matrix, remainder = band_high[:, :width], band_low[:, :width]
    y_terms[:, :width] = (
        jnp.dot(high, matrix, preferred_element_type=F32)
        + jnp.dot(low, matrix, preferred_element_type=F32)
        + jnp.dot(high, remainder, preferred_element_type=F32)
    )
    beyond = jnp.zeros((RADIUS, LANES), F32)
    for z in range(depth):
        for part, (field, out) in enumerate(zip((wave, side), outs)):
            column = jnp.concatenate([beyond, field[z], beyond], axis=0)
            turned = [None] + [
                pltpu.roll(column, rows + 2 * RADIUS - offset, 0) for offset in range(1, RADIUS)
            ]
            total = y_terms[z * rows : (z + 1) * rows, part * LANES : (part + 1) * LANES]
            for offset in range(1, RADIUS + 1):
                if offset < RADIUS:
                    near = turned[offset][RADIUS : RADIUS + rows] + turned[RADIUS - offset][:rows]
                else:
                    near = column[2 * RADIUS :] + column[:rows]
                if z + offset < depth:
                    near = near + field[z + offset]
                if z >= offset:
                    near = near + field[z - offset]
                total = total + WEIGHTS[offset - 1] * near
            out[z] = total


def advance(step, shot, ids, wave, side, older, older_side, stiff, stiff_side, forward, image_in,
            planes, own, own_side, fresh, fresh_side, image, z_halo, x_halo, done=None):
    depth, rows, _ = wave.shape
    last = step == STEPS - 1
    line = lax.broadcasted_iota(jnp.int32, (RADIUS, LANES), 0)
    before_tile = [
        jnp.where(line < offset, WEIGHTS[offset - 1], 0.0) for offset in range(1, RADIUS + 1)
    ]
    behind_tile = [
        jnp.where(line >= RADIUS - offset, WEIGHTS[offset - 1], 0.0)
        for offset in range(1, RADIUS + 1)
    ]
    between = jnp.zeros((rows - 2 * RADIUS, LANES), F32)

    def one(z, part, partial, field, previous, speed, target):
        total = partial[z]
        first = last_rows = None
        head, tail = x_halo[part, z, :RADIUS], x_halo[part, z, RADIUS:]
        for offset in range(1, RADIUS + 1):
            if z < offset:
                total = total + WEIGHTS[offset - 1] * z_halo[part, RADIUS + z - offset]
            if z + offset >= depth:
                total = total + WEIGHTS[offset - 1] * z_halo[part, RADIUS + z + offset - depth]
            above = pltpu.roll(head, offset, 0) if offset < RADIUS else head
            below = pltpu.roll(tail, RADIUS - offset, 0) if offset < RADIUS else tail
            above = before_tile[offset - 1] * above
            below = behind_tile[offset - 1] * below
            first = above if first is None else first + above
            last_rows = below if last_rows is None else last_rows + below
        total = total + jnp.concatenate([first, between, last_rows], axis=0)
        if z == 0:
            total = total + planes[STEPS * part + step]
        value = 2.0 * field[z] - previous[z] + speed[z] * total
        target[z] = value
        return value

    for z in range(depth):
        value = one(z, 0, own, wave, older, stiff, fresh)
        product = forward[step, z].astype(F32) * value
        if step:
            product = product + image_in[z]
        if last:
            product = product * muting(ids, *shot, z, depth, rows)
        image[z] = product
        if done is not None:
            done(z)
        if not last:
            one(z, 1, own_side, side, older_side, stiff_side, fresh_side)


def muting(ids, shot_x, shot_y, z, depth, rows):
    gap_z = (ids[0] * depth + z).astype(F32)
    gap_x = (
        ids[1] * rows + lax.broadcasted_iota(jnp.int32, (rows, LANES), 0) - shot_x
    ).astype(F32)
    gap_y = (ids[2] * LANES + lane_of((rows, LANES)) - shot_y).astype(F32)
    distance = gap_z * gap_z + gap_x * gap_x + gap_y * gap_y
    return jnp.minimum(1.0, distance / 576.0)


def step_kernel(step, total_y, x_odd_in, x_even_in, z_odd_in, z_even_in, wave, side, older,
                older_side, stiff, stiff_side, forward, own, *rest):
    ids = place()
    last = step == STEPS - 1
    own_side = image_in = None
    if not last:
        own_side, *rest = rest
    if step:
        planes, image_in, *rest = rest
    else:
        planes, *rest = rest
        face = z_even_in.shape[1] - 2 * STEPS
        both = z_even_in[0, pl.ds(face, 2 * STEPS)] + z_even_in[1, pl.ds(face, 2 * STEPS)]
        planes[...] = jnp.where(ids[0] == 0, both, 0.0)
    shot = done = None
    copies = []
    if last:
        (source, image_out, wave_out, z_halo, x_halo, image, fresh, sems) = rest
        fresh_side = None
        shot = (lax.div(source[0], total_y), lax.rem(source[0], total_y))

        def done(z):
            if (z + 1) % CHUNK:
                return
            chunk = pl.ds(z + 1 - CHUNK, CHUNK)
            for number, (held, out) in enumerate(((image, image_out), (fresh, wave_out))):
                copies.append(
                    pltpu.make_async_copy(
                        held.at[chunk], out.at[chunk], sems.at[number, z // CHUNK]
                    )
                )
                copies[-1].start()

    else:
        image, fresh, fresh_side, z_even, z_odd, x_even, x_odd, z_halo, x_halo = rest
    fill(strip_width(step), ids, z_even_in, z_odd_in, x_even_in, x_odd_in, z_halo, x_halo)
    advance(step, shot, ids, wave, side, older, older_side, stiff, stiff_side, forward, image_in,
            planes, own, own_side, fresh, fresh_side, image, z_halo, x_halo, done)
    for copy in copies:
        copy.wait()
    if not last:
        write_faces(strip_width(step + 1), ids, fresh, fresh_side, z_even, z_odd, x_even, x_odd)


def swap(block, axis, parity):
    count = lax.axis_size(axis)
    pairs = []
    for left in range(parity, count - 1, 2):
        pairs += [(left, left + 1), (left + 1, left)]
    return lax.ppermute(block, axis, pairs)


def pair_gather(block, axis, parity):
    count = lax.axis_size(axis)
    groups = [
        [(2 * pair + parity) % count, (2 * pair + parity + 1) % count]
        for pair in range(count // 2)
    ]
    return lax.all_gather(block, axis, axis=0, tiled=False, axis_index_groups=groups)


def exchange(faces):
    z_even, z_odd, x_even, x_odd = faces
    z_odd = swap(z_odd, "gz", 1)
    x_even = swap(x_even, "gx", 0)
    x_odd = swap(x_odd, "gx", 1)
    z_even = pair_gather(z_even, "gz", 0)
    return z_even, z_odd, x_even, x_odd


def on_device(
    stiffness, older_wave, wave_now, forward_wave, residuals, owners, receivers, source_cell
):
    depth, rows, cols = wave_now.shape
    span_x, span_y, span_z = (lax.axis_size(axis) for axis in ("gx", "gy", "gz"))
    tiles = span_x * span_y
    band_high, band_low = (jnp.asarray(part) for part in band())
    block = shaped(depth, rows, LANES)

    def faces_out(step):
        width = strip_width(step)
        z_face = shaped(RADIUS + folded(RADIUS, width), rows, LANES)
        x_face = shaped(depth + folded(depth, width), RADIUS, LANES)
        return [z_face, z_face, x_face, x_face]

    strips = shaped(3 * depth * STRIP // LANES, rows, LANES)
    packets, even, odd = call(
        functools.partial(prepare_kernel, span_y, tiles),
        [shaped(tiles, LANES), strips, strips],
        [residuals, owners.reshape(1, -1), receivers.reshape(1, -1), wave_now, older_wave,
         stiffness],
        in_specs=[pl.BlockSpec()] * 6,
        grant=60,
    )
    packets = lax.all_to_all(packets, ("gx", "gy"), 0, 0, tiled=True)
    odd = swap(odd, "gy", 1)
    even = pair_gather(even, "gy", 0)
    side, older_side, stiff_side, *faces = call(
        strip_unpack_kernel,
        [block] * 3 + faces_out(0),
        [even, odd, wave_now],
    )
    packets, faces = lax.optimization_barrier((packets, faces))
    cores = 2
    packets = [packets] + [
        lax.ppermute(packets, "gz", [(chip + core, core) for core in range(cores)])
        for chip in range(cores, span_z, cores)
    ]
    face = faces[0].shape[0]
    faces[0] = call(
        functools.partial(plane_kernel, face, rows),
        shaped(face + 2 * STEPS, rows, LANES),
        [faces[0], *packets],
        scratch=[pltpu.VMEM((LANES, span_z // cores * tiles), F32)],
    )

    scratch = [
        pltpu.VMEM((2, 2 * RADIUS, rows, LANES), F32),
        pltpu.VMEM((2, depth, 2 * RADIUS, LANES), F32),
    ]
    wave, older = wave_now, older_wave
    image = None
    for step in range(STEPS):
        last = step == STEPS - 1
        own = call(
            functools.partial(own_kernel, last),
            [block, block],
            [wave, side, band_high, band_low],
            scratch=[pltpu.VMEM((depth * rows, 2 * LANES), F32)],
        )
        if last:
            *own, last_older = own
        faces = exchange(faces)
        ins = [*faces[::-1], wave, side, older, older_side, stiffness, stiff_side, forward_wave,
               *own]
        outs = [block, block]
        if step:
            ins += [planes, image]
        else:
            outs = [shaped(2 * STEPS, rows, LANES)] + outs
        if not last:
            outs += [block] + faces_out(step + 1)
        room, in_specs, out_specs = scratch, None, None
        if last:
            ins.append(source_cell)
            in_specs = [vmem()] * (len(ins) - 1) + [smem()]
            out_specs = [pl.BlockSpec(memory_space=pl.ANY)] * 2
            held = pltpu.VMEM((depth, rows, LANES), F32)
            room = scratch + [held, held, pltpu.SemaphoreType.DMA((2, depth // CHUNK))]
        rest = call(
            functools.partial(step_kernel, step, cols * span_y), outs, ins, room, in_specs,
            out_specs=out_specs,
        )
        if not step:
            planes, *rest = rest
        image, fresh, *rest = rest
        older, wave = wave, fresh
        if not last:
            older_side, side = side, rest[0]
            faces = rest[1:]
    return image, last_older, wave


def solution(mesh):
    in_specs = (
        P("gz", "gx", "gy"),
        P("gz", "gx", "gy"),
        P("gz", "gx", "gy"),
        P(None, "gz", "gx", "gy"),
        P(None, ("gx", "gy", "gz")),
        P(("gx", "gy", "gz"), None),
        P(("gx", "gy", "gz")),
        P(),
    )
    out_specs = (P("gz", "gx", "gy"), P("gz", "gx", "gy"), P("gz", "gx", "gy"))
    return jax.shard_map(
        on_device, mesh=mesh, in_specs=in_specs, out_specs=out_specs, check_vma=False
    )
```

```python
import functools
import math

import jax
import jax.numpy as jnp
import numpy as np
from jax import lax
from jax.experimental import pallas as pl
from jax.experimental.pallas import tpu as pltpu
from jax.sharding import PartitionSpec as P

STEPS = 4
RADIUS = 8
LANES = 128
STRIP = 32
CAP = 8
CHUNK = 4
SLOTS = 3 * CAP
F32 = jnp.float32
BF16 = jnp.bfloat16


def stencil_weights():
    window = [math.cos(math.pi * offset / 20.0) for offset in range(1, RADIUS + 1)]
    alternating = sum(
        ((-1.0) ** (offset + 1) * window[offset - 1] for offset in range(1, RADIUS + 1))
    )
    factor = 1.0 / (2.0 * alternating)
    weights = []
    for offset in range(1, RADIUS + 1):
        weights.append(
            factor * 2.0 * (-1.0) ** (offset + 1) * window[offset - 1] / (offset * offset)
        )
    return (weights, -2.0 * sum(weights))


WEIGHTS, CENTER = stencil_weights()


def band():
    size = 2 * LANES
    matrix = np.zeros((size, size), np.float64)
    for column in range(size):
        matrix[column, column] = 3.0 * CENTER
        for offset in range(1, RADIUS + 1):
            matrix[(column + offset) % size, column] = WEIGHTS[offset - 1]
            matrix[(column - offset) % size, column] = WEIGHTS[offset - 1]
    matrix = matrix.astype(np.float32)
    high = matrix.astype(jnp.bfloat16)
    low = (matrix - high.astype(np.float32)).astype(jnp.bfloat16)
    return high, low


def lane_of(shape):
    return lax.broadcasted_iota(jnp.int32, shape, len(shape) - 1)


def vmem():
    return pl.BlockSpec(memory_space=pltpu.VMEM)


def call(body, outs, ins, scratch=(), in_specs=None, grant=32, out_specs=None):
    return pl.pallas_call(
        body,
        out_shape=outs,
        in_specs=in_specs or [vmem()] * len(ins),
        out_specs=out_specs or jax.tree.map(lambda _: vmem(), outs),
        scratch_shapes=list(scratch),
        compiler_params=pltpu.CompilerParams(vmem_limit_bytes=grant * 1024 * 1024),
        cost_estimate=pl.CostEstimate(flops=1_000_000, bytes_accessed=2_000_000, transcendentals=0),
    )(*ins)


def shaped(*shape):
    return jax.ShapeDtypeStruct(shape, F32)


def split3(value):
    high = value.astype(BF16)
    rest = value - high.astype(F32)
    middle = rest.astype(BF16)
    return high, middle, (rest - middle.astype(F32)).astype(BF16)


def dot_nt(left, right):
    return lax.dot_general(left, right, (((1,), (1,)), ((), ())), preferred_element_type=F32)


def place():
    return tuple(lax.axis_index(axis) for axis in ("gz", "gx", "gy"))


def prepare_kernel(span_y, tiles, residuals, owners, cells, wave, older, stiff, packets,
                   even, odd):
    pack_slots(span_y, tiles, residuals, owners, cells, packets)
    pack_strips(place(), wave, older, stiff, even, odd)


def pack_slots(span_y, tiles, residuals, owner_row, cell_row, out):
    rows = residuals.shape[1]
    owner = owner_row[...]
    owner_column = jnp.transpose(jnp.broadcast_to(owner.astype(F32), (rows, rows)))
    earlier = (owner_column.astype(jnp.int32) == owner) & (
        lax.broadcasted_iota(jnp.int32, (rows, rows), 0)
        < lax.broadcasted_iota(jnp.int32, (rows, rows), 1)
    )
    rank = jnp.sum(earlier.astype(jnp.int32), axis=0, keepdims=True)
    cell = cell_row[...]
    along = cell & (LANES - 1)
    fields = [residuals[pl.ds(field, 1), :] for field in range(STEPS)] + [cell.astype(F32)]
    stacked = jnp.concatenate(
        [jnp.broadcast_to(field, (SLOTS, rows)) for field in fields]
        + [jnp.zeros((LANES - SLOTS * len(fields), rows), F32)],
        axis=0,
    )
    line = lax.broadcasted_iota(jnp.int32, (LANES, rows), 0)
    slot = line - SLOTS * (line // SLOTS)
    tile = lax.broadcasted_iota(jnp.int32, (tiles, rows), 0)
    place = tile & (span_y - 1)
    total = jnp.zeros((tiles, LANES), F32)
    for group in range(3):
        named = owner == tile + (group - 1)
        wanted = slot == rank + CAP * group
        if group == 0:
            named = named & (place != 0)
            wanted = wanted & (along >= LANES - STRIP)
        if group == 2:
            named = named & (place != span_y - 1)
            wanted = wanted & (along < STRIP)
        chosen = named.astype(F32).astype(BF16)
        for part in split3(jnp.where(wanted, stacked, 0.0)):
            total = total + dot_nt(chosen, part)
    out[...] = total


def plane_kernel(face, rows, z_even, *refs):
    *packets, out, turned = refs
    out[pl.ds(0, face)] = z_even[...]
    out[pl.ds(face, 2 * STEPS)] = jnp.zeros((2 * STEPS, rows, LANES), F32)

    @pl.when(place()[0] < 2)
    def _():
        count = turned.shape[1]
        share = count // len(packets)
        for number, packet in enumerate(packets):
            turned[:, share * number : share * (number + 1)] = jnp.transpose(packet[...])
        line = lax.broadcasted_iota(jnp.int32, (rows, count), 0)
        spot = lax.broadcasted_iota(jnp.int32, (LANES, count), 0)

        def product(slot):
            cell = turned[pl.ds(SLOTS * STEPS + slot, 1), :].astype(jnp.int32)
            hit = (cell >> 7) == line
            highs, lows = [], []
            for step in range(STEPS):
                value = turned[pl.ds(SLOTS * step + slot, 1), :]
                high = value.astype(BF16).astype(F32)
                highs.append(jnp.where(hit, high, 0.0))
                lows.append(jnp.where(hit, value - high, 0.0))
            left = jnp.concatenate(highs + lows, axis=0).astype(BF16)
            right = jnp.where((cell & (LANES - 1)) == spot, 1.0, 0.0).astype(BF16)
            both = dot_nt(left, right)
            return both[: STEPS * rows] + both[STEPS * rows :]

        for part, groups in enumerate(((1,), (0, 2))):
            total = None
            for slot in [CAP * group + rank for group in groups for rank in range(CAP)]:
                total = product(slot) if total is None else total + product(slot)
            out[pl.ds(face + STEPS * part, STEPS)] = total.reshape(STEPS, rows, LANES)


def strip_places(depth):
    short = STRIP - RADIUS
    planes = []
    for pair in range(depth // 2):
        pieces = [(0, pair, STRIP, 0)]
        for number in range(4):
            pieces.append((1 + number // 2, 2 * pair + number % 2, short, STRIP + short * number))
        planes.append(pieces)
    quarters = LANES // STRIP
    for first in range(depth // 2, depth, quarters):
        planes.append([(0, first + turn, STRIP, STRIP * turn) for turn in range(quarters)])
    return planes


def turn_lanes(value, by):
    by = by % LANES
    return pltpu.roll(value, by, 1) if by else value


def pack_strips(ids, wave, older, stiff, even, odd):
    parity = ids[2] & 1
    lane = lane_of(wave.shape[1:])
    fields = (wave, older, stiff)
    for plane, pieces in enumerate(strip_places(wave.shape[0])):
        lows = highs = None
        for field, z, cells, start in pieces:
            value = fields[field][z]
            one = turn_lanes(jnp.where(lane < cells, value, 0.0), start)
            two = turn_lanes(jnp.where(lane >= LANES - cells, value, 0.0), start + cells)
            lows = one if lows is None else lows + one
            highs = two if highs is None else highs + two
        even[plane] = jnp.where(parity == 0, highs, lows)
        odd[plane] = jnp.where(parity == 0, lows, highs)


def strip_width(step):
    return {0: STRIP, 1: STRIP // 2, 2: STRIP // 4}.get(step, 0)


def folds(width):
    return LANES // (2 * width) if width else 0


def folded(length, width):
    return length // folds(width) if width else 0


def kept_lanes(shape, width):
    lane = lane_of(shape)
    return (lane < width) | (lane >= LANES - width)


def fold(pieces, width):
    total = None
    for turn, piece in enumerate(pieces):
        piece = jnp.where(kept_lanes(piece.shape, width), piece, 0.0)
        if turn:
            piece = pltpu.roll(piece, 2 * width * turn, 1)
        total = piece if total is None else total + piece
    return total


def unfold(both, turn, width):
    if turn:
        both = pltpu.roll(both, LANES - 2 * width * turn, 1)
    return jnp.where(kept_lanes(both.shape, width), both, 0.0)


def write_faces(width, ids, main, side, z_even, z_odd, x_even, x_odd):
    z_parity, x_parity = ids[0] & 1, ids[1] & 1
    depth, rows, _ = main.shape
    count = folds(width)
    for face, start in (
        (z_even, (depth - RADIUS) * (1 - z_parity)),
        (z_odd, (depth - RADIUS) * z_parity),
    ):
        face[pl.ds(0, RADIUS)] = main[pl.ds(start, RADIUS)]
        span = folded(RADIUS, width)
        for plane in range(span):
            face[RADIUS + plane] = fold(
                [side[start + plane + span * turn] for turn in range(count)], width
            )
    for face, start in (
        (x_even, (rows - RADIUS) * (1 - x_parity)),
        (x_odd, (rows - RADIUS) * x_parity),
    ):
        start = pl.multiple_of(start, RADIUS)
        face[pl.ds(0, depth)] = main[:, pl.ds(start, RADIUS), :]
        span = folded(depth, width)
        for plane in range(span):
            face[depth + plane] = fold(
                [side[plane + span * turn, pl.ds(start, RADIUS), :] for turn in range(count)],
                width,
            )


def strip_unpack_kernel(
    even, odd, wave, wave_side, older_side, stiff_side, z_even, z_odd, x_even, x_odd
):
    ids = place()
    parity = ids[2] & 1
    lane = lane_of(wave.shape[1:])
    sides = (wave_side, older_side, stiff_side)
    for plane, pieces in enumerate(strip_places(wave.shape[0])):
        one, two = even[1 - parity, plane], odd[plane]
        after = jnp.where(parity == 0, one, two)
        before = jnp.where(parity == 0, two, one)
        for field, z, cells, start in pieces:
            sides[field][z] = jnp.where(
                lane < cells,
                turn_lanes(after, -start),
                jnp.where(lane >= LANES - cells, turn_lanes(before, -start - cells), 0.0),
            )
    write_faces(STRIP, ids, wave, wave_side, z_even, z_odd, x_even, x_odd)


def fill(width, ids, z_even, z_odd, x_even, x_odd, z_halo, x_halo):
    z_parity, x_parity = ids[0] & 1, ids[1] & 1
    depth = x_halo.shape[1]
    count = folds(width)
    pair = z_even.at[1 - z_parity]
    for face, start in ((pair, RADIUS * (1 - z_parity)), (z_odd, RADIUS * z_parity)):
        z_halo[0, pl.ds(start, RADIUS)] = face[pl.ds(0, RADIUS)]
        span = folded(RADIUS, width)
        for plane in range(span):
            both = face[RADIUS + plane]
            for turn in range(count):
                z_halo[1, start + plane + span * turn] = unfold(both, turn, width)
    for face, start in ((x_even, RADIUS * (1 - x_parity)), (x_odd, RADIUS * x_parity)):
        start = pl.multiple_of(start, RADIUS)
        x_halo[0, :, pl.ds(start, RADIUS), :] = face[pl.ds(0, depth)]
        span = folded(depth, width)
        for plane in range(span):
            both = face[depth + plane]
            for turn in range(count):
                x_halo[1, plane + span * turn, pl.ds(start, RADIUS), :] = unfold(both, turn, width)


def own_kernel(last, wave, side, band_high, band_low, *rest):
    *outs, y_terms = rest
    depth, rows, _ = wave.shape
    if last:
        outs, kept = outs[:1], outs[1]
        kept[...] = wave[...]
    width = LANES * len(outs)
    both = jnp.concatenate(
        [wave[...].reshape(depth * rows, LANES), side[...].reshape(depth * rows, LANES)], axis=1
    )
    high = both.astype(BF16)
    low = (both - high.astype(F32)).astype(BF16)
    matrix, remainder = band_high[:, :width], band_low[:, :width]
    y_terms[:, :width] = (
        jnp.dot(high, matrix, preferred_element_type=F32)
        + jnp.dot(low, matrix, preferred_element_type=F32)
        + jnp.dot(high, remainder, preferred_element_type=F32)
    )
    beyond = jnp.zeros((RADIUS, LANES), F32)
    for z in range(depth):
        for part, (field, out) in enumerate(zip((wave, side), outs)):
            column = jnp.concatenate([beyond, field[z], beyond], axis=0)
            turned = [None] + [
                pltpu.roll(column, rows + 2 * RADIUS - offset, 0) for offset in range(1, RADIUS)
            ]
            total = y_terms[z * rows : (z + 1) * rows, part * LANES : (part + 1) * LANES]
            for offset in range(1, RADIUS + 1):
                if offset < RADIUS:
                    near = turned[offset][RADIUS : RADIUS + rows] + turned[RADIUS - offset][:rows]
                else:
                    near = column[2 * RADIUS :] + column[:rows]
                if z + offset < depth:
                    near = near + field[z + offset]
                if z >= offset:
                    near = near + field[z - offset]
                total = total + WEIGHTS[offset - 1] * near
            out[z] = total


def advance(step, shot, ids, wave, side, older, older_side, stiff, stiff_side, forward, image_in,
            planes, own, own_side, fresh, fresh_side, image, z_halo, x_halo, done=None):
    depth, rows, _ = wave.shape
    last = step == STEPS - 1
    line = lax.broadcasted_iota(jnp.int32, (RADIUS, LANES), 0)
    before_tile = [
        jnp.where(line < offset, WEIGHTS[offset - 1], 0.0) for offset in range(1, RADIUS + 1)
    ]
    behind_tile = [
        jnp.where(line >= RADIUS - offset, WEIGHTS[offset - 1], 0.0)
        for offset in range(1, RADIUS + 1)
    ]
    between = jnp.zeros((rows - 2 * RADIUS, LANES), F32)

    def one(z, part, partial, field, previous, speed, target):
        total = partial[z]
        first = last_rows = None
        head, tail = x_halo[part, z, :RADIUS], x_halo[part, z, RADIUS:]
        for offset in range(1, RADIUS + 1):
            if z < offset:
                total = total + WEIGHTS[offset - 1] * z_halo[part, RADIUS + z - offset]
            if z + offset >= depth:
                total = total + WEIGHTS[offset - 1] * z_halo[part, RADIUS + z + offset - depth]
            above = pltpu.roll(head, offset, 0) if offset < RADIUS else head
            below = pltpu.roll(tail, RADIUS - offset, 0) if offset < RADIUS else tail
            above = before_tile[offset - 1] * above
            below = behind_tile[offset - 1] * below
            first = above if first is None else first + above
            last_rows = below if last_rows is None else last_rows + below
        total = total + jnp.concatenate([first, between, last_rows], axis=0)
        if z == 0:
            total = total + planes[STEPS * part + step]
        value = 2.0 * field[z] - previous[z] + speed[z] * total
        target[z] = value
        return value

    for z in range(depth):
        value = one(z, 0, own, wave, older, stiff, fresh)
        product = forward[step, z].astype(F32) * value
        if step:
            product = product + image_in[z]
        if last:
            product = product * muting(ids, *shot, z, depth, rows)
        image[z] = product
        if done is not None:
            done(z)
        if not last:
            one(z, 1, own_side, side, older_side, stiff_side, fresh_side)


def muting(ids, shot_x, shot_y, z, depth, rows):
    gap_z = (ids[0] * depth + z).astype(F32)
    gap_x = (
        ids[1] * rows + lax.broadcasted_iota(jnp.int32, (rows, LANES), 0) - shot_x
    ).astype(F32)
    gap_y = (ids[2] * LANES + lane_of((rows, LANES)) - shot_y).astype(F32)
    distance = gap_z * gap_z + gap_x * gap_x + gap_y * gap_y
    return jnp.minimum(1.0, distance / 576.0)


def step_kernel(step, total_y, x_odd_in, x_even_in, z_odd_in, z_even_in, wave, side, older,
                older_side, stiff, stiff_side, forward, own, *rest):
    ids = place()
    last = step == STEPS - 1
    own_side = image_in = None
    if not last:
        own_side, *rest = rest
    if step:
        planes, image_in, *rest = rest
    else:
        planes, *rest = rest
        face = z_even_in.shape[1] - 2 * STEPS
        both = z_even_in[0, pl.ds(face, 2 * STEPS)] + z_even_in[1, pl.ds(face, 2 * STEPS)]
        planes[...] = jnp.where(ids[0] == 0, both, 0.0)
    shot = done = None
    copies = []
    if last:
        (source, image_out, wave_out, z_halo, x_halo, image, fresh, sems) = rest
        fresh_side = None
        cell = source[0, 0]
        shot = (lax.div(cell, total_y), lax.rem(cell, total_y))

        def done(z):
            if (z + 1) % CHUNK:
                return
            chunk = pl.ds(z + 1 - CHUNK, CHUNK)
            for number, (held, out) in enumerate(((image, image_out), (fresh, wave_out))):
                copies.append(
                    pltpu.make_async_copy(
                        held.at[chunk], out.at[chunk], sems.at[number, z // CHUNK]
                    )
                )
                copies[-1].start()

    else:
        image, fresh, fresh_side, z_even, z_odd, x_even, x_odd, z_halo, x_halo = rest
    fill(strip_width(step), ids, z_even_in, z_odd_in, x_even_in, x_odd_in, z_halo, x_halo)
    advance(step, shot, ids, wave, side, older, older_side, stiff, stiff_side, forward, image_in,
            planes, own, own_side, fresh, fresh_side, image, z_halo, x_halo, done)
    for copy in copies:
        copy.wait()
    if not last:
        write_faces(strip_width(step + 1), ids, fresh, fresh_side, z_even, z_odd, x_even, x_odd)


def swap(block, axis, parity):
    count = lax.axis_size(axis)
    pairs = []
    for left in range(parity, count - 1, 2):
        pairs += [(left, left + 1), (left + 1, left)]
    return lax.ppermute(block, axis, pairs)


def pair_gather(block, axis, parity):
    count = lax.axis_size(axis)
    groups = [
        [(2 * pair + parity) % count, (2 * pair + parity + 1) % count]
        for pair in range(count // 2)
    ]
    return lax.all_gather(block, axis, axis=0, tiled=False, axis_index_groups=groups)


def exchange(faces):
    z_even, z_odd, x_even, x_odd = faces
    z_odd = swap(z_odd, "gz", 1)
    x_even = swap(x_even, "gx", 0)
    x_odd = swap(x_odd, "gx", 1)
    z_even = pair_gather(z_even, "gz", 0)
    return z_even, z_odd, x_even, x_odd


def on_device(
    stiffness, older_wave, wave_now, forward_wave, residuals, owners, receivers, source_cell
):
    depth, rows, cols = wave_now.shape
    span_x, span_y, span_z = (lax.axis_size(axis) for axis in ("gx", "gy", "gz"))
    tiles = span_x * span_y
    band_high, band_low = (jnp.asarray(part) for part in band())
    block = shaped(depth, rows, LANES)

    def faces_out(step):
        width = strip_width(step)
        z_face = shaped(RADIUS + folded(RADIUS, width), rows, LANES)
        x_face = shaped(depth + folded(depth, width), RADIUS, LANES)
        return [z_face, z_face, x_face, x_face]

    strips = shaped(len(strip_places(depth)), rows, LANES)
    packets, even, odd = call(
        functools.partial(prepare_kernel, span_y, tiles),
        [shaped(tiles, LANES), strips, strips],
        [residuals, owners.reshape(1, -1), receivers.reshape(1, -1), wave_now, older_wave,
         stiffness],
        in_specs=[pl.BlockSpec()] * 6,
        grant=60,
    )
    packets = lax.all_to_all(packets, ("gx", "gy"), 0, 0, tiled=True)
    odd = swap(odd, "gy", 1)
    even = pair_gather(even, "gy", 0)
    side, older_side, stiff_side, *faces = call(
        strip_unpack_kernel,
        [block] * 3 + faces_out(0),
        [even, odd, wave_now],
    )
    packets, faces = lax.optimization_barrier((packets, faces))
    cores = 2
    packets = [packets] + [
        lax.ppermute(packets, "gz", [(chip + core, core) for core in range(cores)])
        for chip in range(cores, span_z, cores)
    ]
    face = faces[0].shape[0]
    faces[0] = call(
        functools.partial(plane_kernel, face, rows),
        shaped(face + 2 * STEPS, rows, LANES),
        [faces[0], *packets],
        scratch=[pltpu.VMEM((LANES, span_z // cores * tiles), F32)],
    )

    scratch = [
        pltpu.VMEM((2, 2 * RADIUS, rows, LANES), F32),
        pltpu.VMEM((2, depth, 2 * RADIUS, LANES), F32),
    ]
    wave, older = wave_now, older_wave
    image = None
    for step in range(STEPS):
        last = step == STEPS - 1
        own = call(
            functools.partial(own_kernel, last),
            [block, block],
            [wave, side, band_high, band_low],
            scratch=[pltpu.VMEM((depth * rows, 2 * LANES), F32)],
        )
        if last:
            *own, last_older = own
        faces = exchange(faces)
        ins = [*faces[::-1], wave, side, older, older_side, stiffness, stiff_side, forward_wave,
               *own]
        outs = [block, block]
        if step:
            ins += [planes, image]
        else:
            outs = [shaped(2 * STEPS, rows, LANES)] + outs
        if not last:
            outs += [block] + faces_out(step + 1)
        room, in_specs, out_specs = scratch, None, None
        if last:
            ins.append(source_cell.reshape(1, 1))
            out_specs = [pl.BlockSpec(memory_space=pl.ANY)] * 2
            held = pltpu.VMEM((depth, rows, LANES), F32)
            room = scratch + [held, held, pltpu.SemaphoreType.DMA((2, depth // CHUNK))]
        rest = call(
            functools.partial(step_kernel, step, cols * span_y), outs, ins, room, in_specs,
            out_specs=out_specs,
        )
        if not step:
            planes, *rest = rest
        image, fresh, *rest = rest
        older, wave = wave, fresh
        if not last:
            older_side, side = side, rest[0]
            faces = rest[1:]
    return image, last_older, wave


def solution(mesh):
    in_specs = (
        P("gz", "gx", "gy"),
        P("gz", "gx", "gy"),
        P("gz", "gx", "gy"),
        P(None, "gz", "gx", "gy"),
        P(None, ("gx", "gy", "gz")),
        P(("gx", "gy", "gz"), None),
        P(("gx", "gy", "gz")),
        P(),
    )
    out_specs = (P("gz", "gx", "gy"), P("gz", "gx", "gy"), P("gz", "gx", "gy"))
    return jax.shard_map(
        on_device, mesh=mesh, in_specs=in_specs, out_specs=out_specs, check_vma=False
    )
```

```python
import functools
import math

import jax
import jax.numpy as jnp
import numpy as np
from jax import lax
from jax.experimental import pallas as pl
from jax.experimental.pallas import tpu as pltpu
from jax.sharding import PartitionSpec as P

STEPS = 4
RADIUS = 8
LANES = 128
STRIP = 32
CAP = 8
CHUNK = 4
SLOTS = 3 * CAP
F32 = jnp.float32
BF16 = jnp.bfloat16


def stencil_weights():
    window = [math.cos(math.pi * offset / 20.0) for offset in range(1, RADIUS + 1)]
    alternating = sum(
        ((-1.0) ** (offset + 1) * window[offset - 1] for offset in range(1, RADIUS + 1))
    )
    factor = 1.0 / (2.0 * alternating)
    weights = []
    for offset in range(1, RADIUS + 1):
        weights.append(
            factor * 2.0 * (-1.0) ** (offset + 1) * window[offset - 1] / (offset * offset)
        )
    return (weights, -2.0 * sum(weights))


WEIGHTS, CENTER = stencil_weights()


def band():
    size = 2 * LANES
    matrix = np.zeros((size, size), np.float64)
    for column in range(size):
        matrix[column, column] = 3.0 * CENTER
        for offset in range(1, RADIUS + 1):
            matrix[(column + offset) % size, column] = WEIGHTS[offset - 1]
            matrix[(column - offset) % size, column] = WEIGHTS[offset - 1]
    matrix = matrix.astype(np.float32)
    high = matrix.astype(jnp.bfloat16)
    low = (matrix - high.astype(np.float32)).astype(jnp.bfloat16)
    return high, low


def lane_of(shape):
    return lax.broadcasted_iota(jnp.int32, shape, len(shape) - 1)


def vmem():
    return pl.BlockSpec(memory_space=pltpu.VMEM)


def call(body, outs, ins, scratch=(), in_specs=None, grant=32, out_specs=None):
    return pl.pallas_call(
        body,
        out_shape=outs,
        in_specs=in_specs or [vmem()] * len(ins),
        out_specs=out_specs or jax.tree.map(lambda _: vmem(), outs),
        scratch_shapes=list(scratch),
        compiler_params=pltpu.CompilerParams(vmem_limit_bytes=grant * 1024 * 1024),
        cost_estimate=pl.CostEstimate(flops=1_000_000, bytes_accessed=2_000_000, transcendentals=0),
    )(*ins)


def shaped(*shape):
    return jax.ShapeDtypeStruct(shape, F32)


def split3(value):
    high = value.astype(BF16)
    rest = value - high.astype(F32)
    middle = rest.astype(BF16)
    return high, middle, (rest - middle.astype(F32)).astype(BF16)


def dot_nt(left, right):
    return lax.dot_general(left, right, (((1,), (1,)), ((), ())), preferred_element_type=F32)


def place():
    return tuple(lax.axis_index(axis) for axis in ("gz", "gx", "gy"))


def prepare_kernel(span_y, tiles, residuals, owners, cells, wave, older, stiff, packets,
                   even, odd):
    pack_slots(span_y, tiles, residuals, owners, cells, packets)
    pack_strips(place(), wave, older, stiff, even, odd)


def pack_slots(span_y, tiles, residuals, owner_row, cell_row, out):
    rows = residuals.shape[1]
    owner = owner_row[...]
    owner_column = jnp.transpose(jnp.broadcast_to(owner.astype(F32), (rows, rows)))
    earlier = (owner_column.astype(jnp.int32) == owner) & (
        lax.broadcasted_iota(jnp.int32, (rows, rows), 0)
        < lax.broadcasted_iota(jnp.int32, (rows, rows), 1)
    )
    rank = jnp.sum(earlier.astype(jnp.int32), axis=0, keepdims=True)
    cell = cell_row[...]
    along = cell & (LANES - 1)
    fields = [residuals[pl.ds(field, 1), :] for field in range(STEPS)] + [cell.astype(F32)]
    stacked = jnp.concatenate(
        [jnp.broadcast_to(field, (SLOTS, rows)) for field in fields]
        + [jnp.zeros((LANES - SLOTS * len(fields), rows), F32)],
        axis=0,
    )
    line = lax.broadcasted_iota(jnp.int32, (LANES, rows), 0)
    slot = line - SLOTS * (line // SLOTS)
    tile = lax.broadcasted_iota(jnp.int32, (tiles, rows), 0)
    place = tile & (span_y - 1)
    total = jnp.zeros((tiles, LANES), F32)
    for group in range(3):
        named = owner == tile + (group - 1)
        wanted = slot == rank + CAP * group
        if group == 0:
            named = named & (place != 0)
            wanted = wanted & (along >= LANES - STRIP)
        if group == 2:
            named = named & (place != span_y - 1)
            wanted = wanted & (along < STRIP)
        chosen = named.astype(F32).astype(BF16)
        for part in split3(jnp.where(wanted, stacked, 0.0)):
            total = total + dot_nt(chosen, part)
    out[...] = total


def plane_kernel(face, rows, z_even, *refs):
    *packets, out, turned = refs
    out[pl.ds(0, face)] = z_even[...]
    out[pl.ds(face, 2 * STEPS)] = jnp.zeros((2 * STEPS, rows, LANES), F32)

    @pl.when(place()[0] < 2)
    def _():
        count = turned.shape[1]
        share = count // len(packets)
        for number, packet in enumerate(packets):
            turned[:, share * number : share * (number + 1)] = jnp.transpose(packet[...])
        line = lax.broadcasted_iota(jnp.int32, (rows, count), 0)
        spot = lax.broadcasted_iota(jnp.int32, (LANES, count), 0)

        def product(slot):
            cell = turned[pl.ds(SLOTS * STEPS + slot, 1), :].astype(jnp.int32)
            hit = (cell >> 7) == line
            highs, lows = [], []
            for step in range(STEPS):
                value = turned[pl.ds(SLOTS * step + slot, 1), :]
                high = value.astype(BF16).astype(F32)
                highs.append(jnp.where(hit, high, 0.0))
                lows.append(jnp.where(hit, value - high, 0.0))
            left = jnp.concatenate(highs + lows, axis=0).astype(BF16)
            right = jnp.where((cell & (LANES - 1)) == spot, 1.0, 0.0).astype(BF16)
            both = dot_nt(left, right)
            return both[: STEPS * rows] + both[STEPS * rows :]

        for part, groups in enumerate(((1,), (0, 2))):
            total = None
            for slot in [CAP * group + rank for group in groups for rank in range(CAP)]:
                total = product(slot) if total is None else total + product(slot)
            out[pl.ds(face + STEPS * part, STEPS)] = total.reshape(STEPS, rows, LANES)


def strip_places(depth):
    short = STRIP - RADIUS
    planes = []
    for pair in range(depth // 2):
        pieces = [(0, pair, STRIP, 0)]
        for number in range(4):
            pieces.append((1 + number // 2, 2 * pair + number % 2, short, STRIP + short * number))
        planes.append(pieces)
    quarters = LANES // STRIP
    for first in range(depth // 2, depth, quarters):
        planes.append([(0, first + turn, STRIP, STRIP * turn) for turn in range(quarters)])
    return planes


def turn_lanes(value, by):
    by = by % LANES
    return pltpu.roll(value, by, 1) if by else value


def pack_strips(ids, wave, older, stiff, even, odd):
    parity = ids[2] & 1
    lane = lane_of(wave.shape[1:])
    fields = (wave, older, stiff)
    for plane, pieces in enumerate(strip_places(wave.shape[0])):
        lows = highs = None
        for field, z, cells, start in pieces:
            value = fields[field][z]
            one = turn_lanes(jnp.where(lane < cells, value, 0.0), start)
            two = turn_lanes(jnp.where(lane >= LANES - cells, value, 0.0), start + cells)
            lows = one if lows is None else lows + one
            highs = two if highs is None else highs + two
        even[plane] = jnp.where(parity == 0, highs, lows)
        odd[plane] = jnp.where(parity == 0, lows, highs)


def strip_width(step):
    return {0: STRIP, 1: STRIP // 2, 2: STRIP // 4}.get(step, 0)


def folds(width):
    return LANES // (2 * width) if width else 0


def folded(length, width):
    return length // folds(width) if width else 0


def kept_lanes(shape, width):
    lane = lane_of(shape)
    return (lane < width) | (lane >= LANES - width)


def fold(pieces, width):
    total = None
    for turn, piece in enumerate(pieces):
        piece = jnp.where(kept_lanes(piece.shape, width), piece, 0.0)
        if turn:
            piece = pltpu.roll(piece, 2 * width * turn, 1)
        total = piece if total is None else total + piece
    return total


def unfold(both, turn, width):
    if turn:
        both = pltpu.roll(both, LANES - 2 * width * turn, 1)
    return jnp.where(kept_lanes(both.shape, width), both, 0.0)


def write_faces(width, ids, main, side, z_even, z_odd, x_even, x_odd):
    z_parity, x_parity = ids[0] & 1, ids[1] & 1
    depth, rows, _ = main.shape
    count = folds(width)
    for face, start in (
        (z_even, (depth - RADIUS) * (1 - z_parity)),
        (z_odd, (depth - RADIUS) * z_parity),
    ):
        face[pl.ds(0, RADIUS)] = main[pl.ds(start, RADIUS)]
        span = folded(RADIUS, width)
        for plane in range(span):
            face[RADIUS + plane] = fold(
                [side[start + plane + span * turn] for turn in range(count)], width
            )
    for face, start in (
        (x_even, (rows - RADIUS) * (1 - x_parity)),
        (x_odd, (rows - RADIUS) * x_parity),
    ):
        start = pl.multiple_of(start, RADIUS)
        face[pl.ds(0, depth)] = main[:, pl.ds(start, RADIUS), :]
        span = folded(depth, width)
        for plane in range(span):
            face[depth + plane] = fold(
                [side[plane + span * turn, pl.ds(start, RADIUS), :] for turn in range(count)],
                width,
            )


def strip_unpack_kernel(
    even, odd, wave, wave_side, older_side, stiff_side, z_even, z_odd, x_even, x_odd
):
    ids = place()
    parity = ids[2] & 1
    lane = lane_of(wave.shape[1:])
    sides = (wave_side, older_side, stiff_side)
    for plane, pieces in enumerate(strip_places(wave.shape[0])):
        one, two = even[1 - parity, plane], odd[plane]
        after = jnp.where(parity == 0, one, two)
        before = jnp.where(parity == 0, two, one)
        for field, z, cells, start in pieces:
            sides[field][z] = jnp.where(
                lane < cells,
                turn_lanes(after, -start),
                jnp.where(lane >= LANES - cells, turn_lanes(before, -start - cells), 0.0),
            )
    write_faces(STRIP, ids, wave, wave_side, z_even, z_odd, x_even, x_odd)


def fill(width, ids, z_even, z_odd, x_even, x_odd, z_halo, x_halo):
    z_parity, x_parity = ids[0] & 1, ids[1] & 1
    depth = x_halo.shape[1]
    count = folds(width)
    pair = z_even.at[1 - z_parity]
    for face, start in ((pair, RADIUS * (1 - z_parity)), (z_odd, RADIUS * z_parity)):
        z_halo[0, pl.ds(start, RADIUS)] = face[pl.ds(0, RADIUS)]
        span = folded(RADIUS, width)
        for plane in range(span):
            both = face[RADIUS + plane]
            for turn in range(count):
                z_halo[1, start + plane + span * turn] = unfold(both, turn, width)
    for face, start in ((x_even, RADIUS * (1 - x_parity)), (x_odd, RADIUS * x_parity)):
        start = pl.multiple_of(start, RADIUS)
        x_halo[0, :, pl.ds(start, RADIUS), :] = face[pl.ds(0, depth)]
        span = folded(depth, width)
        for plane in range(span):
            both = face[depth + plane]
            for turn in range(count):
                x_halo[1, plane + span * turn, pl.ds(start, RADIUS), :] = unfold(both, turn, width)


def own_kernel(wave, side, band_high, band_low, *rest):
    *outs, y_terms = rest
    depth, rows, _ = wave.shape
    width = LANES * len(outs)
    both = jnp.concatenate(
        [wave[...].reshape(depth * rows, LANES), side[...].reshape(depth * rows, LANES)], axis=1
    )
    high = both.astype(BF16)
    low = (both - high.astype(F32)).astype(BF16)
    matrix, remainder = band_high[:, :width], band_low[:, :width]
    y_terms[:, :width] = (
        jnp.dot(high, matrix, preferred_element_type=F32)
        + jnp.dot(low, matrix, preferred_element_type=F32)
        + jnp.dot(high, remainder, preferred_element_type=F32)
    )
    beyond = jnp.zeros((RADIUS, LANES), F32)
    for z in range(depth):
        for part, (field, out) in enumerate(zip((wave, side), outs)):
            column = jnp.concatenate([beyond, field[z], beyond], axis=0)
            turned = [None] + [
                pltpu.roll(column, rows + 2 * RADIUS - offset, 0) for offset in range(1, RADIUS)
            ]
            total = y_terms[z * rows : (z + 1) * rows, part * LANES : (part + 1) * LANES]
            for offset in range(1, RADIUS + 1):
                if offset < RADIUS:
                    near = turned[offset][RADIUS : RADIUS + rows] + turned[RADIUS - offset][:rows]
                else:
                    near = column[2 * RADIUS :] + column[:rows]
                if z + offset < depth:
                    near = near + field[z + offset]
                if z >= offset:
                    near = near + field[z - offset]
                total = total + WEIGHTS[offset - 1] * near
            out[z] = total


def advance(step, shot, ids, wave, side, older, older_side, stiff, stiff_side, forward, image_in,
            planes, own, own_side, fresh, fresh_side, image, z_halo, x_halo, done=None):
    depth, rows, _ = wave.shape
    last = step == STEPS - 1
    line = lax.broadcasted_iota(jnp.int32, (RADIUS, LANES), 0)
    before_tile = [
        jnp.where(line < offset, WEIGHTS[offset - 1], 0.0) for offset in range(1, RADIUS + 1)
    ]
    behind_tile = [
        jnp.where(line >= RADIUS - offset, WEIGHTS[offset - 1], 0.0)
        for offset in range(1, RADIUS + 1)
    ]
    between = jnp.zeros((rows - 2 * RADIUS, LANES), F32)

    def one(z, part, partial, field, previous, speed, target):
        total = partial[z]
        first = last_rows = None
        head, tail = x_halo[part, z, :RADIUS], x_halo[part, z, RADIUS:]
        for offset in range(1, RADIUS + 1):
            if z < offset:
                total = total + WEIGHTS[offset - 1] * z_halo[part, RADIUS + z - offset]
            if z + offset >= depth:
                total = total + WEIGHTS[offset - 1] * z_halo[part, RADIUS + z + offset - depth]
            above = pltpu.roll(head, offset, 0) if offset < RADIUS else head
            below = pltpu.roll(tail, RADIUS - offset, 0) if offset < RADIUS else tail
            above = before_tile[offset - 1] * above
            below = behind_tile[offset - 1] * below
            first = above if first is None else first + above
            last_rows = below if last_rows is None else last_rows + below
        total = total + jnp.concatenate([first, between, last_rows], axis=0)
        if z == 0:
            total = total + planes[STEPS * part + step]
        value = 2.0 * field[z] - previous[z] + speed[z] * total
        target[z] = value
        return value

    for z in range(depth):
        value = one(z, 0, own, wave, older, stiff, fresh)
        product = forward[step, z].astype(F32) * value
        if step:
            product = product + image_in[z]
        if last:
            product = product * muting(ids, *shot, z, depth, rows)
        image[z] = product
        if done is not None:
            done(z)
        if not last:
            one(z, 1, own_side, side, older_side, stiff_side, fresh_side)


def muting(ids, shot_x, shot_y, z, depth, rows):
    gap_z = (ids[0] * depth + z).astype(F32)
    gap_x = (
        ids[1] * rows + lax.broadcasted_iota(jnp.int32, (rows, LANES), 0) - shot_x
    ).astype(F32)
    gap_y = (ids[2] * LANES + lane_of((rows, LANES)) - shot_y).astype(F32)
    distance = gap_z * gap_z + gap_x * gap_x + gap_y * gap_y
    return jnp.minimum(1.0, distance / 576.0)


def step_kernel(step, total_y, x_odd_in, x_even_in, z_odd_in, z_even_in, wave, side, older,
                older_side, stiff, stiff_side, forward, own, *rest):
    ids = place()
    last = step == STEPS - 1
    own_side = image_in = None
    if not last:
        own_side, *rest = rest
    if step:
        planes, image_in, *rest = rest
    else:
        planes, *rest = rest
        face = z_even_in.shape[1] - 2 * STEPS
        both = z_even_in[0, pl.ds(face, 2 * STEPS)] + z_even_in[1, pl.ds(face, 2 * STEPS)]
        planes[...] = jnp.where(ids[0] == 0, both, 0.0)
    shot = done = None
    copies = []
    if last:
        (source, image_out, wave_out, older_out, z_halo, x_halo, image, fresh, sems,
         older_sem) = rest
        fresh_side = None
        copies.append(pltpu.make_async_copy(wave, older_out, older_sem))
        copies[-1].start()
        cell = source[0, 0]
        shot = (lax.div(cell, total_y), lax.rem(cell, total_y))

        def done(z):
            if (z + 1) % CHUNK:
                return
            chunk = pl.ds(z + 1 - CHUNK, CHUNK)
            for number, (held, out) in enumerate(((image, image_out), (fresh, wave_out))):
                copies.append(
                    pltpu.make_async_copy(
                        held.at[chunk], out.at[chunk], sems.at[number, z // CHUNK]
                    )
                )
                copies[-1].start()

    else:
        image, fresh, fresh_side, z_even, z_odd, x_even, x_odd, z_halo, x_halo = rest
    fill(strip_width(step), ids, z_even_in, z_odd_in, x_even_in, x_odd_in, z_halo, x_halo)
    advance(step, shot, ids, wave, side, older, older_side, stiff, stiff_side, forward, image_in,
            planes, own, own_side, fresh, fresh_side, image, z_halo, x_halo, done)
    for copy in copies:
        copy.wait()
    if not last:
        write_faces(strip_width(step + 1), ids, fresh, fresh_side, z_even, z_odd, x_even, x_odd)


def swap(block, axis, parity):
    count = lax.axis_size(axis)
    pairs = []
    for left in range(parity, count - 1, 2):
        pairs += [(left, left + 1), (left + 1, left)]
    return lax.ppermute(block, axis, pairs)


def pair_gather(block, axis, parity):
    count = lax.axis_size(axis)
    groups = [
        [(2 * pair + parity) % count, (2 * pair + parity + 1) % count]
        for pair in range(count // 2)
    ]
    return lax.all_gather(block, axis, axis=0, tiled=False, axis_index_groups=groups)


def exchange(faces):
    z_even, z_odd, x_even, x_odd = faces
    z_odd = swap(z_odd, "gz", 1)
    x_even = swap(x_even, "gx", 0)
    x_odd = swap(x_odd, "gx", 1)
    z_even = pair_gather(z_even, "gz", 0)
    return z_even, z_odd, x_even, x_odd


def on_device(
    stiffness, older_wave, wave_now, forward_wave, residuals, owners, receivers, source_cell
):
    depth, rows, cols = wave_now.shape
    span_x, span_y, span_z = (lax.axis_size(axis) for axis in ("gx", "gy", "gz"))
    tiles = span_x * span_y
    band_high, band_low = (jnp.asarray(part) for part in band())
    block = shaped(depth, rows, LANES)

    def faces_out(step):
        width = strip_width(step)
        z_face = shaped(RADIUS + folded(RADIUS, width), rows, LANES)
        x_face = shaped(depth + folded(depth, width), RADIUS, LANES)
        return [z_face, z_face, x_face, x_face]

    strips = shaped(len(strip_places(depth)), rows, LANES)
    packets, even, odd = call(
        functools.partial(prepare_kernel, span_y, tiles),
        [shaped(tiles, LANES), strips, strips],
        [residuals, owners.reshape(1, -1), receivers.reshape(1, -1), wave_now, older_wave,
         stiffness],
        in_specs=[pl.BlockSpec()] * 6,
        grant=60,
    )
    packets = lax.all_to_all(packets, ("gx", "gy"), 0, 0, tiled=True)
    odd = swap(odd, "gy", 1)
    even = pair_gather(even, "gy", 0)
    side, older_side, stiff_side, *faces = call(
        strip_unpack_kernel,
        [block] * 3 + faces_out(0),
        [even, odd, wave_now],
    )
    packets, faces = lax.optimization_barrier((packets, faces))
    cores = 2
    packets = [packets] + [
        lax.ppermute(packets, "gz", [(chip + core, core) for core in range(cores)])
        for chip in range(cores, span_z, cores)
    ]
    face = faces[0].shape[0]
    faces[0] = call(
        functools.partial(plane_kernel, face, rows),
        shaped(face + 2 * STEPS, rows, LANES),
        [faces[0], *packets],
        scratch=[pltpu.VMEM((LANES, span_z // cores * tiles), F32)],
    )

    scratch = [
        pltpu.VMEM((2, 2 * RADIUS, rows, LANES), F32),
        pltpu.VMEM((2, depth, 2 * RADIUS, LANES), F32),
    ]
    wave, older = wave_now, older_wave
    image = None
    for step in range(STEPS):
        last = step == STEPS - 1
        own = call(
            own_kernel,
            [block] if last else [block, block],
            [wave, side, band_high, band_low],
            scratch=[pltpu.VMEM((depth * rows, 2 * LANES), F32)],
        )
        faces = exchange(faces)
        ins = [*faces[::-1], wave, side, older, older_side, stiffness, stiff_side, forward_wave,
               *own]
        outs = [block, block]
        if step:
            ins += [planes, image]
        else:
            outs = [shaped(2 * STEPS, rows, LANES)] + outs
        if not last:
            outs += [block] + faces_out(step + 1)
        room, in_specs, out_specs = scratch, None, None
        if last:
            ins.append(source_cell.reshape(1, 1))
            outs.append(block)
            out_specs = [pl.BlockSpec(memory_space=pl.ANY)] * 3
            held = pltpu.VMEM((depth, rows, LANES), F32)
            room = scratch + [held, held, pltpu.SemaphoreType.DMA((2, depth // CHUNK)),
                              pltpu.SemaphoreType.DMA]
        rest = call(
            functools.partial(step_kernel, step, cols * span_y), outs, ins, room, in_specs,
            out_specs=out_specs,
        )
        if not step:
            planes, *rest = rest
        image, fresh, *rest = rest
        older, wave = wave, fresh
        if not last:
            older_side, side = side, rest[0]
            faces = rest[1:]
    return image, rest[0], wave


def solution(mesh):
    in_specs = (
        P("gz", "gx", "gy"),
        P("gz", "gx", "gy"),
        P("gz", "gx", "gy"),
        P(None, "gz", "gx", "gy"),
        P(None, ("gx", "gy", "gz")),
        P(("gx", "gy", "gz"), None),
        P(("gx", "gy", "gz")),
        P(),
    )
    out_specs = (P("gz", "gx", "gy"), P("gz", "gx", "gy"), P("gz", "gx", "gy"))
    return jax.shard_map(
        on_device, mesh=mesh, in_specs=in_specs, out_specs=out_specs, check_vma=False
    )
```

```python
import functools
import math

import jax
import jax.numpy as jnp
import numpy as np
from jax import lax
from jax.experimental import pallas as pl
from jax.experimental.pallas import tpu as pltpu
from jax.sharding import PartitionSpec as P

STEPS = 4
RADIUS = 8
LANES = 128
STRIP = 32
CAP = 8
CHUNK = 4
SLOTS = 3 * CAP
F32 = jnp.float32
BF16 = jnp.bfloat16


def stencil_weights():
    window = [math.cos(math.pi * offset / 20.0) for offset in range(1, RADIUS + 1)]
    alternating = sum(
        ((-1.0) ** (offset + 1) * window[offset - 1] for offset in range(1, RADIUS + 1))
    )
    factor = 1.0 / (2.0 * alternating)
    weights = []
    for offset in range(1, RADIUS + 1):
        weights.append(
            factor * 2.0 * (-1.0) ** (offset + 1) * window[offset - 1] / (offset * offset)
        )
    return (weights, -2.0 * sum(weights))


WEIGHTS, CENTER = stencil_weights()


def band():
    size = 2 * LANES
    matrix = np.zeros((size, size), np.float64)
    for column in range(size):
        matrix[column, column] = 3.0 * CENTER
        for offset in range(1, RADIUS + 1):
            matrix[(column + offset) % size, column] = WEIGHTS[offset - 1]
            matrix[(column - offset) % size, column] = WEIGHTS[offset - 1]
    matrix = matrix.astype(np.float32)
    high = matrix.astype(jnp.bfloat16)
    low = (matrix - high.astype(np.float32)).astype(jnp.bfloat16)
    return high, low


def lane_of(shape):
    return lax.broadcasted_iota(jnp.int32, shape, len(shape) - 1)


def vmem():
    return pl.BlockSpec(memory_space=pltpu.VMEM)


def call(body, outs, ins, scratch=(), in_specs=None, grant=32, out_specs=None):
    return pl.pallas_call(
        body,
        out_shape=outs,
        in_specs=in_specs or [vmem()] * len(ins),
        out_specs=out_specs or jax.tree.map(lambda _: vmem(), outs),
        scratch_shapes=list(scratch),
        compiler_params=pltpu.CompilerParams(vmem_limit_bytes=grant * 1024 * 1024),
        cost_estimate=pl.CostEstimate(flops=1_000_000, bytes_accessed=2_000_000, transcendentals=0),
    )(*ins)


def shaped(*shape):
    return jax.ShapeDtypeStruct(shape, F32)


def split3(value):
    high = value.astype(BF16)
    rest = value - high.astype(F32)
    middle = rest.astype(BF16)
    return high, middle, (rest - middle.astype(F32)).astype(BF16)


def dot_nt(left, right):
    return lax.dot_general(left, right, (((1,), (1,)), ((), ())), preferred_element_type=F32)


def place():
    return tuple(lax.axis_index(axis) for axis in ("gz", "gx", "gy"))


def prepare_kernel(span_y, tiles, residuals, owners, cells, wave, older, stiff, packets,
                   even, odd):
    pack_slots(span_y, tiles, residuals, owners, cells, packets)
    pack_strips(place(), wave, older, stiff, even, odd)


def pack_slots(span_y, tiles, residuals, owner_row, cell_row, out):
    rows = residuals.shape[1]
    owner = owner_row[...]
    owner_column = jnp.transpose(jnp.broadcast_to(owner.astype(F32), (rows, rows)))
    earlier = (owner_column.astype(jnp.int32) == owner) & (
        lax.broadcasted_iota(jnp.int32, (rows, rows), 0)
        < lax.broadcasted_iota(jnp.int32, (rows, rows), 1)
    )
    rank = jnp.sum(earlier.astype(jnp.int32), axis=0, keepdims=True)
    cell = cell_row[...]
    along = cell & (LANES - 1)
    fields = [residuals[pl.ds(field, 1), :] for field in range(STEPS)] + [cell.astype(F32)]
    stacked = jnp.concatenate(
        [jnp.broadcast_to(field, (SLOTS, rows)) for field in fields]
        + [jnp.zeros((LANES - SLOTS * len(fields), rows), F32)],
        axis=0,
    )
    line = lax.broadcasted_iota(jnp.int32, (LANES, rows), 0)
    slot = line - SLOTS * (line // SLOTS)
    tile = lax.broadcasted_iota(jnp.int32, (tiles, rows), 0)
    place = tile & (span_y - 1)
    total = jnp.zeros((tiles, LANES), F32)
    for group in range(3):
        named = owner == tile + (group - 1)
        wanted = slot == rank + CAP * group
        if group == 0:
            named = named & (place != 0)
            wanted = wanted & (along >= LANES - STRIP)
        if group == 2:
            named = named & (place != span_y - 1)
            wanted = wanted & (along < STRIP)
        chosen = named.astype(F32).astype(BF16)
        for part in split3(jnp.where(wanted, stacked, 0.0)):
            total = total + dot_nt(chosen, part)
    out[...] = total


def plane_kernel(face, rows, z_even, *refs):
    *packets, out, turned = refs
    out[pl.ds(0, face)] = z_even[...]
    out[pl.ds(face, 2 * STEPS)] = jnp.zeros((2 * STEPS, rows, LANES), F32)

    @pl.when(place()[0] < 2)
    def _():
        count = turned.shape[1]
        share = count // len(packets)
        for number, packet in enumerate(packets):
            turned[:, share * number : share * (number + 1)] = jnp.transpose(packet[...])
        line = lax.broadcasted_iota(jnp.int32, (rows, count), 0)
        spot = lax.broadcasted_iota(jnp.int32, (LANES, count), 0)

        def product(slot):
            cell = turned[pl.ds(SLOTS * STEPS + slot, 1), :].astype(jnp.int32)
            hit = (cell >> 7) == line
            highs, lows = [], []
            for step in range(STEPS):
                value = turned[pl.ds(SLOTS * step + slot, 1), :]
                high = value.astype(BF16).astype(F32)
                highs.append(jnp.where(hit, high, 0.0))
                lows.append(jnp.where(hit, value - high, 0.0))
            left = jnp.concatenate(highs + lows, axis=0).astype(BF16)
            right = jnp.where((cell & (LANES - 1)) == spot, 1.0, 0.0).astype(BF16)
            both = dot_nt(left, right)
            return both[: STEPS * rows] + both[STEPS * rows :]

        for part, groups in enumerate(((1,), (0, 2))):
            total = None
            for slot in [CAP * group + rank for group in groups for rank in range(CAP)]:
                total = product(slot) if total is None else total + product(slot)
            out[pl.ds(face + STEPS * part, STEPS)] = total.reshape(STEPS, rows, LANES)


def strip_places(depth):
    short = STRIP - RADIUS
    planes = []
    for pair in range(depth // 2):
        pieces = [(0, pair, STRIP, 0)]
        for number in range(4):
            pieces.append((1 + number // 2, 2 * pair + number % 2, short, STRIP + short * number))
        planes.append(pieces)
    quarters = LANES // STRIP
    for first in range(depth // 2, depth, quarters):
        planes.append([(0, first + turn, STRIP, STRIP * turn) for turn in range(quarters)])
    return planes


def turn_lanes(value, by):
    by = by % LANES
    return pltpu.roll(value, by, 1) if by else value


def pack_strips(ids, wave, older, stiff, even, odd):
    parity = ids[2] & 1
    lane = lane_of(wave.shape[1:])
    fields = (wave, older, stiff)
    for plane, pieces in enumerate(strip_places(wave.shape[0])):
        lows = highs = None
        for field, z, cells, start in pieces:
            value = fields[field][z]
            one = turn_lanes(jnp.where(lane < cells, value, 0.0), start)
            two = turn_lanes(jnp.where(lane >= LANES - cells, value, 0.0), start + cells)
            lows = one if lows is None else lows + one
            highs = two if highs is None else highs + two
        even[plane] = jnp.where(parity == 0, highs, lows)
        odd[plane] = jnp.where(parity == 0, lows, highs)


def strip_width(step):
    return {0: STRIP, 1: STRIP // 2, 2: STRIP // 4}.get(step, 0)


def folds(width):
    return LANES // (2 * width) if width else 0


def folded(length, width):
    return length // folds(width) if width else 0


def kept_lanes(shape, width):
    lane = lane_of(shape)
    return (lane < width) | (lane >= LANES - width)


def fold(pieces, width):
    total = None
    for turn, piece in enumerate(pieces):
        piece = jnp.where(kept_lanes(piece.shape, width), piece, 0.0)
        if turn:
            piece = pltpu.roll(piece, 2 * width * turn, 1)
        total = piece if total is None else total + piece
    return total


def unfold(both, turn, width):
    if turn:
        both = pltpu.roll(both, LANES - 2 * width * turn, 1)
    return jnp.where(kept_lanes(both.shape, width), both, 0.0)


def write_faces(width, ids, main, side, z_even, z_odd, x_even, x_odd):
    z_parity, x_parity = ids[0] & 1, ids[1] & 1
    depth, rows, _ = main.shape
    count = folds(width)
    for face, start in (
        (z_even, (depth - RADIUS) * (1 - z_parity)),
        (z_odd, (depth - RADIUS) * z_parity),
    ):
        face[pl.ds(0, RADIUS)] = main[pl.ds(start, RADIUS)]
        span = folded(RADIUS, width)
        for plane in range(span):
            face[RADIUS + plane] = fold(
                [side[start + plane + span * turn] for turn in range(count)], width
            )
    for face, start in (
        (x_even, (rows - RADIUS) * (1 - x_parity)),
        (x_odd, (rows - RADIUS) * x_parity),
    ):
        start = pl.multiple_of(start, RADIUS)
        face[pl.ds(0, depth)] = main[:, pl.ds(start, RADIUS), :]
        span = folded(depth, width)
        for plane in range(span):
            face[depth + plane] = fold(
                [side[plane + span * turn, pl.ds(start, RADIUS), :] for turn in range(count)],
                width,
            )


def strip_unpack_kernel(
    even, odd, wave, wave_side, older_side, stiff_side, z_even, z_odd, x_even, x_odd
):
    ids = place()
    parity = ids[2] & 1
    lane = lane_of(wave.shape[1:])
    sides = (wave_side, older_side, stiff_side)
    for plane, pieces in enumerate(strip_places(wave.shape[0])):
        one, two = even[1 - parity, plane], odd[plane]
        after = jnp.where(parity == 0, one, two)
        before = jnp.where(parity == 0, two, one)
        for field, z, cells, start in pieces:
            sides[field][z] = jnp.where(
                lane < cells,
                turn_lanes(after, -start),
                jnp.where(lane >= LANES - cells, turn_lanes(before, -start - cells), 0.0),
            )
    write_faces(STRIP, ids, wave, wave_side, z_even, z_odd, x_even, x_odd)


def fill(width, ids, z_even, z_odd, x_even, x_odd, z_halo, x_halo):
    z_parity, x_parity = ids[0] & 1, ids[1] & 1
    depth = x_halo.shape[1]
    count = folds(width)
    pair = z_even.at[1 - z_parity]
    for face, start in ((pair, RADIUS * (1 - z_parity)), (z_odd, RADIUS * z_parity)):
        z_halo[0, pl.ds(start, RADIUS)] = face[pl.ds(0, RADIUS)]
        span = folded(RADIUS, width)
        for plane in range(span):
            both = face[RADIUS + plane]
            for turn in range(count):
                z_halo[1, start + plane + span * turn] = unfold(both, turn, width)
    for face, start in ((x_even, RADIUS * (1 - x_parity)), (x_odd, RADIUS * x_parity)):
        start = pl.multiple_of(start, RADIUS)
        x_halo[0, :, pl.ds(start, RADIUS), :] = face[pl.ds(0, depth)]
        span = folded(depth, width)
        for plane in range(span):
            both = face[depth + plane]
            for turn in range(count):
                x_halo[1, plane + span * turn, pl.ds(start, RADIUS), :] = unfold(both, turn, width)


def own_kernel(wave, side, band_high, band_low, *rest):
    *outs, y_terms = rest
    depth, rows, _ = wave.shape
    width = LANES * len(outs)
    both = jnp.concatenate(
        [wave[...].reshape(depth * rows, LANES), side[...].reshape(depth * rows, LANES)], axis=1
    )
    high = both.astype(BF16)
    low = (both - high.astype(F32)).astype(BF16)
    matrix, remainder = band_high[:, :width], band_low[:, :width]
    y_terms[:, :width] = (
        jnp.dot(high, matrix, preferred_element_type=F32)
        + jnp.dot(low, matrix, preferred_element_type=F32)
        + jnp.dot(high, remainder, preferred_element_type=F32)
    )
    beyond = jnp.zeros((RADIUS, LANES), F32)
    for z in range(depth):
        for part, (field, out) in enumerate(zip((wave, side), outs)):
            column = jnp.concatenate([beyond, field[z], beyond], axis=0)
            turned = [None] + [
                pltpu.roll(column, rows + 2 * RADIUS - offset, 0) for offset in range(1, RADIUS)
            ]
            total = y_terms[z * rows : (z + 1) * rows, part * LANES : (part + 1) * LANES]
            for offset in range(1, RADIUS + 1):
                if offset < RADIUS:
                    near = turned[offset][RADIUS : RADIUS + rows] + turned[RADIUS - offset][:rows]
                else:
                    near = column[2 * RADIUS :] + column[:rows]
                if z + offset < depth:
                    near = near + field[z + offset]
                if z >= offset:
                    near = near + field[z - offset]
                total = total + WEIGHTS[offset - 1] * near
            out[z] = total


def advance(step, shot, ids, wave, side, older, older_side, stiff, stiff_side, forward, image_in,
            planes, own, own_side, fresh, fresh_side, image, z_halo, x_halo, done=None):
    depth, rows, _ = wave.shape
    last = step == STEPS - 1
    line = lax.broadcasted_iota(jnp.int32, (RADIUS, LANES), 0)
    before_tile = [
        jnp.where(line < offset, WEIGHTS[offset - 1], 0.0) for offset in range(1, RADIUS + 1)
    ]
    behind_tile = [
        jnp.where(line >= RADIUS - offset, WEIGHTS[offset - 1], 0.0)
        for offset in range(1, RADIUS + 1)
    ]
    between = jnp.zeros((rows - 2 * RADIUS, LANES), F32)

    def one(z, part, partial, field, previous, speed, target):
        total = partial[z]
        first = last_rows = None
        head, tail = x_halo[part, z, :RADIUS], x_halo[part, z, RADIUS:]
        for offset in range(1, RADIUS + 1):
            if z < offset:
                total = total + WEIGHTS[offset - 1] * z_halo[part, RADIUS + z - offset]
            if z + offset >= depth:
                total = total + WEIGHTS[offset - 1] * z_halo[part, RADIUS + z + offset - depth]
            above = pltpu.roll(head, offset, 0) if offset < RADIUS else head
            below = pltpu.roll(tail, RADIUS - offset, 0) if offset < RADIUS else tail
            above = before_tile[offset - 1] * above
            below = behind_tile[offset - 1] * below
            first = above if first is None else first + above
            last_rows = below if last_rows is None else last_rows + below
        total = total + jnp.concatenate([first, between, last_rows], axis=0)
        if z == 0:
            total = total + planes[STEPS * part + step]
        value = 2.0 * field[z] - previous[z] + speed[z] * total
        target[z] = value
        return value

    for z in range(depth):
        value = one(z, 0, own, wave, older, stiff, fresh)
        product = forward[step, z].astype(F32) * value
        if step:
            product = product + image_in[z]
        if last:
            product = product * muting(ids, *shot, z, depth, rows)
        image[z] = product
        if done is not None:
            done(z)
        if not last:
            one(z, 1, own_side, side, older_side, stiff_side, fresh_side)


def muting(ids, shot_x, shot_y, z, depth, rows):
    gap_z = (ids[0] * depth + z).astype(F32)
    gap_x = (
        ids[1] * rows + lax.broadcasted_iota(jnp.int32, (rows, LANES), 0) - shot_x
    ).astype(F32)
    gap_y = (ids[2] * LANES + lane_of((rows, LANES)) - shot_y).astype(F32)
    distance = gap_z * gap_z + gap_x * gap_x + gap_y * gap_y
    return jnp.minimum(1.0, distance / 576.0)


def step_kernel(step, total_y, x_odd_in, x_even_in, z_odd_in, z_even_in, wave, side, older,
                older_side, stiff, stiff_side, forward, own, *rest):
    ids = place()
    last = step == STEPS - 1
    own_side = image_in = None
    if not last:
        own_side, *rest = rest
    if step:
        planes, image_in, *rest = rest
    else:
        planes, *rest = rest
        face = z_even_in.shape[1] - 2 * STEPS
        both = z_even_in[0, pl.ds(face, 2 * STEPS)] + z_even_in[1, pl.ds(face, 2 * STEPS)]
        planes[...] = jnp.where(ids[0] == 0, both, 0.0)
    shot = done = None
    copies = []
    if last:
        (source, image_out, wave_out, older_out, z_halo, x_halo, image, fresh, sems,
         older_sem) = rest
        fresh_side = None
        copies.append(pltpu.make_async_copy(wave, older_out, older_sem))
        copies[-1].start()
        cell = source[0, 0]
        shot = (lax.div(cell, total_y), lax.rem(cell, total_y))

        def done(z):
            if (z + 1) % CHUNK:
                return
            chunk = pl.ds(z + 1 - CHUNK, CHUNK)
            for number, (held, out) in enumerate(((image, image_out), (fresh, wave_out))):
                copies.append(
                    pltpu.make_async_copy(
                        held.at[chunk], out.at[chunk], sems.at[number, z // CHUNK]
                    )
                )
                copies[-1].start()

    else:
        image, fresh, fresh_side, z_even, z_odd, x_even, x_odd, z_halo, x_halo = rest
    fill(strip_width(step), ids, z_even_in, z_odd_in, x_even_in, x_odd_in, z_halo, x_halo)
    advance(step, shot, ids, wave, side, older, older_side, stiff, stiff_side, forward, image_in,
            planes, own, own_side, fresh, fresh_side, image, z_halo, x_halo, done)
    for copy in copies:
        copy.wait()
    if not last:
        write_faces(strip_width(step + 1), ids, fresh, fresh_side, z_even, z_odd, x_even, x_odd)


def swap(block, axis, parity):
    count = lax.axis_size(axis)
    pairs = []
    for left in range(parity, count - 1, 2):
        pairs += [(left, left + 1), (left + 1, left)]
    return lax.ppermute(block, axis, pairs)


def pair_gather(block, axis, parity):
    count = lax.axis_size(axis)
    groups = [
        [(2 * pair + parity) % count, (2 * pair + parity + 1) % count]
        for pair in range(count // 2)
    ]
    return lax.all_gather(block, axis, axis=0, tiled=False, axis_index_groups=groups)


def exchange(faces):
    z_even, z_odd, x_even, x_odd = faces
    z_odd = swap(z_odd, "gz", 1)
    x_even = swap(x_even, "gx", 0)
    x_odd = swap(x_odd, "gx", 1)
    z_even = pair_gather(z_even, "gz", 0)
    return z_even, z_odd, x_even, x_odd


def on_device(
    stiffness, older_wave, wave_now, forward_wave, residuals, owners, receivers, source_cell
):
    depth, rows, cols = wave_now.shape
    span_x, span_y, span_z = (lax.axis_size(axis) for axis in ("gx", "gy", "gz"))
    tiles = span_x * span_y
    band_high, band_low = (jnp.asarray(part) for part in band())
    block = shaped(depth, rows, LANES)

    def faces_out(step):
        width = strip_width(step)
        z_face = shaped(RADIUS + folded(RADIUS, width), rows, LANES)
        x_face = shaped(depth + folded(depth, width), RADIUS, LANES)
        return [z_face, z_face, x_face, x_face]

    strips = shaped(len(strip_places(depth)), rows, LANES)
    packets, even, odd = call(
        functools.partial(prepare_kernel, span_y, tiles),
        [shaped(tiles, LANES), strips, strips],
        [residuals, owners.reshape(1, -1), receivers.reshape(1, -1), wave_now, older_wave,
         stiffness],
        in_specs=[pl.BlockSpec()] * 6,
        grant=60,
    )
    packets = lax.all_to_all(packets, ("gx", "gy"), 0, 0, tiled=True)
    odd = swap(odd, "gy", 1)
    even = pair_gather(even, "gy", 0)
    side, older_side, stiff_side, *faces = call(
        strip_unpack_kernel,
        [block] * 3 + faces_out(0),
        [even, odd, wave_now],
    )
    packets, faces = lax.optimization_barrier((packets, faces))
    cores = 2
    packets = [packets] + [
        lax.ppermute(packets, "gz", [(chip + core, core) for core in range(cores)])
        for chip in range(cores, span_z, cores)
    ]
    face = faces[0].shape[0]
    faces[0] = call(
        functools.partial(plane_kernel, face, rows),
        shaped(face + 2 * STEPS, rows, LANES),
        [faces[0], *packets],
        scratch=[pltpu.VMEM((LANES, span_z // cores * tiles), F32)],
    )

    scratch = [
        pltpu.VMEM((2, 2 * RADIUS, rows, LANES), F32),
        pltpu.VMEM((2, depth, 2 * RADIUS, LANES), F32),
    ]
    wave, older = wave_now, older_wave
    image = None
    for step in range(STEPS):
        last = step == STEPS - 1
        own = call(
            own_kernel,
            [block, block],
            [wave, side, band_high, band_low],
            scratch=[pltpu.VMEM((depth * rows, 2 * LANES), F32)],
        )
        faces = exchange(faces)
        ins = [*faces[::-1], wave, side, older, older_side, stiffness, stiff_side, forward_wave,
               *(own[:1] if last else own)]
        outs = [block, block]
        if step:
            ins += [planes, image]
        else:
            outs = [shaped(2 * STEPS, rows, LANES)] + outs
        if not last:
            outs += [block] + faces_out(step + 1)
        room, in_specs, out_specs = scratch, None, None
        if last:
            ins.append(source_cell.reshape(1, 1))
            outs.append(block)
            out_specs = [pl.BlockSpec(memory_space=pl.ANY)] * 3
            held = pltpu.VMEM((depth, rows, LANES), F32)
            room = scratch + [held, held, pltpu.SemaphoreType.DMA((2, depth // CHUNK)),
                              pltpu.SemaphoreType.DMA]
        rest = call(
            functools.partial(step_kernel, step, cols * span_y), outs, ins, room, in_specs,
            out_specs=out_specs,
        )
        if not step:
            planes, *rest = rest
        image, fresh, *rest = rest
        older, wave = wave, fresh
        if not last:
            older_side, side = side, rest[0]
            faces = rest[1:]
    return image, rest[0], wave


def solution(mesh):
    in_specs = (
        P("gz", "gx", "gy"),
        P("gz", "gx", "gy"),
        P("gz", "gx", "gy"),
        P(None, "gz", "gx", "gy"),
        P(None, ("gx", "gy", "gz")),
        P(("gx", "gy", "gz"), None),
        P(("gx", "gy", "gz")),
        P(),
    )
    out_specs = (P("gz", "gx", "gy"), P("gz", "gx", "gy"), P("gz", "gx", "gy"))
    return jax.shard_map(
        on_device, mesh=mesh, in_specs=in_specs, out_specs=out_specs, check_vma=False
    )
```
